128 devices in a mesh: section: 2 (over core), peer: 64 (over z, y, x).
Axes of the slice: x: 4, y: 4, z: 4, core: 2. Of those that a mesh axis runs over, the one named last changes fastest.
Arguments:
- inputs: bfloat16 [64, 3, 128, 5120], P('peer'), may hold values from -6 to 6
- cotangent: bfloat16 [64, 3, 128, 5120], P('peer'), may hold values from -6 to 6
- down_proj: bfloat16 [2, 2, 5120, 128], P('section'), may hold values from -0.078125 to 0.078125
- up_proj: bfloat16 [2, 2, 5120, 128], P('section'), may hold values from -0.5 to 0.5
- norm_gain: float32 [2, 2, 5120], P('section'), may hold values from 0.5 to 1.5
- wiring: int32 [2, 144], replicated, may hold values from 0 to 63, as said below
- live_mask: int32 [2, 64], replicated, may hold values from 0 to 1, as said below
Outputs:
- down_step: bfloat16 [2, 2, 5120, 128], P('section')
- up_step: bfloat16 [2, 2, 5120, 128], P('section')
The draws below stay inside these ranges and needn't reach their ends.
Inputs may be any that keep to these rules, and one draw needn't show every extreme that they name: `live_mask`: every segment has at least 48 live peers; exactly one segment has all 64 peers live, every other segment has at least one dead peer. wiring[s, m] is smaller than the number of live peers of segment s. No two micro-batches of one lane share a peer at one segment, and in every segment the live peer of highest index receives a micro-batch of every lane. Entries of inputs and cotangent that no micro-batch names are unused.
All inputs are finite; a program needn't handle non-finite values.
Results may differ from the reference program's by a relative error of at most 0.015.
Values may be sent and summed in bfloat16 or wider, within the bound.
No kernel may reach another device: no remote copies, remote signals or barrier semaphores. Data moves between devices by JAX's collectives and lax.ppermute only.
A program may use at most 192 MiB of HBM per device.

```python
import jax
import jax.numpy as jnp
from jax import lax

D = 5120
RANK = 128
LAYERS = 2
ROWS = 128
CAP = 3
GROUP = 48
SEGMENTS = 2
N_PEER = 64


def live_peers(key):
    count_key, order_key, full_key = jax.random.split(key, 3)
    partial_counts = jax.random.randint(count_key, (SEGMENTS,), GROUP, N_PEER)
    full_segment = jax.random.randint(full_key, (), 0, SEGMENTS)
    counts = jnp.where(jnp.arange(SEGMENTS) == full_segment, N_PEER, partial_counts).astype(jnp.int32)
    orders = jax.vmap(lambda subkey: jax.random.permutation(subkey, N_PEER))(jax.random.split(order_key, SEGMENTS))
    return (counts, (orders < counts[:, None]).astype(jnp.int32))


def draw_live_mask(key, part):
    counts, masks = live_peers(key)
    return masks


def draw_wiring(key, part):
    counts, masks = live_peers(key)
    key = jax.random.fold_in(key, 7)

    def lane_pick(pair_key, count):
        first_key, second_key = jax.random.split(pair_key)
        scores = jax.random.permutation(first_key, N_PEER - 1).astype(jnp.int32)
        values = jnp.arange(1, N_PEER, dtype=jnp.int32)
        order = jnp.argsort(scores + jnp.where(values >= count, N_PEER, 0), stable=True)
        chosen = jnp.concatenate([jnp.zeros((1,), jnp.int32), values[order][:GROUP - 1]])
        placed = chosen[jax.random.permutation(second_key, GROUP)]
        return ((placed + count - 1) % count).astype(jnp.int32)
    segment_of = jnp.arange(SEGMENTS * CAP) // CAP
    picks = jax.vmap(lane_pick)(jax.random.split(key, SEGMENTS * CAP), counts[segment_of])
    return picks.reshape(SEGMENTS, CAP * GROUP).astype(jnp.int32)


def steps_of(stream_key, dims, shards, smallest, largest):
    gain, own = 1.0, jax.random.fold_in(stream_key, 6)
    for dim, parts in shards:
        heights = jnp.exp(jax.random.uniform(jax.random.fold_in(own, dim), (parts,), jnp.float32, smallest / len(shards), largest / len(shards)))
        gain = gain * jnp.repeat(heights, dims[dim] // parts).reshape([-1 if axis == dim else 1 for axis in range(len(dims))])
    return gain


def scatter_about(own_key, extent, deviation, bound, cuts=(), kind=jnp.bfloat16):
    drawn = jax.random.normal(own_key, extent, jnp.float32) * deviation
    if len(cuts) > 0:
        drawn = steps_of(own_key, extent, cuts, -0.22, 0.18) * drawn
    return jnp.clip(drawn, min=-bound, max=bound).astype(kind)


def setup_inputs(seed: int = 0) -> dict:
    key_of = jax.random.split(jax.random.key(seed), 8)
    return {
        "inputs": scatter_about(key_of[0], (N_PEER, CAP, ROWS, D), 1.0, 6.0, ((0, 64),)),
        "cotangent": scatter_about(key_of[1], (N_PEER, CAP, ROWS, D), 1.0, 6.0, ((0, 64),)),
        "down_proj": scatter_about(key_of[2], (SEGMENTS, LAYERS, D, RANK), D ** -0.5, 0.078125, ((0, 2),)),
        "up_proj": scatter_about(key_of[3], (SEGMENTS, LAYERS, D, RANK), RANK ** -0.5, 0.5, ((0, 2),)),
        "norm_gain": jnp.clip(1.0 + 0.1 * jax.random.normal(key_of[4], (SEGMENTS, LAYERS, D), jnp.float32), 0.5, 1.5),
        "wiring": draw_wiring(jax.random.fold_in(key_of[7], 71), 0),
        "live_mask": draw_live_mask(jax.random.fold_in(key_of[7], 71), 0),
    }


norm_eps = 1e-05
step_eps = 1e-06

def peer_table(wiring, live_mask):
    live_rank = jnp.cumsum(live_mask, axis=1) - 1
    matches = (live_mask[:, None, :] == 1) & (live_rank[:, None, :] == wiring[:, :, None])
    peer_ids = jnp.arange(live_mask.shape[1], dtype=jnp.int32)
    return lax.optimization_barrier(jnp.sum(jnp.where(matches, peer_ids, 0), axis=2)).astype(jnp.int32)

def layer_forward(states, down_weight, up_weight, gain_vector):
    inverse = lax.rsqrt(lax.optimization_barrier(jnp.mean(states * states, axis=-1, keepdims=True)) + norm_eps)
    normed = lax.optimization_barrier((states * inverse * gain_vector).astype(jnp.bfloat16))
    hidden = jnp.einsum('mrd,dk->mrk', normed.astype(jnp.float32), down_weight.astype(jnp.float32))
    active = lax.optimization_barrier(jax.nn.silu(hidden).astype(jnp.bfloat16))
    output = states + jnp.einsum('mrk,dk->mrd', active.astype(jnp.float32), up_weight.astype(jnp.float32))
    return (output, (states, normed, hidden, active))

def segment_forward(slot_data, down_segment, up_segment, gain_segment):
    states = slot_data.astype(jnp.float32)
    saved_acts = []
    for layer_index in range(LAYERS):
        states, kept_acts = layer_forward(states, down_segment[layer_index], up_segment[layer_index], gain_segment[layer_index])
        saved_acts.append(kept_acts)
    return (states.astype(jnp.bfloat16), saved_acts)

def layer_backward(kept_acts, gradient, down_weight, up_weight, gain_vector):
    states, normed, hidden, active = kept_acts
    grad_low = lax.optimization_barrier(gradient.astype(jnp.bfloat16)).astype(jnp.float32)
    up_grad = jnp.einsum('mrd,mrk->dk', grad_low, active.astype(jnp.float32))
    act_grad = jnp.einsum('mrd,dk->mrk', grad_low, up_weight.astype(jnp.float32))
    sigmoid_hidden = jax.nn.sigmoid(hidden)
    hid_grad = act_grad * sigmoid_hidden * (1.0 + hidden * (1.0 - sigmoid_hidden))
    hid_grad = lax.optimization_barrier(hid_grad.astype(jnp.bfloat16)).astype(jnp.float32)
    down_grad = jnp.einsum('mrd,mrk->dk', normed.astype(jnp.float32), hid_grad)
    norm_grad = jnp.einsum('mrk,dk->mrd', hid_grad, down_weight.astype(jnp.float32))
    inverse = lax.rsqrt(lax.optimization_barrier(jnp.mean(states * states, axis=-1, keepdims=True)) + norm_eps)
    scaled = gain_vector * norm_grad
    centred = lax.optimization_barrier(jnp.mean(states * scaled, axis=-1, keepdims=True))
    gradient = gradient + inverse * (scaled - states * inverse * inverse * centred)
    return (gradient, down_grad, up_grad)

def segment_backward(saved_acts, incoming, down_segment, up_segment, gain_segment):
    gradient = incoming.astype(jnp.float32)
    down_list = [None] * LAYERS
    up_list = [None] * LAYERS
    for layer_index in reversed(range(LAYERS)):
        gradient, down_list[layer_index], up_list[layer_index] = layer_backward(saved_acts[layer_index], gradient, down_segment[layer_index], up_segment[layer_index], gain_segment[layer_index])
    return (gradient.astype(jnp.bfloat16), jnp.stack([jnp.stack(down_list), jnp.stack(up_list)]))

def reference(inputs, cotangent, down_proj, up_proj, norm_gain, wiring, live_mask):
    holder = peer_table(wiring, live_mask)
    lane_of = (jnp.arange(wiring.shape[1], dtype=jnp.int32) // GROUP).astype(jnp.int32)
    first_slots = inputs[holder[0], lane_of]
    incoming = cotangent[holder[-1], lane_of]

    def forward(slot_data, weights):
        down_segment, up_segment, gain_segment = weights
        output, unused = segment_forward(slot_data, down_segment, up_segment, gain_segment)
        return (output, slot_data)
    unused_last, stored = lax.scan(forward, first_slots, (down_proj, up_proj, norm_gain))

    def backward(gradient, operands):
        down_segment, up_segment, gain_segment, slot_data = operands
        unused, saved_acts = segment_forward(slot_data, down_segment, up_segment, gain_segment)
        return segment_backward(saved_acts, gradient, down_segment, up_segment, gain_segment)
    unused_first, totals = lax.scan(backward, incoming, (down_proj, up_proj, norm_gain, stored), reverse=True)
    mean_square = lax.optimization_barrier(jnp.mean(totals * totals, axis=(3, 4), keepdims=True))
    step_out = (totals * lax.rsqrt(mean_square + step_eps)).astype(jnp.bfloat16)
    return (step_out[:, 0], step_out[:, 1])
```

```python
import jax
import jax.numpy as jnp
from jax import lax
from jax.sharding import PartitionSpec as P

norm_eps = 1e-05
step_eps = 1e-06
bf16 = jnp.bfloat16
f32 = jnp.float32


def dot(a, b):
    return jnp.dot(a.astype(bf16), b.astype(bf16), preferred_element_type=f32)


def dot_nt(a, b):
    return lax.dot_general(
        a.astype(bf16), b.astype(bf16), (((1,), (1,)), ((), ())), preferred_element_type=f32
    )


def dot_tn(a, b):
    return lax.dot_general(
        a.astype(bf16), b.astype(bf16), (((0,), (0,)), ((), ())), preferred_element_type=f32
    )


def peer_table(wiring, live_mask):
    live_rank = jnp.cumsum(live_mask, axis=1) - 1
    matches = (live_mask[:, None, :] == 1) & (live_rank[:, None, :] == wiring[:, :, None])
    peer_ids = jnp.arange(live_mask.shape[1], dtype=jnp.int32)
    return jnp.sum(jnp.where(matches, peer_ids, 0), axis=2)


def row_sum(values):
    return jnp.sum(values, axis=1, keepdims=True)


def row_stage(proj, cot, square_sum, gram_first, gram_second, gram_cross, feature_count):
    k = cot[0].shape[1]

    def cut(g, i, j):
        return g[i * k : (i + 1) * k, j * k : (j + 1) * k].astype(bf16)

    ugd = {(0, 1): cut(gram_first, 0, 0), (2, 3): cut(gram_second, 0, 0)}
    uu = {
        (0, 0): cut(gram_first, 0, 1),
        (0, 1): cut(gram_first, 0, 2),
        (1, 1): cut(gram_first, 1, 2),
        (2, 2): cut(gram_second, 0, 1),
    }
    for i in (0, 1):
        ugd[(i, 2)] = cut(gram_cross, i, 0)
        ugd[(i, 3)] = cut(gram_cross, i, 1)
        uu[(i, 2)] = cut(gram_cross, i, 2)

    hidden, active, inverse, full = [], [], [], []
    for l in range(4):
        r = lax.rsqrt(square_sum * (1.0 / feature_count) + norm_eps)
        pre = proj[l][0]
        for i in range(l):
            pre = pre + dot(active[i], ugd[(i, l)])
        h = r * pre
        a = (h * jax.nn.sigmoid(h)).astype(bf16)
        hidden.append(h)
        active.append(a)
        inverse.append(r)
        if l < 3:
            along = proj[l][1]
            for i in range(l):
                along = along + dot(active[i], uu[(i, l)])
            own = dot(a, uu[(l, l)])
            square_sum = square_sum + row_sum((2.0 * along + own) * a.astype(f32))
            full.append(along + own)

    back = [None] * 4
    weight = [None] * 4
    weight[3] = jnp.zeros_like(square_sum)
    for l in (3, 2, 1, 0):
        grad = cot[l]
        for j in range(l + 1, 4):
            grad = grad + dot_nt(back[j], ugd[(l, j)])
        if l < 3:
            grad = grad - weight[l] * full[l]
        for i in range(l + 1, 3):
            grad = grad - weight[i] * dot_nt(active[i], uu[(l, i)])
        sig = jax.nn.sigmoid(hidden[l])
        hid_grad = (grad * sig * (1.0 + hidden[l] * (1.0 - sig))).astype(bf16).astype(f32)
        back[l] = (inverse[l] * hid_grad).astype(bf16)
        if l > 0:
            centred = row_sum(hidden[l] * hid_grad) * (1.0 / feature_count)
            weight[l - 1] = weight[l] + inverse[l] * inverse[l] * centred
    less = [(-weight[l] * active[l].astype(f32)).astype(bf16) for l in range(4)]

    def scaled(w, l):
        return (-w * active[l].astype(f32)).astype(bf16)

    zero = jnp.zeros((k, k), f32)

    def table(rows):
        return jnp.concatenate([jnp.concatenate(row, axis=1) for row in rows], axis=0)

    a, b, w = active, back, weight
    mix_first = table(
        [
            [zero, zero, dot_tn(b[1], a[0]), zero],
            [zero, dot_tn(a[0], b[1]), dot_tn(a[0], less[0]), dot_tn(a[0], less[1])],
            [zero, zero, dot_tn(a[1], scaled(w[1], 0)), dot_tn(a[1], less[1])],
            [zero, zero, dot_tn(b[2], a[0]), dot_tn(b[2], a[1])],
            [zero, zero, dot_tn(b[3], a[0]), dot_tn(b[3], a[1])],
            [zero, zero, dot_tn(a[2], scaled(w[2], 0)), dot_tn(a[2], scaled(w[2], 1))],
        ]
    ).astype(bf16)
    mix_second = table(
        [
            [zero, zero, dot_tn(b[3], a[2]), zero],
            [zero, dot_tn(a[2], b[3]), dot_tn(a[2], less[2]), zero],
            [zero, zero, zero, zero],
            [zero, zero, zero, zero],
            [dot_tn(a[0], b[2]), dot_tn(a[0], b[3]), dot_tn(a[0], less[2]), zero],
            [dot_tn(a[1], b[2]), dot_tn(a[1], b[3]), dot_tn(a[1], less[2]), zero],
        ]
    ).astype(bf16)
    return active, back, less, mix_first, mix_second


def slot_rows(holder, lane_of, count, across):
    base = holder * 8 + lane_of * 2
    if across:
        grid = lax.broadcasted_iota(jnp.int32, (count, base.shape[1]), 0)
    else:
        grid = lax.broadcasted_iota(jnp.int32, (base.shape[0], count), 1)
    return base, grid


def meet(received, holders, gram_first, gram_second, gram_cross, lanes, feature_count):
    total = holders.shape[1]
    group = total // lanes
    slots = received.shape[1]
    k = received.shape[2] // 3
    lane_of = jnp.arange(total, dtype=jnp.int32) // group
    grid = lax.broadcasted_iota(jnp.int32, (total, slots), 1)

    def pick(base):
        return (grid == base[:, None]).astype(bf16)

    first = holders[0] * 8 + lane_of * 2
    second = holders[1] * 8 + lane_of * 2
    at_start = pick(first)
    at_start_next = pick(first + 1)
    at_end = pick(second + 1)
    coarse = dot(pick(holders[0] * 8 + 6), received[0])
    fine = dot(pick(holders[0] * 8 + 7), received[0])
    square_sum = jnp.concatenate(
        [
            coarse[j * group : (j + 1) * group, j * k : j * k + 1]
            + fine[j * group : (j + 1) * group, j * k : j * k + 1]
            for j in range(lanes)
        ],
        axis=0,
    )
    proj, cot = [], []
    for s in range(2):
        low = dot(at_start, received[s])
        high = dot(at_start_next, received[s][:, :k])
        tail = dot(at_end, received[s][:, k:])
        proj += [(low[:, :k], low[:, 2 * k :]), (low[:, k : 2 * k], high)]
        cot += [tail[:, :k], tail[:, k:]]
    active, back, less, mix_first, mix_second = row_stage(
        proj, cot, square_sum, gram_first, gram_second, gram_cross, feature_count
    )
    out = []
    for s in range(2):
        l0, l1 = 2 * s, 2 * s + 1
        zero = jnp.zeros_like(active[0])
        part = dot_tn(at_start, jnp.concatenate([back[l0], back[l1], less[l0]], axis=1))
        part = part + dot_tn(at_start_next, jnp.concatenate([less[l1], zero, zero], axis=1))
        part = part + dot_tn(at_end, jnp.concatenate([zero, active[l0], active[l1]], axis=1))
        out.append(part.astype(bf16))
    return jnp.stack(out), mix_first, mix_second


def coords(peer):
    return peer // 16, (peer // 4) % 4, peer % 4


def hop_pairs(stage, by):
    pairs = []
    for s in range(2):
        axis = (0, 1, 2)[stage] if s == 0 else (1, 0, 2)[stage]
        for p in range(64):
            c = list(coords(p))
            c[axis] = (c[axis] + by) % 4
            pairs.append((s * 64 + p, s * 64 + c[0] * 16 + c[1] * 4 + c[2]))
    return pairs


def hop(values, stage, by):
    return lax.ppermute(values, ("section", "peer"), hop_pairs(stage, by))


def local(inputs, cotangent, down_proj, up_proj, norm_gain, wiring, live_mask):
    section = lax.axis_index("section")
    peer = lax.axis_index("peer")
    _, lanes, rows, features = inputs.shape
    k = down_proj.shape[3]
    x = inputs[0].reshape(lanes * rows, features)
    c = cotangent[0].reshape(lanes * rows, features)
    gain = norm_gain[0]
    gained = (down_proj[0].astype(f32) * gain[:, :, None]).astype(bf16)
    own = jnp.concatenate([gained, up_proj[0]], axis=0)
    swap = [(0, 1), (1, 0)]
    other = lax.ppermute(
        lax.dynamic_slice_in_dim(own, 1 - section, 3, axis=0), "section", swap
    )
    wide = jnp.concatenate([own[0], own[1], own[2], own[3]], axis=1)
    px = dot(x, wide)
    qc = dot(c, wide[:, 2 * k :])
    square = jnp.sum(x.astype(f32) * x.astype(f32), axis=1).reshape(lanes, rows)
    gram_own = dot_tn(wide[:, 2 * k :], wide[:, k:])
    gram_other = lax.ppermute(gram_own, "section", swap)

    both = jnp.concatenate([px, qc], axis=1).astype(bf16).reshape(lanes, rows, 2, 3 * k)
    coarse = square.astype(bf16)
    fine = (square - coarse.astype(f32)).astype(bf16)
    norms = jnp.stack([coarse, fine])
    norms = jnp.broadcast_to(
        norms.transpose(2, 0, 1)[:, :, :, None], (rows, 2, lanes, k)
    ).reshape(rows, 2, lanes * k)
    sent = jnp.concatenate(
        [both.transpose(1, 0, 2, 3).reshape(rows, lanes * 2, 3 * k), norms], axis=1
    )
    received = lax.all_to_all(sent, ("section", "peer"), 0, 0, tiled=True)
    received = received.reshape(2, -1, 3 * k)
    gram_cross = lax.cond(
        section == 0,
        lambda: dot_tn(wide[:, 2 * k :], jnp.concatenate(list(other), axis=1)),
        lambda: dot_tn(jnp.concatenate([other[1], other[2]], axis=1), wide[:, : 3 * k]),
    )
    gram_first = jnp.where(section == 0, gram_own, gram_other)
    gram_second = jnp.where(section == 0, gram_other, gram_own)
    holders = peer_table(wiring, live_mask)
    out, mix_first, mix_second = meet(
        received, holders, gram_first, gram_second, gram_cross, lanes, features
    )
    mix_other = lax.ppermute(jnp.where(section == 0, mix_second, mix_first), "section", swap)
    returned = lax.all_to_all(
        out.reshape(rows, 8, 3 * k), ("section", "peer"), 0, 0, tiled=True
    )
    mix = jnp.where(section == 0, mix_first, mix_second).astype(f32) + mix_other.astype(f32)

    def spread(half, start, stop):
        return jnp.concatenate(
            [returned[:, 2 * j + half, start * k : stop * k] for j in range(lanes)], axis=0
        )

    x_side = jnp.concatenate([spread(0, 0, 3), spread(1, 0, 1)], axis=1)
    c_side = spread(1, 1, 3)
    z, y, xx = coords(peer)
    first = jnp.where(section == 0, z, y)
    second = jnp.where(section == 0, y, z)
    third = xx

    mix = mix.astype(bf16)
    quarter = features // 4
    weights = jnp.concatenate([own[1], own[2], own[3], other[0], other[1], other[2]], axis=1)

    def piece(index):
        at = index * quarter
        x_cut = lax.dynamic_slice_in_dim(x, at, quarter, axis=1)
        c_cut = lax.dynamic_slice_in_dim(c, at, quarter, axis=1)
        w_cut = lax.dynamic_slice_in_dim(weights, at, quarter, axis=0)
        g_cut = lax.dynamic_slice_in_dim(gain, at, quarter, axis=1)
        total = dot_tn(x_cut, x_side) + dot(w_cut, mix)
        low = total[:, : 2 * k].reshape(quarter, 2, k) * g_cut.T[:, :, None]
        high = total[:, 2 * k :] + dot_tn(c_cut, c_side)
        return jnp.concatenate([low.reshape(quarter, 2 * k), high], axis=1).astype(bf16)

    arrived = [hop(piece((first + by) % 4), 0, by) for by in (2, 1, 3)]
    total = piece(first).astype(f32) + sum(part.astype(f32) for part in arrived)
    for stage, at in ((1, second), (2, third)):
        step = total.shape[0] // 4

        def cut(by):
            return lax.dynamic_slice_in_dim(total, ((at + by) % 4) * step, step, axis=0)

        arrived = [hop(cut(by).astype(bf16), stage, by) for by in (2, 1, 3)]
        total = cut(0) + sum(part.astype(f32) for part in arrived)

    block = total.astype(bf16)
    for stage, at in ((2, third), (1, second), (0, first)):
        step = block.shape[0]
        arrived = [block] + [hop(block, stage, by) for by in (1, 2, 3)]
        wide_block = jnp.zeros((4 * step, block.shape[1]), bf16)
        for by in range(4):
            wide_block = lax.dynamic_update_slice_in_dim(
                wide_block, arrived[by], ((at - by) % 4) * step, axis=0
            )
        block = wide_block
    grads = block.astype(f32).reshape(features, 4, k)
    mean_square = jnp.mean(grads * grads, axis=(0, 2), keepdims=True)
    steps = (grads * lax.rsqrt(mean_square + step_eps)).astype(bf16).transpose(1, 0, 2)
    return steps[None, :2], steps[None, 2:]


def solution(mesh):
    placed = (
        P("peer", None, None, None),
        P("peer", None, None, None),
        P("section", None, None, None),
        P("section", None, None, None),
        P("section", None, None),
        P(),
        P(),
    )
    return jax.shard_map(
        local,
        mesh=mesh,
        in_specs=placed,
        out_specs=(P("section", None, None, None), P("section", None, None, None)),
        check_vma=False,
    )
```

```python
import jax
import jax.numpy as jnp
from jax import lax
from jax.experimental import pallas as pl
from jax.experimental.pallas import tpu as pltpu
from jax.sharding import PartitionSpec as P

norm_eps = 1e-05
step_eps = 1e-06
bf16 = jnp.bfloat16
f32 = jnp.float32


def dot(a, b):
    return jnp.dot(a.astype(bf16), b.astype(bf16), preferred_element_type=f32)


def dot_nt(a, b):
    return lax.dot_general(
        a.astype(bf16), b.astype(bf16), (((1,), (1,)), ((), ())), preferred_element_type=f32
    )


def dot_tn(a, b):
    return lax.dot_general(
        a.astype(bf16), b.astype(bf16), (((0,), (0,)), ((), ())), preferred_element_type=f32
    )


def peer_table(wiring, live_mask):
    live_rank = jnp.cumsum(live_mask, axis=1) - 1
    matches = (live_mask[:, None, :] == 1) & (live_rank[:, None, :] == wiring[:, :, None])
    peer_ids = jnp.arange(live_mask.shape[1], dtype=jnp.int32)
    return jnp.sum(jnp.where(matches, peer_ids, 0), axis=2)


def row_sum(values):
    return jnp.sum(values, axis=1, keepdims=True)


def row_stage(proj, cot, square_sum, gram_low, gram_high, feature_count):
    k = cot[0].shape[1]

    def cut(g, i, j):
        return g[i * k : (i + 1) * k, j * k : (j + 1) * k].astype(bf16)

    ugd = {(0, 1): cut(gram_low, 0, 0), (2, 3): cut(gram_high, 0, 0)}
    uu = {
        (0, 0): cut(gram_low, 0, 1),
        (0, 1): cut(gram_low, 0, 2),
        (1, 1): cut(gram_low, 1, 2),
        (2, 2): cut(gram_high, 0, 1),
    }
    for i in (0, 1):
        ugd[(i, 2)] = cut(gram_low, i, 3)
        ugd[(i, 3)] = cut(gram_low, i, 4)
        uu[(i, 2)] = cut(gram_low, i, 5)

    hidden, active, inverse, full = [], [], [], []
    for l in range(4):
        r = lax.rsqrt(square_sum * (1.0 / feature_count) + norm_eps)
        pre = proj[l][0]
        for i in range(l):
            pre = pre + dot(active[i], ugd[(i, l)])
        h = r * pre
        a = (h * jax.nn.sigmoid(h)).astype(bf16)
        hidden.append(h)
        active.append(a)
        inverse.append(r)
        if l < 3:
            along = proj[l][1]
            for i in range(l):
                along = along + dot(active[i], uu[(i, l)])
            own = dot(a, uu[(l, l)])
            square_sum = square_sum + row_sum((2.0 * along + own) * a.astype(f32))
            full.append(along + own)

    back = [None] * 4
    weight = [None] * 4
    weight[3] = jnp.zeros_like(square_sum)
    for l in (3, 2, 1, 0):
        grad = cot[l]
        for j in range(l + 1, 4):
            grad = grad + dot_nt(back[j], ugd[(l, j)])
        if l < 3:
            grad = grad - weight[l] * full[l]
        for i in range(l + 1, 3):
            grad = grad - weight[i] * dot_nt(active[i], uu[(l, i)])
        sig = jax.nn.sigmoid(hidden[l])
        hid_grad = (grad * sig * (1.0 + hidden[l] * (1.0 - sig))).astype(bf16).astype(f32)
        back[l] = (inverse[l] * hid_grad).astype(bf16)
        if l > 0:
            centred = row_sum(hidden[l] * hid_grad) * (1.0 / feature_count)
            weight[l - 1] = weight[l] + inverse[l] * inverse[l] * centred
    less = [(-weight[l] * active[l].astype(f32)).astype(bf16) for l in range(4)]

    def scaled(w, l):
        return (-w * active[l].astype(f32)).astype(bf16)

    def against(left, parts):
        turned = left.astype(f32).T.astype(bf16)
        product = dot(turned, jnp.concatenate(parts, axis=1))
        return [product[:, i * k : (i + 1) * k] for i in range(len(parts))]

    a, b, w = active, back, weight
    a0 = against(a[0], [b[1], less[0], less[1], b[2], b[3], less[2]])
    a1 = against(a[1], [scaled(w[1], 0), less[1], b[2], b[3], less[2]])
    a2 = against(a[2], [scaled(w[2], 0), scaled(w[2], 1), b[3], less[2]])
    b1 = against(b[1], [a[0]])
    b2 = against(b[2], [a[0], a[1]])
    b3 = against(b[3], [a[0], a[1], a[2]])
    none = jnp.zeros((k, k), f32)
    mix_first = [
        [none, none, b1[0], none],
        [none, a0[0], a0[1], a0[2]],
        [none, none, a1[0], a1[1]],
        [none, none, b2[0], b2[1]],
        [none, none, b3[0], b3[1]],
        [none, none, a2[0], a2[1]],
    ]
    mix_second = [
        [none, none, none, none],
        [a0[3], a0[4], a0[5], none],
        [a1[2], a1[3], a1[4], none],
        [none, none, none, none],
        [none, none, b3[2], none],
        [none, a2[2], a2[3], none],
    ]
    return active, back, less, mix_first, mix_second


def joined(parts):
    return jnp.concatenate(list(parts), axis=1)


def front(x, c, down, up, gain):
    lanes, rows, features = x.shape
    k = down.shape[2]
    block = 1024
    steps = features // block
    total = lanes * rows

    def kernel(x_ref, c_ref, d_ref, u_ref, g_ref, sent_ref, acc, squares, packed):
        step = pl.program_id(0)
        columns = jnp.concatenate([g_ref[...]] * 4, axis=0).T
        gained = [
            (d_ref[l].astype(f32) * columns[:, l : l + 1]).astype(bf16) for l in range(2)
        ]
        ups = [u_ref[0], u_ref[1]]
        flat = x_ref[...].reshape(total, block)
        of_x = dot(flat, joined(gained + ups))
        of_c = dot(c_ref[...].reshape(total, block), joined(ups))
        part = jnp.zeros((total, k), f32)
        for j in range(block // k):
            wide = flat[:, j * k : (j + 1) * k].astype(f32)
            part = part + wide * wide

        @pl.when(step == 0)
        def _():
            acc[:, : 4 * k] = of_x
            acc[:, 4 * k :] = of_c
            squares[...] = part

        @pl.when(step > 0)
        def _():
            acc[:, : 4 * k] += of_x
            acc[:, 4 * k :] += of_c
            squares[...] += part

        @pl.when(step == steps - 1)
        def _():
            for j in range(lanes):
                at = slice(j * rows, (j + 1) * rows)
                for half in range(2):
                    for t in range(3):
                        packed[t, pl.ds(2 * j + half, rows, stride=8), :] = acc[
                            at, (half * 3 + t) * k : (half * 3 + t + 1) * k
                        ]
                square = jnp.broadcast_to(row_sum(squares[at, :]), (rows, k))
                coarse = square.astype(bf16).astype(f32)
                packed[j, pl.ds(6, rows, stride=8), :] = coarse
                packed[j, pl.ds(7, rows, stride=8), :] = square - coarse
            for t in range(3):
                sent_ref[:, t * k : (t + 1) * k] = packed[t].astype(bf16)

    return pl.pallas_call(
        kernel,
        grid=(steps,),
        in_specs=[
            pl.BlockSpec((lanes, rows, block), lambda i: (0, 0, i)),
            pl.BlockSpec((lanes, rows, block), lambda i: (0, 0, i)),
            pl.BlockSpec((2, block, k), lambda i: (0, i, 0)),
            pl.BlockSpec((2, block, k), lambda i: (0, i, 0)),
            pl.BlockSpec((2, block), lambda i: (0, i)),
        ],
        out_specs=pl.BlockSpec((8 * rows, 3 * k), lambda i: (0, 0)),
        out_shape=jax.ShapeDtypeStruct((8 * rows, 3 * k), bf16),
        scratch_shapes=[
            pltpu.VMEM((total, 6 * k), f32),
            pltpu.VMEM((total, k), f32),
            pltpu.VMEM((3, 8 * rows, k), f32),
        ],
        compiler_params=pltpu.CompilerParams(vmem_limit_bytes=48 << 20),
        name="front",
    )(x, c, down, up, gain)


def prepare(section, down, up, gain, down_other, up_other, gain_other):
    _, features, k = down.shape
    block = 1024
    steps = features // block

    def kernel(s_ref, d, u, g, d2, u2, g2, w_ref, low_ref, high_ref):
        step = pl.program_id(0)
        gains = jnp.concatenate([g[...], g2[...]] * 2, axis=0).T
        first = s_ref[0] == 0

        def choose(one, two):
            return jnp.where(first, one.astype(f32), two.astype(f32))

        gain_one = choose(gains[:, :2], gains[:, 2:4])
        gain_two = choose(gains[:, 2:4], gains[:, :2])
        parts = [
            choose(d[1], d2[1]) * gain_one[:, 1:2],
            choose(u[0], u2[0]),
            choose(u[1], u2[1]),
            choose(d2[0], d[0]) * gain_two[:, :1],
            choose(d2[1], d[1]) * gain_two[:, 1:2],
            choose(u2[0], u[0]),
        ]
        parts = [part.astype(bf16) for part in parts]
        weights = joined(parts)
        w_ref[...] = weights
        low = dot_tn(joined(parts[1:3]), weights)
        high = dot_tn(parts[5], joined(parts[4:]))

        @pl.when(step == 0)
        def _():
            low_ref[...] = low
            high_ref[...] = high

        @pl.when(step > 0)
        def _():
            low_ref[...] += low
            high_ref[...] += high

    two = pl.BlockSpec((2, block, k), lambda i, s: (0, i, 0))
    row = pl.BlockSpec((2, block), lambda i, s: (0, i))
    return pl.pallas_call(
        kernel,
        grid_spec=pltpu.PrefetchScalarGridSpec(
            num_scalar_prefetch=1,
            grid=(steps,),
            in_specs=[two, two, row, two, two, row],
            out_specs=[
                pl.BlockSpec((block, 6 * k), lambda i, s: (i, 0)),
                pl.BlockSpec((2 * k, 6 * k), lambda i, s: (0, 0)),
                pl.BlockSpec((k, 2 * k), lambda i, s: (0, 0)),
            ],
        ),
        out_shape=[
            jax.ShapeDtypeStruct((features, 6 * k), bf16),
            jax.ShapeDtypeStruct((2 * k, 6 * k), f32),
            jax.ShapeDtypeStruct((k, 2 * k), f32),
        ],
        compiler_params=pltpu.CompilerParams(vmem_limit_bytes=48 << 20),
        name="prepare",
    )(section[None], down, up, gain, down_other, up_other, gain_other)


def turn(x, c):
    lanes, rows, features = x.shape
    block = 1024

    def kernel(x_ref, c_ref, out):
        for j in range(lanes):
            out[:, j * rows : (j + 1) * rows] = x_ref[j].T
            out[:, (lanes + j) * rows : (lanes + j + 1) * rows] = c_ref[j].T

    spec = pl.BlockSpec((lanes, rows, block), lambda i: (0, 0, i))
    return pl.pallas_call(
        kernel,
        grid=(features // block,),
        in_specs=[spec, spec],
        out_specs=pl.BlockSpec((block, 2 * lanes * rows), lambda i: (i, 0)),
        out_shape=jax.ShapeDtypeStruct((features, 2 * lanes * rows), bf16),
        compiler_params=pltpu.CompilerParams(vmem_limit_bytes=48 << 20),
        name="turn",
    )(x, c)


def meet(received, first, second, gram_low, gram_high, lanes, features):
    total = first.shape[0]
    group = total // lanes
    slots = received.shape[1]
    k = received.shape[2] // 3

    def kernel(rec, i0, i1, t0, t1, low_gram, high_gram, out, mix):
        grid = lax.broadcasted_iota(jnp.int32, (total, slots), 1)
        turned = lax.broadcasted_iota(jnp.int32, (slots, total), 0)

        def pick(base):
            return (grid == base).astype(f32).astype(bf16)

        def place(base):
            return (turned == base).astype(f32).astype(bf16)

        at_start = pick(i0[...])
        at_start_next = pick(i0[...] + 1)
        at_end = pick(i1[...] + 1)
        lane = lax.broadcasted_iota(jnp.int32, (total, 1), 0) // group
        norm_row = i0[...] - 2 * lane + 6
        sums = dot(pick(norm_row), rec[0]) + dot(pick(norm_row + 1), rec[0])
        square_sum = jnp.concatenate(
            [sums[j * group : (j + 1) * group, j * k : (j + 1) * k] for j in range(lanes)], axis=0
        )[:, :1]
        proj, cot = [], []
        for s in range(2):
            low = dot(at_start, rec[s])
            high = dot(at_start_next, rec[s, :, :k])
            tail = dot(at_end, rec[s, :, k:])
            proj += [(low[:, :k], low[:, 2 * k :]), (low[:, k : 2 * k], high)]
            cot += [tail[:, :k], tail[:, k:]]
        active, back, less, mix_first, mix_second = row_stage(
            proj, cot, square_sum, low_gram[...], high_gram[...], features
        )
        to_start = place(t0[...])
        to_start_next = place(t0[...] + 1)
        to_end = place(t1[...] + 1)
        for s in range(2):
            l0, l1 = 2 * s, 2 * s + 1
            out[s] = dot(to_start, joined([back[l0], back[l1], less[l0]])).astype(bf16)
            high = dot(to_start_next, less[l1])
            tail = dot(to_end, joined([active[l0], active[l1]]))
            out[s] += joined([high, tail]).astype(bf16)
        for s, table in enumerate((mix_first, mix_second)):
            for i, row in enumerate(table):
                mix[s, i * k : (i + 1) * k, :] = joined(row).astype(bf16)

    return pl.pallas_call(
        kernel,
        out_shape=[
            jax.ShapeDtypeStruct(received.shape, bf16),
            jax.ShapeDtypeStruct((2, 6 * k, 4 * k), bf16),
        ],
        compiler_params=pltpu.CompilerParams(vmem_limit_bytes=48 << 20),
        name="meet",
    )(
        received,
        first[:, None],
        second[:, None],
        first[None, :],
        second[None, :],
        gram_low,
        gram_high,
    )


def unpack(returned, mix_own, mix_other, lanes):
    rows, k = returned.shape[0] // 8, returned.shape[1] // 3

    def kernel(ret, own, oth, xs, cs, mix, wide):
        for t in range(3):
            wide[t] = ret[:, t * k : (t + 1) * k].astype(f32)
        for j in range(lanes):
            at = slice(j * rows, (j + 1) * rows)
            low = [wide[t, pl.ds(2 * j, rows, stride=8), :].astype(bf16) for t in range(3)]
            high = [wide[t, pl.ds(2 * j + 1, rows, stride=8), :].astype(bf16) for t in range(3)]
            xs[at, :] = joined(low + high[:1])
            cs[at, :] = joined(high[1:])
        mix[...] = (own[...].astype(f32) + oth[...].astype(f32)).astype(bf16)

    return pl.pallas_call(
        kernel,
        out_shape=[
            jax.ShapeDtypeStruct((lanes * rows, 4 * k), bf16),
            jax.ShapeDtypeStruct((lanes * rows, 2 * k), bf16),
            jax.ShapeDtypeStruct(mix_own.shape, bf16),
        ],
        scratch_shapes=[pltpu.VMEM((3, 8 * rows, k), f32)],
        compiler_params=pltpu.CompilerParams(vmem_limit_bytes=48 << 20),
        name="unpack",
    )(returned, mix_own, mix_other)


def piece(at, turned, weights, gain, xs, cs, mix, minor):
    features, both = turned.shape
    k = cs.shape[1] // 2
    quarter = features // 4
    block = 640
    steps = quarter // block
    total = both // 2
    fresh = minor is None

    def kernel(at_ref, t_ref, w_ref, g_ref, xs_ref, cs_ref, mix_ref, *refs):
        out, last_out = refs[-2:]
        value = dot(t_ref[:, :total], xs_ref[...]) + dot(w_ref[...], mix_ref[...])
        last = dot(t_ref[:, total:], cs_ref[...])
        gains = jnp.concatenate([g_ref[...]] * 4, axis=0).T
        out[:, :k] = (value[:, :k] * gains[:, :1]).astype(bf16)
        out[:, k : 2 * k] = (value[:, k : 2 * k] * gains[:, 1:2]).astype(bf16)
        out[:, 2 * k :] = (value[:, 2 * k : 3 * k] + last[:, :k]).astype(bf16)
        last_out[0] = (value[:, 3 * k :] + last[:, k:]).astype(bf16)

    in_specs = [
        pl.BlockSpec((block, both), lambda i, at: (at[0] * steps + i, 0)),
        pl.BlockSpec((block, 6 * k), lambda i, at: (at[0] * steps + i, 0)),
        pl.BlockSpec((2, block), lambda i, at: (0, at[0] * steps + i)),
        pl.BlockSpec((total, 4 * k), lambda i, at: (0, 0)),
        pl.BlockSpec((total, 2 * k), lambda i, at: (0, 0)),
        pl.BlockSpec((6 * k, 4 * k), lambda i, at: (0, 0)),
    ]
    operands = [at[None], turned, weights, gain, xs, cs, mix]
    if not fresh:
        in_specs.append(pl.BlockSpec(memory_space=pl.ANY))
        operands.append(minor)
    return pl.pallas_call(
        kernel,
        grid_spec=pltpu.PrefetchScalarGridSpec(
            num_scalar_prefetch=1,
            grid=(steps,),
            in_specs=in_specs,
            out_specs=[
                pl.BlockSpec((block, 3 * k), lambda i, at: (i, 0)),
                pl.BlockSpec((1, block, k), lambda i, at: (at[0], i, 0)),
            ],
        ),
        out_shape=[
            jax.ShapeDtypeStruct((quarter, 3 * k), bf16),
            jax.ShapeDtypeStruct((4, quarter, k), bf16),
        ],
        input_output_aliases={} if fresh else {7: 1},
        compiler_params=pltpu.CompilerParams(vmem_limit_bytes=48 << 20),
        name="piece",
    )(*operands)


def finish(starts, major, minor, features, k):
    quarter = features // 4
    part = quarter // 4

    def kernel(at, *refs):
        ins, (down, up) = refs[:8], refs[8:]
        group = pl.program_id(0)

        def run(blocks, out, which):
            total = jnp.zeros((8, k), f32)
            for ref in blocks:
                v = ref[...].astype(f32)
                total = total + jnp.sum((v * v).reshape(quarter // 8, 8, k), axis=0)
            mean = jnp.sum(total) * (1.0 / (features * k))
            scale = lax.rsqrt(jnp.full((1, k), mean, f32) + step_eps)
            for i, ref in enumerate(blocks):
                for j in range(4):
                    row = pl.multiple_of(at[which, i, j], 16)
                    v = ref[j * part : (j + 1) * part, :].astype(f32)
                    out[0, pl.ds(row, part), :] = (v * scale).astype(bf16)

        @pl.when(group < 2)
        def _():
            run(ins[:4], down, 0)

        @pl.when(group == 2)
        def _():
            run(ins[:4], up, 0)

        @pl.when(group == 3)
        def _():
            run(ins[4:], up, 1)

    return pl.pallas_call(
        kernel,
        grid_spec=pltpu.PrefetchScalarGridSpec(
            num_scalar_prefetch=1,
            grid=(4,),
            in_specs=[pl.BlockSpec((quarter, k), lambda g, at: (0, jnp.minimum(g, 2)))] * 4
            + [pl.BlockSpec((quarter, k), lambda g, at: (0, 0))] * 4,
            out_specs=[
                pl.BlockSpec((1, features, k), lambda g, at: (jnp.minimum(g, 1), 0, 0)),
                pl.BlockSpec((1, features, k), lambda g, at: (jnp.maximum(g - 2, 0), 0, 0)),
            ],
        ),
        out_shape=[jax.ShapeDtypeStruct((2, features, k), bf16)] * 2,
        compiler_params=pltpu.CompilerParams(vmem_limit_bytes=48 << 20),
        name="finish",
    )(starts, *major, *minor)


def coords(peer):
    return peer // 16, (peer // 4) % 4, peer % 4


MAJOR = ((0, 1, 2), (1, 0, 2))
MINOR = ((2, 1, 0), (2, 0, 1))


def hop(values, order, stage, by):
    pairs = []
    for s in range(2):
        axis = order[s][stage]
        for p in range(64):
            c = list(coords(p))
            c[axis] = (c[axis] + by) % 4
            pairs.append((s * 64 + p, s * 64 + c[0] * 16 + c[1] * 4 + c[2]))
    return lax.ppermute(values, ("section", "peer"), pairs)


def summed(parts, order, at):
    step = parts[0].shape[0] // 4

    def cut(by):
        start = ((at + by) % 4) * step
        return sum(lax.dynamic_slice_in_dim(p, start, step, axis=0).astype(f32) for p in parts)

    arrived = [hop(cut(by).astype(bf16), order, 1, by) for by in (2, 1, 3)]
    own = cut(0) + sum(part.astype(f32) for part in arrived)
    own = lax.optimization_barrier(own.astype(bf16))
    two, one, three = [hop(own, order, 2, by).astype(f32) for by in (2, 1, 3)]
    return ((own.astype(f32) + two) + (one + three)).astype(bf16)


def gathered(block, order):
    wide = jnp.concatenate([block] + [hop(block, order, 1, by) for by in (1, 2, 3)], axis=0)
    return [wide] + [hop(wide, order, 0, by) for by in (1, 2, 3)]


def local(inputs, cotangent, down_proj, up_proj, norm_gain, wiring, live_mask):
    section = lax.axis_index("section")
    peer = lax.axis_index("peer")
    _, lanes, rows, features = inputs.shape
    k = down_proj.shape[3]
    x, c = inputs[0], cotangent[0]
    gain, up = norm_gain[0], up_proj[0]
    is_first = section == 0
    swap = [(0, 1), (1, 0)]
    down = down_proj[0]
    down_other = lax.ppermute(down, "section", swap)
    up_other = lax.ppermute(up, "section", swap)
    gain_other = lax.ppermute(gain, "section", swap)
    sent = front(x, c, down, up, gain)
    received = lax.all_to_all(
        sent.reshape(rows, 8, 3 * k), ("section", "peer"), 0, 0, tiled=True
    ).reshape(2, -1, 3 * k)
    weights, gram_low, gram_high = prepare(
        section, down, up, gain, down_other, up_other, gain_other
    )
    holders = peer_table(wiring, live_mask)
    total = holders.shape[1]
    lane_of = jnp.arange(total, dtype=jnp.int32) // (total // lanes)
    base = holders * 8 + 2 * lane_of
    out, mix = meet(
        received, base[0], base[1], gram_low, gram_high, lanes, features
    )
    mix_own = lax.dynamic_index_in_dim(mix, section, 0, keepdims=False)
    mix_other = lax.ppermute(
        lax.dynamic_index_in_dim(mix, 1 - section, 0, keepdims=False), "section", swap
    )
    returned = lax.all_to_all(
        out.reshape(rows, 8, 3 * k), ("section", "peer"), 0, 0, tiled=True
    ).reshape(8 * rows, 3 * k)
    turned = turn(*lax.optimization_barrier((x, c, mix))[:2])
    xs, cs, mix = unpack(returned, mix_own, mix_other, lanes)

    where = jnp.stack(coords(peer))
    at_major = [jnp.where(is_first, where[MAJOR[0][i]], where[MAJOR[1][i]]) for i in range(3)]
    at_minor = [jnp.where(is_first, where[MINOR[0][i]], where[MINOR[1][i]]) for i in range(3)]

    major, minor = [], None
    for by in (2, 1, 3, 0):
        index = ((at_major[0] + by) % 4).astype(jnp.int32)
        part, minor = piece(index, turned, weights, gain, xs, cs, mix, minor)
        major.append(hop(part, MAJOR, 0, by) if by else part)

    def pick_minor(by):
        return lax.dynamic_index_in_dim(minor, (at_minor[0] + by) % 4, 0, keepdims=False)

    minor = [hop(pick_minor(by), MINOR, 0, by) for by in (2, 1, 3)] + [pick_minor(0)]
    minor = gathered(summed(minor, MINOR, at_minor[1]), MINOR)
    major = gathered(summed(major, MAJOR, at_major[1]), MAJOR)

    back = jnp.arange(4, dtype=jnp.int32)
    starts = jnp.stack(
        [
            ((at[0] - back) % 4)[:, None] * (features // 4)
            + ((at[1] - back) % 4)[None, :] * (features // 16)
            for at in (at_major, at_minor)
        ]
    ).astype(jnp.int32)
    down_step, up_step = finish(starts, major, minor, features, k)
    return down_step[None], up_step[None]


def solution(mesh):
    placed = (
        P("peer", None, None, None),
        P("peer", None, None, None),
        P("section", None, None, None),
        P("section", None, None, None),
        P("section", None, None),
        P(),
        P(),
    )
    return jax.shard_map(
        local,
        mesh=mesh,
        in_specs=placed,
        out_specs=(P("section", None, None, None), P("section", None, None, None)),
        check_vma=False,
    )
```

```python
import jax
import jax.numpy as jnp
from jax import lax
from jax.experimental import pallas as pl
from jax.experimental.pallas import tpu as pltpu
from jax.sharding import PartitionSpec as P

norm_eps = 1e-05
step_eps = 1e-06
bf16 = jnp.bfloat16
f32 = jnp.float32


def dot(a, b):
    return jnp.dot(a.astype(bf16), b.astype(bf16), preferred_element_type=f32)


def dot_nt(a, b):
    return lax.dot_general(
        a.astype(bf16), b.astype(bf16), (((1,), (1,)), ((), ())), preferred_element_type=f32
    )


def dot_tn(a, b):
    return lax.dot_general(
        a.astype(bf16), b.astype(bf16), (((0,), (0,)), ((), ())), preferred_element_type=f32
    )


def peer_table(wiring, live_mask):
    live_rank = jnp.cumsum(live_mask, axis=1) - 1
    matches = (live_mask[:, None, :] == 1) & (live_rank[:, None, :] == wiring[:, :, None])
    peer_ids = jnp.arange(live_mask.shape[1], dtype=jnp.int32)
    return jnp.sum(jnp.where(matches, peer_ids, 0), axis=2)


def row_sum(values):
    return jnp.sum(values, axis=1, keepdims=True)


def row_stage(proj, cot, square_sum, gram_low, gram_high, feature_count):
    k = cot[0].shape[1]

    def cut(g, i, j):
        return g[i * k : (i + 1) * k, j * k : (j + 1) * k].astype(bf16)

    ugd = {(0, 1): cut(gram_low, 0, 0), (2, 3): cut(gram_high, 0, 0)}
    uu = {
        (0, 0): cut(gram_low, 0, 1),
        (0, 1): cut(gram_low, 0, 2),
        (1, 1): cut(gram_low, 1, 2),
        (2, 2): cut(gram_high, 0, 1),
    }
    for i in (0, 1):
        ugd[(i, 2)] = cut(gram_low, i, 3)
        ugd[(i, 3)] = cut(gram_low, i, 4)
        uu[(i, 2)] = cut(gram_low, i, 5)

    hidden, active, inverse, full = [], [], [], []
    for l in range(4):
        r = lax.rsqrt(square_sum * (1.0 / feature_count) + norm_eps)
        pre = proj[l][0]
        for i in range(l):
            pre = pre + dot(active[i], ugd[(i, l)])
        h = r * pre
        a = (h * jax.nn.sigmoid(h)).astype(bf16)
        hidden.append(h)
        active.append(a)
        inverse.append(r)
        if l < 3:
            along = proj[l][1]
            for i in range(l):
                along = along + dot(active[i], uu[(i, l)])
            own = dot(a, uu[(l, l)])
            square_sum = square_sum + row_sum((2.0 * along + own) * a.astype(f32))
            full.append(along + own)

    back = [None] * 4
    weight = [None] * 4
    weight[3] = jnp.zeros_like(square_sum)
    for l in (3, 2, 1, 0):
        grad = cot[l]
        for j in range(l + 1, 4):
            grad = grad + dot_nt(back[j], ugd[(l, j)])
        if l < 3:
            grad = grad - weight[l] * full[l]
        for i in range(l + 1, 3):
            grad = grad - weight[i] * dot_nt(active[i], uu[(l, i)])
        sig = jax.nn.sigmoid(hidden[l])
        hid_grad = (grad * sig * (1.0 + hidden[l] * (1.0 - sig))).astype(bf16).astype(f32)
        back[l] = (inverse[l] * hid_grad).astype(bf16)
        if l > 0:
            centred = row_sum(hidden[l] * hid_grad) * (1.0 / feature_count)
            weight[l - 1] = weight[l] + inverse[l] * inverse[l] * centred
    less = [(-weight[l] * active[l].astype(f32)).astype(bf16) for l in range(4)]

    def scaled(w, l):
        return (-w * active[l].astype(f32)).astype(bf16)

    def against(left, parts):
        turned = left.astype(f32).T.astype(bf16)
        product = dot(turned, jnp.concatenate(parts, axis=1))
        return [product[:, i * k : (i + 1) * k] for i in range(len(parts))]

    a, b, w = active, back, weight
    a0 = against(a[0], [b[1], less[0], less[1], b[2], b[3], less[2]])
    a1 = against(a[1], [scaled(w[1], 0), less[1], b[2], b[3], less[2]])
    a2 = against(a[2], [scaled(w[2], 0), scaled(w[2], 1), b[3], less[2]])
    b1 = against(b[1], [a[0]])
    b2 = against(b[2], [a[0], a[1]])
    b3 = against(b[3], [a[0], a[1], a[2]])
    none = jnp.zeros((k, k), f32)
    mix_first = [
        [none, none, b1[0], none],
        [none, a0[0], a0[1], a0[2]],
        [none, none, a1[0], a1[1]],
        [none, none, b2[0], b2[1]],
        [none, none, b3[0], b3[1]],
        [none, none, a2[0], a2[1]],
    ]
    mix_second = [
        [none, none, none, none],
        [a0[3], a0[4], a0[5], none],
        [a1[2], a1[3], a1[4], none],
        [none, none, none, none],
        [none, none, b3[2], none],
        [none, a2[2], a2[3], none],
    ]
    return active, back, less, mix_first, mix_second


def in_hbm(*arrays):
    return [pltpu.with_memory_space_constraint(array, pltpu.HBM) for array in arrays]


def joined(parts):
    return jnp.concatenate(list(parts), axis=1)


def front(x, c, down, up, gain):
    lanes, rows, features = x.shape
    k = down.shape[2]
    block = 1024
    steps = features // block
    total = lanes * rows

    def kernel(x_ref, c_ref, d_ref, u_ref, g_ref, sent_ref, acc, squares, packed):
        step = pl.program_id(0)
        columns = jnp.concatenate([g_ref[...]] * 4, axis=0).T
        gained = [
            (d_ref[l].astype(f32) * columns[:, l : l + 1]).astype(bf16) for l in range(2)
        ]
        ups = [u_ref[0], u_ref[1]]
        flat = x_ref[...].reshape(total, block)
        of_x = dot(flat, joined(gained + ups))
        of_c = dot(c_ref[...].reshape(total, block), joined(ups))
        part = jnp.zeros((total, k), f32)
        for j in range(block // k):
            wide = flat[:, j * k : (j + 1) * k].astype(f32)
            part = part + wide * wide

        @pl.when(step == 0)
        def _():
            acc[:, : 4 * k] = of_x
            acc[:, 4 * k :] = of_c
            squares[...] = part

        @pl.when(step > 0)
        def _():
            acc[:, : 4 * k] += of_x
            acc[:, 4 * k :] += of_c
            squares[...] += part

        @pl.when(step == steps - 1)
        def _():
            for j in range(lanes):
                at = slice(j * rows, (j + 1) * rows)
                for half in range(2):
                    for t in range(3):
                        packed[t, pl.ds(2 * j + half, rows, stride=8), :] = acc[
                            at, (half * 3 + t) * k : (half * 3 + t + 1) * k
                        ]
                square = jnp.broadcast_to(row_sum(squares[at, :]), (rows, k))
                coarse = square.astype(bf16).astype(f32)
                packed[j, pl.ds(6, rows, stride=8), :] = coarse
                packed[j, pl.ds(7, rows, stride=8), :] = square - coarse
            for t in range(3):
                sent_ref[:, t * k : (t + 1) * k] = packed[t].astype(bf16)

    return pl.pallas_call(
        kernel,
        grid=(steps,),
        in_specs=[
            pl.BlockSpec((lanes, rows, block), lambda i: (0, 0, i)),
            pl.BlockSpec((lanes, rows, block), lambda i: (0, 0, i)),
            pl.BlockSpec((2, block, k), lambda i: (0, i, 0)),
            pl.BlockSpec((2, block, k), lambda i: (0, i, 0)),
            pl.BlockSpec((2, block), lambda i: (0, i)),
        ],
        out_specs=pl.BlockSpec((8 * rows, 3 * k), lambda i: (0, 0)),
        out_shape=jax.ShapeDtypeStruct((8 * rows, 3 * k), bf16),
        scratch_shapes=[
            pltpu.VMEM((total, 6 * k), f32),
            pltpu.VMEM((total, k), f32),
            pltpu.VMEM((3, 8 * rows, k), f32),
        ],
        compiler_params=pltpu.CompilerParams(vmem_limit_bytes=20 << 20),
        name="front",
    )(*in_hbm(x, c, down, up, gain))


def prepare(section, down, up, gain, down_other, up_other, gain_other):
    _, features, k = down.shape
    block = 1024
    steps = features // block

    def kernel(s_ref, d, u, g, d2, u2, g2, w_ref, low_out, high_out, low_ref, high_ref):
        step = pl.program_id(0)
        gains = jnp.concatenate([g[...], g2[...]] * 2, axis=0).T
        first = s_ref[0] == 0

        def choose(one, two):
            return jnp.where(first, one.astype(f32), two.astype(f32))

        gain_one = choose(gains[:, :2], gains[:, 2:4])
        gain_two = choose(gains[:, 2:4], gains[:, :2])
        parts = [
            choose(d[1], d2[1]) * gain_one[:, 1:2],
            choose(u[0], u2[0]),
            choose(u[1], u2[1]),
            choose(d2[0], d[0]) * gain_two[:, :1],
            choose(d2[1], d[1]) * gain_two[:, 1:2],
            choose(u2[0], u[0]),
        ]
        parts = [part.astype(bf16) for part in parts]
        weights = joined(parts)
        w_ref[...] = weights
        low = dot_tn(joined(parts[1:3]), weights)
        high = dot_tn(parts[5], joined(parts[4:]))

        @pl.when(step == 0)
        def _():
            low_ref[...] = low
            high_ref[...] = high

        @pl.when(step > 0)
        def _():
            low_ref[...] += low
            high_ref[...] += high

        @pl.when(step == steps - 1)
        def _():
            low_out[...] = low_ref[...].astype(bf16)
            high_out[...] = high_ref[...].astype(bf16)

    two = pl.BlockSpec((2, block, k), lambda i, s: (0, i, 0))
    row = pl.BlockSpec((2, block), lambda i, s: (0, i))
    return pl.pallas_call(
        kernel,
        grid_spec=pltpu.PrefetchScalarGridSpec(
            num_scalar_prefetch=1,
            grid=(steps,),
            in_specs=[two, two, row, two, two, row],
            out_specs=[
                pl.BlockSpec((block, 6 * k), lambda i, s: (i, 0)),
                pl.BlockSpec((2 * k, 6 * k), lambda i, s: (0, 0)),
                pl.BlockSpec((k, 2 * k), lambda i, s: (0, 0)),
            ],
            scratch_shapes=[pltpu.VMEM((2 * k, 6 * k), f32), pltpu.VMEM((k, 2 * k), f32)],
        ),
        out_shape=[
            pltpu.HBM((features, 6 * k), bf16),
            pltpu.HBM((2 * k, 6 * k), bf16),
            pltpu.HBM((k, 2 * k), bf16),
        ],
        compiler_params=pltpu.CompilerParams(vmem_limit_bytes=24 << 20),
        name="prepare",
    )(section[None], *in_hbm(down, up, gain), down_other, up_other, gain_other)


def turn(x, c):
    lanes, rows, features = x.shape
    block = 1024

    def kernel(x_ref, c_ref, out):
        for j in range(lanes):
            out[:, j * rows : (j + 1) * rows] = x_ref[j].T
            out[:, (lanes + j) * rows : (lanes + j + 1) * rows] = c_ref[j].T

    spec = pl.BlockSpec((lanes, rows, block), lambda i: (0, 0, i))
    return pl.pallas_call(
        kernel,
        grid=(features // block,),
        in_specs=[spec, spec],
        out_specs=pl.BlockSpec((block, 2 * lanes * rows), lambda i: (i, 0)),
        out_shape=pltpu.HBM((features, 2 * lanes * rows), bf16),
        compiler_params=pltpu.CompilerParams(vmem_limit_bytes=12 << 20),
        name="turn",
    )(*in_hbm(x, c))


def meet(section, received, first, second, gram_low, gram_high, lanes, features):
    total = first.shape[0]
    group = total // lanes
    slots = received.shape[1]
    k = received.shape[2] // 3

    def kernel(mine, rec, columns, rows, far_low, far_high, out, own, oth, low, high, sems):
        copies = [
            pltpu.make_async_copy(far_low, low, sems.at[0]),
            pltpu.make_async_copy(far_high, high, sems.at[1]),
        ]
        for copy in copies:
            copy.start()
        i0, i1 = columns[:, :1], columns[:, 1:]
        t0, t1 = rows[:1, :], rows[1:, :]
        grid = lax.broadcasted_iota(jnp.int32, (total, slots), 1)
        turned = lax.broadcasted_iota(jnp.int32, (slots, total), 0)

        def pick(base):
            return (grid == base).astype(f32).astype(bf16)

        def place(base):
            return (turned == base).astype(f32).astype(bf16)

        at_start = pick(i0)
        at_start_next = pick(i0 + 1)
        at_end = pick(i1 + 1)
        lane = lax.broadcasted_iota(jnp.int32, (total, 1), 0) // group
        norm_row = i0 - 2 * lane + 6
        sums = dot(pick(norm_row), rec[0]) + dot(pick(norm_row + 1), rec[0])
        square_sum = jnp.concatenate(
            [sums[j * group : (j + 1) * group, j * k : (j + 1) * k] for j in range(lanes)], axis=0
        )[:, :1]
        proj, cot = [], []
        for s in range(2):
            near = dot(at_start, rec[s])
            next_up = dot(at_start_next, rec[s, :, :k])
            tail = dot(at_end, rec[s, :, k:])
            proj += [(near[:, :k], near[:, 2 * k :]), (near[:, k : 2 * k], next_up)]
            cot += [tail[:, :k], tail[:, k:]]
        for copy in copies:
            copy.wait()
        active, back, less, mix_first, mix_second = row_stage(
            proj, cot, square_sum, low[...], high[...], features
        )
        to_start = place(t0)
        to_start_next = place(t0 + 1)
        to_end = place(t1 + 1)
        for s in range(2):
            l0, l1 = 2 * s, 2 * s + 1
            out[s] = dot(to_start, joined([back[l0], back[l1], less[l0]])).astype(bf16)
            weighted = dot(to_start_next, less[l1])
            tail = dot(to_end, joined([active[l0], active[l1]]))
            out[s] += joined([weighted, tail]).astype(bf16)
        first_section = mine[0] == 0
        for i, (one, two) in enumerate(zip(mix_first, mix_second)):
            at = slice(i * k, (i + 1) * k)
            one, two = joined(one), joined(two)
            own[at, :] = jnp.where(first_section, one, two).astype(bf16)
            oth[at, :] = jnp.where(first_section, two, one).astype(bf16)

    columns = jnp.stack([first, second], axis=1)
    rows = jnp.stack([first, second])
    local_ref = pl.BlockSpec(memory_space=pltpu.VMEM)
    far_ref = pl.BlockSpec(memory_space=pl.ANY)
    mix = jax.ShapeDtypeStruct((6 * k, 4 * k), bf16)
    return pl.pallas_call(
        kernel,
        in_specs=[pl.BlockSpec(memory_space=pltpu.SMEM)] + [local_ref] * 3 + [far_ref] * 2,
        out_shape=[jax.ShapeDtypeStruct(received.shape, bf16), mix, mix],
        scratch_shapes=[
            pltpu.VMEM(gram_low.shape, bf16),
            pltpu.VMEM(gram_high.shape, bf16),
            pltpu.SemaphoreType.DMA((2,)),
        ],
        compiler_params=pltpu.CompilerParams(vmem_limit_bytes=16 << 20),
        name="meet",
    )(section[None], received, columns, rows, *in_hbm(gram_low, gram_high))


def unpack(returned, mix_own, mix_other, lanes):
    rows, k = returned.shape[0] // 8, returned.shape[1] // 3

    def kernel(ret, own, far, xs, cs, mix, wide, oth, sem):
        copy = pltpu.make_async_copy(far, oth, sem)
        copy.start()
        for t in range(3):
            wide[t] = ret[:, t * k : (t + 1) * k].astype(f32)
        for j in range(lanes):
            at = slice(j * rows, (j + 1) * rows)
            low = [wide[t, pl.ds(2 * j, rows, stride=8), :].astype(bf16) for t in range(3)]
            high = [wide[t, pl.ds(2 * j + 1, rows, stride=8), :].astype(bf16) for t in range(3)]
            xs[at, :] = joined(low + high[:1])
            cs[at, :] = joined(high[1:])
        copy.wait()
        mix[...] = (own[...].astype(f32) + oth[...].astype(f32)).astype(bf16)

    local_ref = pl.BlockSpec(memory_space=pltpu.VMEM)
    shapes = [(lanes * rows, 4 * k), (lanes * rows, 2 * k), mix_own.shape]
    return pl.pallas_call(
        kernel,
        in_specs=[local_ref, local_ref, pl.BlockSpec(memory_space=pl.ANY)],
        out_shape=[jax.ShapeDtypeStruct(shape, bf16) for shape in shapes],
        scratch_shapes=[
            pltpu.VMEM((3, 8 * rows, k), f32),
            pltpu.VMEM(mix_own.shape, bf16),
            pltpu.SemaphoreType.DMA,
        ],
        compiler_params=pltpu.CompilerParams(vmem_limit_bytes=8 << 20),
        name="unpack",
    )(returned, mix_own, *in_hbm(mix_other))


def piece(at, size, turned, weights, xs, cs, mix):
    both = turned.shape[1]
    k = cs.shape[1] // 2
    total = both // 2
    parts = 4
    chunk = size // parts

    def kernel(at_ref, t_ref, w_ref, xs_ref, cs_ref, mix_ref, major, minor, t_buf, w_buf, sems):
        copies = []
        for i in range(parts):
            rows = pl.ds(pl.multiple_of(at_ref[0] + i * chunk, 16), chunk)
            copies.append(
                [
                    pltpu.make_async_copy(t_ref.at[rows, :], t_buf.at[i], sems.at[i, 0]),
                    pltpu.make_async_copy(w_ref.at[rows, :], w_buf.at[i], sems.at[i, 1]),
                ]
            )
        for copy in copies[0] + copies[1]:
            copy.start()
        for i in range(parts):
            rows = slice(i * chunk, (i + 1) * chunk)
            for copy in copies[i]:
                copy.wait()
            if i + 2 < parts:
                for copy in copies[i + 2]:
                    copy.start()
            value = dot(t_buf[i, :, :total], xs_ref[...]) + dot(w_buf[i], mix_ref[...])
            last = dot(t_buf[i, :, total:], cs_ref[...])
            major[rows, : 2 * k] = value[:, : 2 * k].astype(bf16)
            major[rows, 2 * k :] = (value[:, 2 * k : 3 * k] + last[:, :k]).astype(bf16)
            minor[rows, :] = (value[:, 3 * k :] + last[:, k:]).astype(bf16)

    local_ref = pl.BlockSpec(memory_space=pltpu.VMEM)
    far_ref = pl.BlockSpec(memory_space=pl.ANY)
    return pl.pallas_call(
        kernel,
        in_specs=[pl.BlockSpec(memory_space=pltpu.SMEM)] + [far_ref] * 2 + [local_ref] * 3,
        out_specs=[local_ref] * 2,
        out_shape=[
            jax.ShapeDtypeStruct((size, 3 * k), bf16),
            jax.ShapeDtypeStruct((size, k), bf16),
        ],
        scratch_shapes=[
            pltpu.VMEM((parts, chunk, both), bf16),
            pltpu.VMEM((parts, chunk, 6 * k), bf16),
            pltpu.SemaphoreType.DMA((parts, 2)),
        ],
        compiler_params=pltpu.CompilerParams(vmem_limit_bytes=16 << 20),
        name="piece",
    )(at[None], *in_hbm(turned, weights), xs, cs, mix)


def squares(block):
    rows, width = block.shape

    def kernel(ref, out):
        v = ref[...].astype(f32)
        out[...] = jnp.sum((v * v).reshape(4, rows // 32, 8, width), axis=1)

    return pl.pallas_call(
        kernel,
        out_shape=jax.ShapeDtypeStruct((4, 8, width), f32),
        compiler_params=pltpu.CompilerParams(vmem_limit_bytes=8 << 20),
        name="squares",
    )(block)


def finish(starts, major, minor, features, k):
    quarter = features // 4
    part = quarter // 4
    late = 2
    early = [i for i in range(4) if i != late]
    blocks = [*major, *minor]
    known = [squares(major[i]) for i in early] + [squares(minor[i]) for i in early]

    def kernel(at, *refs):
        ins, known, (down, up) = refs[:8], refs[8:14], refs[14:]
        group = pl.program_id(0)

        def run(which, out):
            sums = [None] * 4
            for i in range(4):
                if i == late:
                    v = ins[which * 4 + i][...].astype(f32)
                    v = jnp.sum((v * v).reshape(4, part // 8, 8, k), axis=1)
                else:
                    v = known[which * 3 + early.index(i)][...]
                sums[i] = ring_sum(v[0], v[2], v[1], v[3])
            total = ring_sum(sums[0], sums[2], sums[1], sums[3])
            mean = jnp.sum(total) * (1.0 / (features * k))
            scale = lax.rsqrt(jnp.full((1, k), mean, f32) + step_eps)
            for i in range(4):
                for j in range(4):
                    row = pl.multiple_of(at[which, i, j], 16)
                    v = ins[which * 4 + i][j * part : (j + 1) * part, :].astype(f32)
                    out[0, pl.ds(row, part), :] = (v * scale).astype(bf16)

        @pl.when(group < 2)
        def _():
            run(0, down)

        @pl.when(group == 2)
        def _():
            run(0, up)

        @pl.when(group == 3)
        def _():
            run(1, up)

    def specs(shape, columns):
        zeros = (0,) * (len(shape) - 1)
        return pl.BlockSpec(shape, lambda g, at: (*zeros, columns(g)))

    def clipped(g):
        return jnp.minimum(g, 2)

    def fixed(g):
        return 0

    return pl.pallas_call(
        kernel,
        grid_spec=pltpu.PrefetchScalarGridSpec(
            num_scalar_prefetch=1,
            grid=(4,),
            in_specs=[specs((quarter, k), clipped)] * 4
            + [specs((quarter, k), fixed)] * 4
            + [specs((4, 8, k), clipped)] * 3
            + [specs((4, 8, k), fixed)] * 3,
            out_specs=[
                pl.BlockSpec((1, features, k), lambda g, at: (jnp.minimum(g, 1), 0, 0)),
                pl.BlockSpec((1, features, k), lambda g, at: (jnp.maximum(g - 2, 0), 0, 0)),
            ],
        ),
        out_shape=[jax.ShapeDtypeStruct((2, features, k), bf16)] * 2,
        compiler_params=pltpu.CompilerParams(vmem_limit_bytes=16 << 20),
        name="finish",
    )(starts, *blocks, *known)


def coords(peer):
    return peer // 16, (peer // 4) % 4, peer % 4


MAJOR = ((0, 1, 2), (1, 2, 0))
MINOR = ((2, 1, 0), (2, 0, 1))


def hop(values, order, stage, by):
    pairs = []
    for s in range(2):
        axis = order[s][stage]
        for p in range(64):
            c = list(coords(p))
            c[axis] = (c[axis] + by) % 4
            pairs.append((s * 64 + p, s * 64 + c[0] * 16 + c[1] * 4 + c[2]))
    return lax.ppermute(values, ("section", "peer"), pairs)


def ring_sum(own, two, one, three):
    return (own + two) + (one + three)


def summed(parts, order, at, gains=None):
    step = parts[0].shape[0] // 4

    def cut(by):
        start = ((at[1] + by) % 4) * step
        return sum(lax.dynamic_slice_in_dim(p, start, step, axis=0).astype(f32) for p in parts)

    arrived = [hop(cut(by).astype(bf16), order, 1, by) for by in (2, 1, 3)]
    own = cut(0) + sum(part.astype(f32) for part in arrived)
    own = lax.optimization_barrier(own.astype(bf16))
    two, one, three = [hop(own, order, 2, by).astype(f32) for by in (2, 1, 3)]
    total = ring_sum(own.astype(f32), two, one, three)
    return (total if gains is None else total * gains).astype(bf16)


def gathered(block, order):
    wide = jnp.concatenate([block] + [hop(block, order, 1, by) for by in (1, 2, 3)], axis=0)
    return [wide] + [hop(wide, order, 0, by) for by in (1, 2, 3)]


def local(inputs, cotangent, down_proj, up_proj, norm_gain, wiring, live_mask):
    section = lax.axis_index("section")
    peer = lax.axis_index("peer")
    _, lanes, rows, features = inputs.shape
    k = down_proj.shape[3]
    x, c = inputs[0], cotangent[0]
    gain, up = norm_gain[0], up_proj[0]
    is_first = section == 0
    swap = [(0, 1), (1, 0)]
    down = down_proj[0]
    down_other = lax.ppermute(down, "section", swap)
    up_other = lax.ppermute(up, "section", swap)
    gain_other = lax.ppermute(gain, "section", swap)
    sent = front(x, c, down, up, gain)
    received = lax.all_to_all(
        sent.reshape(rows, 8, 3 * k), ("section", "peer"), 0, 0, tiled=True
    ).reshape(2, -1, 3 * k)
    weights, gram_low, gram_high = prepare(
        section, down, up, gain, down_other, up_other, gain_other
    )
    holders = peer_table(wiring, live_mask)
    total = holders.shape[1]
    lane_of = jnp.arange(total, dtype=jnp.int32) // (total // lanes)
    base = holders * 8 + 2 * lane_of
    out, mix_own, mix_leaving = meet(
        section, received, base[0], base[1], gram_low, gram_high, lanes, features
    )
    mix_other = lax.ppermute(mix_leaving, "section", swap)
    returned = lax.all_to_all(
        out.reshape(rows, 8, 3 * k), ("section", "peer"), 0, 0, tiled=True
    ).reshape(8 * rows, 3 * k)
    turned = turn(*lax.optimization_barrier((x, c, mix_own))[:2])
    xs, cs, mix = unpack(returned, mix_own, mix_other, lanes)

    where = jnp.stack(coords(peer))
    at_major, at_minor = (
        [jnp.where(is_first, where[order[0][i]], where[order[1][i]]) for i in range(3)]
        for order in (MAJOR, MINOR)
    )
    quarter = features // 4
    major, minor = [], []
    for by in (2, 1, 3, 0):
        index = ((at_major[0] + by) % 4) * quarter
        part, rest = piece(index.astype(jnp.int32), quarter, turned, weights, xs, cs, mix)
        major.append(hop(part, MAJOR, 0, by) if by else part)
        minor.append(rest)

    def pick_minor(by):
        ahead = (at_minor[0] + by - at_major[0]) % 4
        return lax.select_n(
            jnp.broadcast_to(ahead, minor[0].shape), minor[3], minor[1], minor[0], minor[2]
        )

    step = features // 16
    row = at_major[0] * quarter + at_major[1] * step
    gains = lax.dynamic_slice_in_dim(gain, row, step, axis=1).T
    gains = joined([jnp.broadcast_to(gains[:, l : l + 1], (step, k)) for l in range(2)])
    gains = joined([gains, jnp.ones((step, k), f32)])
    minor = [hop(pick_minor(by), MINOR, 0, by) for by in (2, 1, 3)] + [pick_minor(0)]
    minor = gathered(summed(minor, MINOR, at_minor), MINOR)
    major = gathered(summed(major, MAJOR, at_major, gains), MAJOR)

    back = jnp.arange(4, dtype=jnp.int32)
    starts = jnp.stack(
        [
            ((at[0] - back) % 4)[:, None] * quarter + ((at[1] - back) % 4)[None, :] * step
            for at in (at_major, at_minor)
        ]
    ).astype(jnp.int32)
    down_step, up_step = finish(starts, major, minor, features, k)
    return down_step[None], up_step[None]


def solution(mesh):
    placed = (
        P("peer", None, None, None),
        P("peer", None, None, None),
        P("section", None, None, None),
        P("section", None, None, None),
        P("section", None, None),
        P(),
        P(),
    )
    return jax.shard_map(
        local,
        mesh=mesh,
        in_specs=placed,
        out_specs=(P("section", None, None, None), P("section", None, None, None)),
        check_vma=False,
    )
```

```python
import jax
import jax.numpy as jnp
from jax import lax
from jax.experimental import pallas as pl
from jax.experimental.pallas import tpu as pltpu
from jax.sharding import PartitionSpec as P

norm_eps = 1e-05
step_eps = 1e-06
bf16 = jnp.bfloat16
f32 = jnp.float32


def dot(a, b):
    return jnp.dot(a.astype(bf16), b.astype(bf16), preferred_element_type=f32)


def dot_nt(a, b):
    return lax.dot_general(
        a.astype(bf16), b.astype(bf16), (((1,), (1,)), ((), ())), preferred_element_type=f32
    )


def dot_tn(a, b):
    return lax.dot_general(
        a.astype(bf16), b.astype(bf16), (((0,), (0,)), ((), ())), preferred_element_type=f32
    )


def peer_table(wiring, live_mask):
    live_rank = jnp.cumsum(live_mask, axis=1) - 1
    matches = (live_mask[:, None, :] == 1) & (live_rank[:, None, :] == wiring[:, :, None])
    peer_ids = jnp.arange(live_mask.shape[1], dtype=jnp.int32)
    return jnp.sum(jnp.where(matches, peer_ids, 0), axis=2)


def row_sum(values):
    return jnp.sum(values, axis=1, keepdims=True)


def row_stage(proj, cot, square_sum, gram_low, gram_high, feature_count):
    k = cot[0].shape[1]

    def cut(g, i, j):
        return g[i * k : (i + 1) * k, j * k : (j + 1) * k].astype(bf16)

    ugd = {(0, 1): cut(gram_low, 0, 0), (2, 3): cut(gram_high, 0, 0)}
    uu = {
        (0, 0): cut(gram_low, 0, 1),
        (0, 1): cut(gram_low, 0, 2),
        (1, 1): cut(gram_low, 1, 2),
        (2, 2): cut(gram_high, 0, 1),
    }
    for i in (0, 1):
        ugd[(i, 2)] = cut(gram_low, i, 3)
        ugd[(i, 3)] = cut(gram_low, i, 4)
        uu[(i, 2)] = cut(gram_low, i, 5)

    hidden, active, inverse, full = [], [], [], []
    for l in range(4):
        r = lax.rsqrt(square_sum * (1.0 / feature_count) + norm_eps)
        pre = proj[l][0]
        for i in range(l):
            pre = pre + dot(active[i], ugd[(i, l)])
        h = r * pre
        a = (h * jax.nn.sigmoid(h)).astype(bf16)
        hidden.append(h)
        active.append(a)
        inverse.append(r)
        if l < 3:
            along = proj[l][1]
            for i in range(l):
                along = along + dot(active[i], uu[(i, l)])
            own = dot(a, uu[(l, l)])
            square_sum = square_sum + row_sum((2.0 * along + own) * a.astype(f32))
            full.append(along + own)

    back = [None] * 4
    weight = [None] * 4
    weight[3] = jnp.zeros_like(square_sum)
    for l in (3, 2, 1, 0):
        grad = cot[l]
        for j in range(l + 1, 4):
            grad = grad + dot_nt(back[j], ugd[(l, j)])
        if l < 3:
            grad = grad - weight[l] * full[l]
        for i in range(l + 1, 3):
            grad = grad - weight[i] * dot_nt(active[i], uu[(l, i)])
        sig = jax.nn.sigmoid(hidden[l])
        hid_grad = (grad * sig * (1.0 + hidden[l] * (1.0 - sig))).astype(bf16).astype(f32)
        back[l] = (inverse[l] * hid_grad).astype(bf16)
        if l > 0:
            centred = row_sum(hidden[l] * hid_grad) * (1.0 / feature_count)
            weight[l - 1] = weight[l] + inverse[l] * inverse[l] * centred
    less = [(-weight[l] * active[l].astype(f32)).astype(bf16) for l in range(4)]

    def scaled(w, l):
        return (-w * active[l].astype(f32)).astype(bf16)

    def against(left, parts):
        turned = left.astype(f32).T.astype(bf16)
        product = dot(turned, jnp.concatenate(parts, axis=1))
        return [product[:, i * k : (i + 1) * k] for i in range(len(parts))]

    a, b, w = active, back, weight
    a0 = against(a[0], [b[1], less[0], less[1], b[2], b[3], less[2]])
    a1 = against(a[1], [scaled(w[1], 0), less[1], b[2], b[3], less[2]])
    a2 = against(a[2], [scaled(w[2], 0), scaled(w[2], 1), b[3], less[2]])
    b1 = against(b[1], [a[0]])
    b2 = against(b[2], [a[0], a[1]])
    b3 = against(b[3], [a[0], a[1], a[2]])
    none = jnp.zeros((k, k), f32)
    mix_first = [
        [none, none, b1[0], none],
        [none, a0[0], a0[1], a0[2]],
        [none, none, a1[0], a1[1]],
        [none, none, b2[0], b2[1]],
        [none, none, b3[0], b3[1]],
        [none, none, a2[0], a2[1]],
    ]
    mix_second = [
        [none, none, none, none],
        [a0[3], a0[4], a0[5], none],
        [a1[2], a1[3], a1[4], none],
        [none, none, none, none],
        [none, none, b3[2], none],
        [none, a2[2], a2[3], none],
    ]
    return active, back, less, mix_first, mix_second


def in_hbm(*arrays):
    return [pltpu.with_memory_space_constraint(array, pltpu.HBM) for array in arrays]


def joined(parts):
    return jnp.concatenate(list(parts), axis=1)


def front(x, c, down, up, gain):
    lanes, rows, features = x.shape
    k = down.shape[2]
    block = 1024
    steps = features // block
    total = lanes * rows

    def kernel(x_ref, c_ref, d_ref, u_ref, g_ref, sent_ref, acc, squares, packed):
        step = pl.program_id(0)
        columns = jnp.concatenate([g_ref[...]] * 4, axis=0).T
        gained = [
            (d_ref[l].astype(f32) * columns[:, l : l + 1]).astype(bf16) for l in range(2)
        ]
        ups = [u_ref[0], u_ref[1]]
        flat = x_ref[...].reshape(total, block)
        of_x = dot(flat, joined(gained + ups))
        of_c = dot(c_ref[...].reshape(total, block), joined(ups))
        part = jnp.zeros((total, k), f32)
        for j in range(block // k):
            wide = flat[:, j * k : (j + 1) * k].astype(f32)
            part = part + wide * wide

        @pl.when(step == 0)
        def _():
            acc[:, : 4 * k] = of_x
            acc[:, 4 * k :] = of_c
            squares[...] = part

        @pl.when(step > 0)
        def _():
            acc[:, : 4 * k] += of_x
            acc[:, 4 * k :] += of_c
            squares[...] += part

        @pl.when(step == steps - 1)
        def _():
            for j in range(lanes):
                at = slice(j * rows, (j + 1) * rows)
                for half in range(2):
                    for t in range(3):
                        packed[t, pl.ds(2 * j + half, rows, stride=8), :] = acc[
                            at, (half * 3 + t) * k : (half * 3 + t + 1) * k
                        ]
                square = jnp.broadcast_to(row_sum(squares[at, :]), (rows, k))
                coarse = square.astype(bf16).astype(f32)
                packed[j, pl.ds(6, rows, stride=8), :] = coarse
                packed[j, pl.ds(7, rows, stride=8), :] = square - coarse
            for t in range(3):
                sent_ref[:, t * k : (t + 1) * k] = packed[t].astype(bf16)

    return pl.pallas_call(
        kernel,
        grid=(steps,),
        in_specs=[
            pl.BlockSpec((lanes, rows, block), lambda i: (0, 0, i)),
            pl.BlockSpec((lanes, rows, block), lambda i: (0, 0, i)),
            pl.BlockSpec((2, block, k), lambda i: (0, i, 0)),
            pl.BlockSpec((2, block, k), lambda i: (0, i, 0)),
            pl.BlockSpec((2, block), lambda i: (0, i)),
        ],
        out_specs=pl.BlockSpec((8 * rows, 3 * k), lambda i: (0, 0)),
        out_shape=jax.ShapeDtypeStruct((8 * rows, 3 * k), bf16),
        scratch_shapes=[
            pltpu.VMEM((total, 6 * k), f32),
            pltpu.VMEM((total, k), f32),
            pltpu.VMEM((3, 8 * rows, k), f32),
        ],
        compiler_params=pltpu.CompilerParams(vmem_limit_bytes=20 << 20),
        name="front",
    )(*in_hbm(x, c, down, up, gain))


def prepare(section, down, up, gain, down_other, up_other, gain_other):
    _, features, k = down.shape
    block = 1024
    steps = features // block

    def kernel(s_ref, d, u, g, d2, u2, g2, w_ref, low_out, high_out, low_ref, high_ref):
        step = pl.program_id(0)
        gains = jnp.concatenate([g[...], g2[...]] * 2, axis=0).T
        first = s_ref[0] == 0

        def choose(one, two):
            return jnp.where(first, one.astype(f32), two.astype(f32))

        gain_one = choose(gains[:, :2], gains[:, 2:4])
        gain_two = choose(gains[:, 2:4], gains[:, :2])
        parts = [
            choose(d[1], d2[1]) * gain_one[:, 1:2],
            choose(u[0], u2[0]),
            choose(u[1], u2[1]),
            choose(d2[0], d[0]) * gain_two[:, :1],
            choose(d2[1], d[1]) * gain_two[:, 1:2],
            choose(u2[0], u[0]),
        ]
        parts = [part.astype(bf16) for part in parts]
        weights = joined(parts)
        w_ref[...] = weights
        low = dot_tn(joined(parts[1:3]), weights)
        high = dot_tn(parts[5], joined(parts[4:]))

        @pl.when(step == 0)
        def _():
            low_ref[...] = low
            high_ref[...] = high

        @pl.when(step > 0)
        def _():
            low_ref[...] += low
            high_ref[...] += high

        @pl.when(step == steps - 1)
        def _():
            low_out[...] = low_ref[...].astype(bf16)
            high_out[...] = high_ref[...].astype(bf16)

    two = pl.BlockSpec((2, block, k), lambda i, s: (0, i, 0))
    row = pl.BlockSpec((2, block), lambda i, s: (0, i))
    return pl.pallas_call(
        kernel,
        grid_spec=pltpu.PrefetchScalarGridSpec(
            num_scalar_prefetch=1,
            grid=(steps,),
            in_specs=[two, two, row, two, two, row],
            out_specs=[
                pl.BlockSpec((block, 6 * k), lambda i, s: (i, 0)),
                pl.BlockSpec((2 * k, 6 * k), lambda i, s: (0, 0)),
                pl.BlockSpec((k, 2 * k), lambda i, s: (0, 0)),
            ],
            scratch_shapes=[pltpu.VMEM((2 * k, 6 * k), f32), pltpu.VMEM((k, 2 * k), f32)],
        ),
        out_shape=[
            pltpu.HBM((features, 6 * k), bf16),
            pltpu.HBM((2 * k, 6 * k), bf16),
            pltpu.HBM((k, 2 * k), bf16),
        ],
        compiler_params=pltpu.CompilerParams(vmem_limit_bytes=24 << 20),
        name="prepare",
    )(section[None], *in_hbm(down, up, gain), down_other, up_other, gain_other)


def turn(x, c):
    lanes, rows, features = x.shape
    block = 1024

    def kernel(x_ref, c_ref, out):
        for j in range(lanes):
            out[:, j * rows : (j + 1) * rows] = x_ref[j].T
            out[:, (lanes + j) * rows : (lanes + j + 1) * rows] = c_ref[j].T

    spec = pl.BlockSpec((lanes, rows, block), lambda i: (0, 0, i))
    return pl.pallas_call(
        kernel,
        grid=(features // block,),
        in_specs=[spec, spec],
        out_specs=pl.BlockSpec((block, 2 * lanes * rows), lambda i: (i, 0)),
        out_shape=pltpu.HBM((features, 2 * lanes * rows), bf16),
        compiler_params=pltpu.CompilerParams(vmem_limit_bytes=12 << 20),
        name="turn",
    )(*in_hbm(x, c))


def meet(section, received, first, second, gram_low, gram_high, lanes, features):
    total = first.shape[0]
    group = total // lanes
    slots = received.shape[1]
    k = received.shape[2] // 3

    def kernel(mine, rec, columns, rows, far_low, far_high, out, own, oth, low, high, sems):
        copies = [
            pltpu.make_async_copy(far_low, low, sems.at[0]),
            pltpu.make_async_copy(far_high, high, sems.at[1]),
        ]
        for copy in copies:
            copy.start()
        i0, i1 = columns[:, :1], columns[:, 1:]
        t0, t1 = rows[:1, :], rows[1:, :]
        grid = lax.broadcasted_iota(jnp.int32, (total, slots), 1)
        turned = lax.broadcasted_iota(jnp.int32, (slots, total), 0)

        def pick(base):
            return (grid == base).astype(f32).astype(bf16)

        def place(base):
            return (turned == base).astype(f32).astype(bf16)

        at_start = pick(i0)
        at_start_next = pick(i0 + 1)
        at_end = pick(i1 + 1)
        lane = lax.broadcasted_iota(jnp.int32, (total, 1), 0) // group
        norm_row = i0 - 2 * lane + 6
        sums = dot(pick(norm_row), rec[0]) + dot(pick(norm_row + 1), rec[0])
        square_sum = jnp.concatenate(
            [sums[j * group : (j + 1) * group, j * k : (j + 1) * k] for j in range(lanes)], axis=0
        )[:, :1]
        proj, cot = [], []
        for s in range(2):
            near = dot(at_start, rec[s])
            next_up = dot(at_start_next, rec[s, :, :k])
            tail = dot(at_end, rec[s, :, k:])
            proj += [(near[:, :k], near[:, 2 * k :]), (near[:, k : 2 * k], next_up)]
            cot += [tail[:, :k], tail[:, k:]]
        to_start = place(t0)
        to_start_next = place(t0 + 1)
        to_end = place(t1 + 1)
        for copy in copies:
            copy.wait()
        active, back, less, mix_first, mix_second = row_stage(
            proj, cot, square_sum, low[...], high[...], features
        )
        for s in range(2):
            l0, l1 = 2 * s, 2 * s + 1
            out[s] = dot(to_start, joined([back[l0], back[l1], less[l0]])).astype(bf16)
            weighted = dot(to_start_next, less[l1])
            tail = dot(to_end, joined([active[l0], active[l1]]))
            out[s] += joined([weighted, tail]).astype(bf16)
        first_section = mine[0] == 0
        for i, (one, two) in enumerate(zip(mix_first, mix_second)):
            at = slice(i * k, (i + 1) * k)
            one, two = joined(one), joined(two)
            own[at, :] = jnp.where(first_section, one, two).astype(bf16)
            oth[at, :] = jnp.where(first_section, two, one).astype(bf16)

    columns = jnp.stack([first, second], axis=1)
    rows = jnp.stack([first, second])
    local_ref = pl.BlockSpec(memory_space=pltpu.VMEM)
    far_ref = pl.BlockSpec(memory_space=pl.ANY)
    mix = jax.ShapeDtypeStruct((6 * k, 4 * k), bf16)
    return pl.pallas_call(
        kernel,
        in_specs=[pl.BlockSpec(memory_space=pltpu.SMEM)] + [local_ref] * 3 + [far_ref] * 2,
        out_shape=[jax.ShapeDtypeStruct(received.shape, bf16), mix, mix],
        scratch_shapes=[
            pltpu.VMEM(gram_low.shape, bf16),
            pltpu.VMEM(gram_high.shape, bf16),
            pltpu.SemaphoreType.DMA((2,)),
        ],
        compiler_params=pltpu.CompilerParams(vmem_limit_bytes=16 << 20),
        name="meet",
    )(section[None], received, columns, rows, *in_hbm(gram_low, gram_high))


def unpack(returned, mix_own, mix_other, lanes):
    rows, k = returned.shape[0] // 8, returned.shape[1] // 3

    def kernel(ret, own, far, xs, cs, mix, wide, oth, sem):
        copy = pltpu.make_async_copy(far, oth, sem)
        copy.start()
        for t in range(3):
            wide[t] = ret[:, t * k : (t + 1) * k].astype(f32)
        for j in range(lanes):
            at = slice(j * rows, (j + 1) * rows)
            low = [wide[t, pl.ds(2 * j, rows, stride=8), :].astype(bf16) for t in range(3)]
            high = [wide[t, pl.ds(2 * j + 1, rows, stride=8), :].astype(bf16) for t in range(3)]
            xs[at, :] = joined(low + high[:1])
            cs[at, :] = joined(high[1:])
        copy.wait()
        mix[...] = (own[...].astype(f32) + oth[...].astype(f32)).astype(bf16)

    local_ref = pl.BlockSpec(memory_space=pltpu.VMEM)
    shapes = [(lanes * rows, 4 * k), (lanes * rows, 2 * k), mix_own.shape]
    return pl.pallas_call(
        kernel,
        in_specs=[local_ref, local_ref, pl.BlockSpec(memory_space=pl.ANY)],
        out_shape=[jax.ShapeDtypeStruct(shape, bf16) for shape in shapes],
        scratch_shapes=[
            pltpu.VMEM((3, 8 * rows, k), f32),
            pltpu.VMEM(mix_own.shape, bf16),
            pltpu.SemaphoreType.DMA,
        ],
        compiler_params=pltpu.CompilerParams(vmem_limit_bytes=8 << 20),
        name="unpack",
    )(returned, mix_own, *in_hbm(mix_other))


def piece(at, size, turned, weights, xs, cs, mix):
    both = turned.shape[1]
    k = cs.shape[1] // 2
    total = both // 2
    parts = 2
    chunk = size // parts

    def kernel(at_ref, t_ref, w_ref, xs_ref, cs_ref, mix_ref, major, minor, t_buf, w_buf, sems):
        copies = []
        for i in range(parts):
            rows = pl.ds(pl.multiple_of(at_ref[0] + i * chunk, 16), chunk)
            copies.append(
                [
                    pltpu.make_async_copy(t_ref.at[rows, :], t_buf.at[i], sems.at[i, 0]),
                    pltpu.make_async_copy(w_ref.at[rows, :], w_buf.at[i], sems.at[i, 1]),
                ]
            )
        for copy in copies[0] + copies[1]:
            copy.start()
        for i in range(parts):
            rows = slice(i * chunk, (i + 1) * chunk)
            for copy in copies[i]:
                copy.wait()
            if i + 2 < parts:
                for copy in copies[i + 2]:
                    copy.start()
            value = dot(t_buf[i, :, :total], xs_ref[...]) + dot(w_buf[i], mix_ref[...])
            last = dot(t_buf[i, :, total:], cs_ref[...])
            major[rows, : 2 * k] = value[:, : 2 * k].astype(bf16)
            major[rows, 2 * k :] = (value[:, 2 * k : 3 * k] + last[:, :k]).astype(bf16)
            minor[rows, :] = (value[:, 3 * k :] + last[:, k:]).astype(bf16)

    local_ref = pl.BlockSpec(memory_space=pltpu.VMEM)
    far_ref = pl.BlockSpec(memory_space=pl.ANY)
    return pl.pallas_call(
        kernel,
        in_specs=[pl.BlockSpec(memory_space=pltpu.SMEM)] + [far_ref] * 2 + [local_ref] * 3,
        out_specs=[local_ref] * 2,
        out_shape=[
            jax.ShapeDtypeStruct((size, 3 * k), bf16),
            jax.ShapeDtypeStruct((size, k), bf16),
        ],
        scratch_shapes=[
            pltpu.VMEM((parts, chunk, both), bf16),
            pltpu.VMEM((parts, chunk, 6 * k), bf16),
            pltpu.SemaphoreType.DMA((parts, 2)),
        ],
        compiler_params=pltpu.CompilerParams(vmem_limit_bytes=16 << 20),
        name="piece",
    )(at[None], *in_hbm(turned, weights), xs, cs, mix)


def squares(block):
    rows, width = block.shape

    def kernel(ref, out):
        v = ref[...].astype(f32)
        out[...] = jnp.sum((v * v).reshape(4, rows // 32, 8, width), axis=1)

    return pl.pallas_call(
        kernel,
        out_shape=jax.ShapeDtypeStruct((4, 8, width), f32),
        compiler_params=pltpu.CompilerParams(vmem_limit_bytes=8 << 20),
        name="squares",
    )(block)


def finish(starts, major, minor, features, k):
    quarter = features // 4
    part = quarter // 4
    late = 2
    early = [i for i in range(4) if i != late]
    blocks = [*major, *minor]
    known = [squares(major[i]) for i in early] + [squares(minor[i]) for i in early]

    def kernel(at, *refs):
        ins, known, (down, up) = refs[:8], refs[8:14], refs[14:]
        group = pl.program_id(0)

        def run(which, out):
            sums = [None] * 4
            for i in range(4):
                if i == late:
                    v = ins[which * 4 + i][...].astype(f32)
                    v = jnp.sum((v * v).reshape(4, part // 8, 8, k), axis=1)
                else:
                    v = known[which * 3 + early.index(i)][...]
                sums[i] = ring_sum(v[0], v[2], v[1], v[3])
            total = ring_sum(sums[0], sums[2], sums[1], sums[3])
            mean = jnp.sum(total) * (1.0 / (features * k))
            scale = lax.rsqrt(jnp.full((1, k), mean, f32) + step_eps)
            for i in range(4):
                for j in range(4):
                    row = pl.multiple_of(at[which, i, j], 16)
                    v = ins[which * 4 + i][j * part : (j + 1) * part, :].astype(f32)
                    out[0, pl.ds(row, part), :] = (v * scale).astype(bf16)

        @pl.when(group < 2)
        def _():
            run(0, down)

        @pl.when(group == 2)
        def _():
            run(0, up)

        @pl.when(group == 3)
        def _():
            run(1, up)

    def specs(shape, columns):
        zeros = (0,) * (len(shape) - 1)
        return pl.BlockSpec(shape, lambda g, at: (*zeros, columns(g)))

    def clipped(g):
        return jnp.minimum(g, 2)

    def fixed(g):
        return 0

    return pl.pallas_call(
        kernel,
        grid_spec=pltpu.PrefetchScalarGridSpec(
            num_scalar_prefetch=1,
            grid=(4,),
            in_specs=[specs((quarter, k), clipped)] * 4
            + [specs((quarter, k), fixed)] * 4
            + [specs((4, 8, k), clipped)] * 3
            + [specs((4, 8, k), fixed)] * 3,
            out_specs=[
                pl.BlockSpec((1, features, k), lambda g, at: (jnp.minimum(g, 1), 0, 0)),
                pl.BlockSpec((1, features, k), lambda g, at: (jnp.maximum(g - 2, 0), 0, 0)),
            ],
        ),
        out_shape=[jax.ShapeDtypeStruct((2, features, k), bf16)] * 2,
        compiler_params=pltpu.CompilerParams(vmem_limit_bytes=16 << 20),
        name="finish",
    )(starts, *blocks, *known)


def coords(peer):
    return peer // 16, (peer // 4) % 4, peer % 4


MAJOR = ((0, 1, 2), (1, 2, 0))
MINOR = ((2, 1, 0), (2, 0, 1))


def hop(values, order, stage, by):
    pairs = []
    for s in range(2):
        axis = order[s][stage]
        for p in range(64):
            c = list(coords(p))
            c[axis] = (c[axis] + by) % 4
            pairs.append((s * 64 + p, s * 64 + c[0] * 16 + c[1] * 4 + c[2]))
    return lax.ppermute(values, ("section", "peer"), pairs)


def ring_sum(own, two, one, three):
    return (own + two) + (one + three)


def summed(parts, order, at, gains=None):
    step = parts[0].shape[0] // 4

    def cut(by):
        start = ((at[1] + by) % 4) * step
        return sum(lax.dynamic_slice_in_dim(p, start, step, axis=0).astype(f32) for p in parts)

    arrived = [hop(cut(by).astype(bf16), order, 1, by) for by in (2, 1, 3)]
    own = cut(0) + sum(part.astype(f32) for part in arrived)
    own = lax.optimization_barrier(own.astype(bf16))
    two, one, three = [hop(own, order, 2, by).astype(f32) for by in (2, 1, 3)]
    total = ring_sum(own.astype(f32), two, one, three)
    return (total if gains is None else total * gains).astype(bf16)


def gathered(block, order):
    wide = jnp.concatenate([block] + [hop(block, order, 1, by) for by in (1, 2, 3)], axis=0)
    return [wide] + [hop(wide, order, 0, by) for by in (1, 2, 3)]


def local(inputs, cotangent, down_proj, up_proj, norm_gain, wiring, live_mask):
    section = lax.axis_index("section")
    peer = lax.axis_index("peer")
    _, lanes, rows, features = inputs.shape
    k = down_proj.shape[3]
    x, c = inputs[0], cotangent[0]
    gain, up = norm_gain[0], up_proj[0]
    is_first = section == 0
    swap = [(0, 1), (1, 0)]
    down = down_proj[0]
    down_other = lax.ppermute(down, "section", swap)
    up_other = lax.ppermute(up, "section", swap)
    gain_other = lax.ppermute(gain, "section", swap)
    sent = front(x, c, down, up, gain)
    received = lax.all_to_all(
        sent.reshape(rows, 8, 3 * k), ("section", "peer"), 0, 0, tiled=True
    ).reshape(2, -1, 3 * k)
    weights, gram_low, gram_high = prepare(
        section, down, up, gain, down_other, up_other, gain_other
    )
    holders = peer_table(wiring, live_mask)
    total = holders.shape[1]
    lane_of = jnp.arange(total, dtype=jnp.int32) // (total // lanes)
    base = holders * 8 + 2 * lane_of
    out, mix_own, mix_leaving = meet(
        section, received, base[0], base[1], gram_low, gram_high, lanes, features
    )
    mix_other = lax.ppermute(mix_leaving, "section", swap)
    returned = lax.all_to_all(
        out.reshape(rows, 8, 3 * k), ("section", "peer"), 0, 0, tiled=True
    ).reshape(8 * rows, 3 * k)
    turned = turn(*lax.optimization_barrier((x, c, mix_own))[:2])
    xs, cs, mix = unpack(returned, mix_own, mix_other, lanes)

    where = jnp.stack(coords(peer))
    at_major, at_minor = (
        [jnp.where(is_first, where[order[0][i]], where[order[1][i]]) for i in range(3)]
        for order in (MAJOR, MINOR)
    )
    quarter = features // 4
    major, minor = [], []
    for by in (2, 1, 3, 0):
        index = ((at_major[0] + by) % 4) * quarter
        part, rest = piece(index.astype(jnp.int32), quarter, turned, weights, xs, cs, mix)
        major.append(hop(part, MAJOR, 0, by) if by else part)
        minor.append(rest)

    def pick_minor(by):
        ahead = (at_minor[0] + by - at_major[0]) % 4
        return lax.select_n(
            jnp.broadcast_to(ahead, minor[0].shape), minor[3], minor[1], minor[0], minor[2]
        )

    step = features // 16
    row = at_major[0] * quarter + at_major[1] * step
    gains = lax.dynamic_slice_in_dim(gain, row, step, axis=1).T
    gains = joined([jnp.broadcast_to(gains[:, l : l + 1], (step, k)) for l in range(2)])
    gains = joined([gains, jnp.ones((step, k), f32)])
    minor = [hop(pick_minor(by), MINOR, 0, by) for by in (2, 1, 3)] + [pick_minor(0)]
    minor = gathered(summed(minor, MINOR, at_minor), MINOR)
    major = gathered(summed(major, MAJOR, at_major, gains), MAJOR)

    back = jnp.arange(4, dtype=jnp.int32)
    starts = jnp.stack(
        [
            ((at[0] - back) % 4)[:, None] * quarter + ((at[1] - back) % 4)[None, :] * step
            for at in (at_major, at_minor)
        ]
    ).astype(jnp.int32)
    down_step, up_step = finish(starts, major, minor, features, k)
    return down_step[None], up_step[None]


def solution(mesh):
    placed = (
        P("peer", None, None, None),
        P("peer", None, None, None),
        P("section", None, None, None),
        P("section", None, None, None),
        P("section", None, None),
        P(),
        P(),
    )
    return jax.shard_map(
        local,
        mesh=mesh,
        in_specs=placed,
        out_specs=(P("section", None, None, None), P("section", None, None, None)),
        check_vma=False,
    )
```

```python
import jax
import jax.numpy as jnp
from jax import lax
from jax.experimental import pallas as pl
from jax.experimental.pallas import tpu as pltpu
from jax.sharding import PartitionSpec as P

norm_eps = 1e-05
step_eps = 1e-06
bf16 = jnp.bfloat16
f32 = jnp.float32


def dot(a, b):
    return jnp.dot(a.astype(bf16), b.astype(bf16), preferred_element_type=f32)


def dot_nt(a, b):
    return lax.dot_general(
        a.astype(bf16), b.astype(bf16), (((1,), (1,)), ((), ())), preferred_element_type=f32
    )


def dot_tn(a, b):
    return lax.dot_general(
        a.astype(bf16), b.astype(bf16), (((0,), (0,)), ((), ())), preferred_element_type=f32
    )


def peer_table(wiring, live_mask):
    live_rank = jnp.cumsum(live_mask, axis=1) - 1
    matches = (live_mask[:, None, :] == 1) & (live_rank[:, None, :] == wiring[:, :, None])
    peer_ids = jnp.arange(live_mask.shape[1], dtype=jnp.int32)
    return jnp.sum(jnp.where(matches, peer_ids, 0), axis=2)


def row_sum(values):
    return jnp.sum(values, axis=1, keepdims=True)


def row_stage(proj, cot, square_sum, grams, feature_count):
    k = cot[0].shape[1]

    def activated(pre):
        r = lax.rsqrt(square_sum * (1.0 / feature_count) + norm_eps)
        h = r * pre
        return r, h, (h * jax.nn.sigmoid(h)).astype(bf16)

    first_layer = activated(proj[0][0])
    gram_low, gram_high = grams()

    def cut(g, i, j):
        return g[i * k : (i + 1) * k, j * k : (j + 1) * k].astype(bf16)

    ugd = {(0, 1): cut(gram_low, 0, 0), (2, 3): cut(gram_high, 0, 0)}
    uu = {
        (0, 0): cut(gram_low, 0, 1),
        (0, 1): cut(gram_low, 0, 2),
        (1, 1): cut(gram_low, 1, 2),
        (2, 2): cut(gram_high, 0, 1),
    }
    for i in (0, 1):
        ugd[(i, 2)] = cut(gram_low, i, 3)
        ugd[(i, 3)] = cut(gram_low, i, 4)
        uu[(i, 2)] = cut(gram_low, i, 5)

    hidden, active, inverse, full = [], [], [], []
    for l in range(4):
        pre = proj[l][0]
        for i in range(l):
            pre = pre + dot(active[i], ugd[(i, l)])
        r, h, a = activated(pre) if l else first_layer
        hidden.append(h)
        active.append(a)
        inverse.append(r)
        if l < 3:
            along = proj[l][1]
            for i in range(l):
                along = along + dot(active[i], uu[(i, l)])
            own = dot(a, uu[(l, l)])
            square_sum = square_sum + row_sum((2.0 * along + own) * a.astype(f32))
            full.append(along + own)

    back = [None] * 4
    weight = [None] * 4
    weight[3] = jnp.zeros_like(square_sum)
    for l in (3, 2, 1, 0):
        grad = cot[l]
        for j in range(l + 1, 4):
            grad = grad + dot_nt(back[j], ugd[(l, j)])
        if l < 3:
            grad = grad - weight[l] * full[l]
        for i in range(l + 1, 3):
            grad = grad - weight[i] * dot_nt(active[i], uu[(l, i)])
        sig = jax.nn.sigmoid(hidden[l])
        hid_grad = (grad * sig * (1.0 + hidden[l] * (1.0 - sig))).astype(bf16).astype(f32)
        back[l] = (inverse[l] * hid_grad).astype(bf16)
        if l > 0:
            centred = row_sum(hidden[l] * hid_grad) * (1.0 / feature_count)
            weight[l - 1] = weight[l] + inverse[l] * inverse[l] * centred
    less = [(-weight[l] * active[l].astype(f32)).astype(bf16) for l in range(4)]

    def scaled(w, l):
        return (-w * active[l].astype(f32)).astype(bf16)

    def against(left, parts):
        turned = left.astype(f32).T.astype(bf16)
        product = dot(turned, jnp.concatenate(parts, axis=1))
        return [product[:, i * k : (i + 1) * k] for i in range(len(parts))]

    a, b, w = active, back, weight
    a0 = against(a[0], [b[1], less[0], less[1], b[2], b[3], less[2]])
    a1 = against(a[1], [scaled(w[1], 0), less[1], b[2], b[3], less[2]])
    a2 = against(a[2], [scaled(w[2], 0), scaled(w[2], 1), b[3], less[2]])
    b1 = against(b[1], [a[0]])
    b2 = against(b[2], [a[0], a[1]])
    b3 = against(b[3], [a[0], a[1], a[2]])
    none = jnp.zeros((k, k), f32)
    mix_first = [
        [none, none, b1[0], none],
        [none, a0[0], a0[1], a0[2]],
        [none, none, a1[0], a1[1]],
        [none, none, b2[0], b2[1]],
        [none, none, b3[0], b3[1]],
        [none, none, a2[0], a2[1]],
    ]
    mix_second = [
        [none, none, none, none],
        [a0[3], a0[4], a0[5], none],
        [a1[2], a1[3], a1[4], none],
        [none, none, none, none],
        [none, none, b3[2], none],
        [none, a2[2], a2[3], none],
    ]
    return active, back, less, mix_first, mix_second


def in_hbm(*arrays):
    return [pltpu.with_memory_space_constraint(array, pltpu.HBM) for array in arrays]


def joined(parts):
    return jnp.concatenate(list(parts), axis=1)


def front(x, c, down, up, gain):
    lanes, rows, features = x.shape
    k = down.shape[2]
    block = 1024
    steps = features // block
    total = lanes * rows

    def kernel(x_ref, c_ref, d_ref, u_ref, g_ref, sent_ref, acc, squares, packed):
        step = pl.program_id(0)
        columns = jnp.concatenate([g_ref[...]] * 4, axis=0).T
        gained = [
            (d_ref[l].astype(f32) * columns[:, l : l + 1]).astype(bf16) for l in range(2)
        ]
        ups = [u_ref[0], u_ref[1]]
        flat = x_ref[...].reshape(total, block)
        of_x = dot(flat, joined(gained + ups))
        of_c = dot(c_ref[...].reshape(total, block), joined(ups))
        part = jnp.zeros((total, k), f32)
        for j in range(block // k):
            wide = flat[:, j * k : (j + 1) * k].astype(f32)
            part = part + wide * wide

        @pl.when(step == 0)
        def _():
            acc[:, : 4 * k] = of_x
            acc[:, 4 * k :] = of_c
            squares[...] = part

        @pl.when(step > 0)
        def _():
            acc[:, : 4 * k] += of_x
            acc[:, 4 * k :] += of_c
            squares[...] += part

        @pl.when(step == steps - 1)
        def _():
            for j in range(lanes):
                at = slice(j * rows, (j + 1) * rows)
                for half in range(2):
                    for t in range(3):
                        packed[t, pl.ds(2 * j + half, rows, stride=8), :] = acc[
                            at, (half * 3 + t) * k : (half * 3 + t + 1) * k
                        ]
                square = jnp.broadcast_to(row_sum(squares[at, :]), (rows, k))
                coarse = square.astype(bf16).astype(f32)
                packed[j, pl.ds(6, rows, stride=8), :] = coarse
                packed[j, pl.ds(7, rows, stride=8), :] = square - coarse
            for t in range(3):
                sent_ref[:, t * k : (t + 1) * k] = packed[t].astype(bf16)

    return pl.pallas_call(
        kernel,
        grid=(steps,),
        in_specs=[
            pl.BlockSpec((lanes, rows, block), lambda i: (0, 0, i)),
            pl.BlockSpec((lanes, rows, block), lambda i: (0, 0, i)),
            pl.BlockSpec((2, block, k), lambda i: (0, i, 0)),
            pl.BlockSpec((2, block, k), lambda i: (0, i, 0)),
            pl.BlockSpec((2, block), lambda i: (0, i)),
        ],
        out_specs=pl.BlockSpec((8 * rows, 3 * k), lambda i: (0, 0)),
        out_shape=jax.ShapeDtypeStruct((8 * rows, 3 * k), bf16),
        scratch_shapes=[
            pltpu.VMEM((total, 6 * k), f32),
            pltpu.VMEM((total, k), f32),
            pltpu.VMEM((3, 8 * rows, k), f32),
        ],
        compiler_params=pltpu.CompilerParams(vmem_limit_bytes=20 << 20),
        name="front",
    )(*in_hbm(x, c, down, up, gain))


def prepare(section, down, up, gain, down_other, up_other, gain_other):
    _, features, k = down.shape
    block = 1024
    steps = features // block

    def kernel(s_ref, d, u, g, d2, u2, g2, w_ref, low_out, high_out, low_ref, high_ref):
        step = pl.program_id(0)
        gains = jnp.concatenate([g[...], g2[...]] * 2, axis=0).T
        first = s_ref[0] == 0

        def choose(one, two):
            return jnp.where(first, one.astype(f32), two.astype(f32))

        gain_one = choose(gains[:, :2], gains[:, 2:4])
        gain_two = choose(gains[:, 2:4], gains[:, :2])
        parts = [
            choose(d[1], d2[1]) * gain_one[:, 1:2],
            choose(u[0], u2[0]),
            choose(u[1], u2[1]),
            choose(d2[0], d[0]) * gain_two[:, :1],
            choose(d2[1], d[1]) * gain_two[:, 1:2],
            choose(u2[0], u[0]),
        ]
        parts = [part.astype(bf16) for part in parts]
        weights = joined(parts)
        w_ref[...] = weights
        low = dot_tn(joined(parts[1:3]), weights)
        high = dot_tn(parts[5], joined(parts[4:]))

        @pl.when(step == 0)
        def _():
            low_ref[...] = low
            high_ref[...] = high

        @pl.when(step > 0)
        def _():
            low_ref[...] += low
            high_ref[...] += high

        @pl.when(step == steps - 1)
        def _():
            low_out[...] = low_ref[...].astype(bf16)
            high_out[...] = high_ref[...].astype(bf16)

    two = pl.BlockSpec((2, block, k), lambda i, s: (0, i, 0))
    row = pl.BlockSpec((2, block), lambda i, s: (0, i))
    return pl.pallas_call(
        kernel,
        grid_spec=pltpu.PrefetchScalarGridSpec(
            num_scalar_prefetch=1,
            grid=(steps,),
            in_specs=[two, two, row, two, two, row],
            out_specs=[
                pl.BlockSpec((block, 6 * k), lambda i, s: (i, 0)),
                pl.BlockSpec((2 * k, 6 * k), lambda i, s: (0, 0)),
                pl.BlockSpec((k, 2 * k), lambda i, s: (0, 0)),
            ],
            scratch_shapes=[pltpu.VMEM((2 * k, 6 * k), f32), pltpu.VMEM((k, 2 * k), f32)],
        ),
        out_shape=[
            pltpu.HBM((features, 6 * k), bf16),
            pltpu.HBM((2 * k, 6 * k), bf16),
            pltpu.HBM((k, 2 * k), bf16),
        ],
        compiler_params=pltpu.CompilerParams(vmem_limit_bytes=24 << 20),
        name="prepare",
    )(section[None], *in_hbm(down, up, gain), down_other, up_other, gain_other)


def turn(x, c):
    lanes, rows, features = x.shape
    block = 1024

    def kernel(x_ref, c_ref, out):
        for j in range(lanes):
            out[:, j * rows : (j + 1) * rows] = x_ref[j].T
            out[:, (lanes + j) * rows : (lanes + j + 1) * rows] = c_ref[j].T

    spec = pl.BlockSpec((lanes, rows, block), lambda i: (0, 0, i))
    return pl.pallas_call(
        kernel,
        grid=(features // block,),
        in_specs=[spec, spec],
        out_specs=pl.BlockSpec((block, 2 * lanes * rows), lambda i: (i, 0)),
        out_shape=pltpu.HBM((features, 2 * lanes * rows), bf16),
        compiler_params=pltpu.CompilerParams(vmem_limit_bytes=12 << 20),
        name="turn",
    )(*in_hbm(x, c))


def meet(section, received, first, second, gram_low, gram_high, lanes, features):
    total = first.shape[0]
    group = total // lanes
    slots = received.shape[1]
    k = received.shape[2] // 3

    def kernel(mine, rec, columns, rows, far_low, far_high, out, own, oth, low, high, sems):
        copies = [
            pltpu.make_async_copy(far_low, low, sems.at[0]),
            pltpu.make_async_copy(far_high, high, sems.at[1]),
        ]
        for copy in copies:
            copy.start()
        i0, i1 = columns[:, :1], columns[:, 1:]
        t0, t1 = rows[:1, :], rows[1:, :]
        grid = lax.broadcasted_iota(jnp.int32, (total, slots), 1)
        turned = lax.broadcasted_iota(jnp.int32, (slots, total), 0)

        def pick(base):
            return (grid == base).astype(f32).astype(bf16)

        def place(base):
            return (turned == base).astype(f32).astype(bf16)

        at_start = pick(i0)
        at_start_next = pick(i0 + 1)
        at_end = pick(i1 + 1)
        lane = lax.broadcasted_iota(jnp.int32, (total, 1), 0) // group
        norm_row = i0 - 2 * lane + 6
        sums = dot(pick(norm_row), rec[0]) + dot(pick(norm_row + 1), rec[0])
        square_sum = jnp.concatenate(
            [sums[j * group : (j + 1) * group, j * k : (j + 1) * k] for j in range(lanes)], axis=0
        )[:, :1]
        proj, cot = [], []
        for s in range(2):
            near = dot(at_start, rec[s])
            next_up = dot(at_start_next, rec[s, :, :k])
            tail = dot(at_end, rec[s, :, k:])
            proj += [(near[:, :k], near[:, 2 * k :]), (near[:, k : 2 * k], next_up)]
            cot += [tail[:, :k], tail[:, k:]]
        to_start = place(t0)
        to_start_next = place(t0 + 1)
        to_end = place(t1 + 1)

        def grams():
            for copy in copies:
                copy.wait()
            return low[...], high[...]

        active, back, less, mix_first, mix_second = row_stage(
            proj, cot, square_sum, grams, features
        )
        for s in range(2):
            l0, l1 = 2 * s, 2 * s + 1
            out[s] = dot(to_start, joined([back[l0], back[l1], less[l0]])).astype(bf16)
            weighted = dot(to_start_next, less[l1])
            tail = dot(to_end, joined([active[l0], active[l1]]))
            out[s] += joined([weighted, tail]).astype(bf16)
        first_section = mine[0] == 0
        for i, (one, two) in enumerate(zip(mix_first, mix_second)):
            at = slice(i * k, (i + 1) * k)
            one, two = joined(one), joined(two)
            own[at, :] = jnp.where(first_section, one, two).astype(bf16)
            oth[at, :] = jnp.where(first_section, two, one).astype(bf16)

    columns = jnp.stack([first, second], axis=1)
    rows = jnp.stack([first, second])
    local_ref = pl.BlockSpec(memory_space=pltpu.VMEM)
    far_ref = pl.BlockSpec(memory_space=pl.ANY)
    mix = jax.ShapeDtypeStruct((6 * k, 4 * k), bf16)
    return pl.pallas_call(
        kernel,
        in_specs=[pl.BlockSpec(memory_space=pltpu.SMEM)] + [local_ref] * 3 + [far_ref] * 2,
        out_shape=[jax.ShapeDtypeStruct(received.shape, bf16), mix, mix],
        scratch_shapes=[
            pltpu.VMEM(gram_low.shape, bf16),
            pltpu.VMEM(gram_high.shape, bf16),
            pltpu.SemaphoreType.DMA((2,)),
        ],
        compiler_params=pltpu.CompilerParams(vmem_limit_bytes=16 << 20),
        name="meet",
    )(section[None], received, columns, rows, *in_hbm(gram_low, gram_high))


def unpack(returned, mix_own, mix_other, lanes):
    rows, k = returned.shape[0] // 8, returned.shape[1] // 3

    def kernel(ret, own, far, xs, cs, mix, wide, oth, sem):
        copy = pltpu.make_async_copy(far, oth, sem)
        copy.start()
        for t in range(3):
            wide[t] = ret[:, t * k : (t + 1) * k].astype(f32)
        for j in range(lanes):
            at = slice(j * rows, (j + 1) * rows)
            low = [wide[t, pl.ds(2 * j, rows, stride=8), :].astype(bf16) for t in range(3)]
            high = [wide[t, pl.ds(2 * j + 1, rows, stride=8), :].astype(bf16) for t in range(3)]
            xs[at, :] = joined(low + high[:1])
            cs[at, :] = joined(high[1:])
        copy.wait()
        mix[...] = (own[...].astype(f32) + oth[...].astype(f32)).astype(bf16)

    local_ref = pl.BlockSpec(memory_space=pltpu.VMEM)
    shapes = [(lanes * rows, 4 * k), (lanes * rows, 2 * k), mix_own.shape]
    return pl.pallas_call(
        kernel,
        in_specs=[local_ref, local_ref, pl.BlockSpec(memory_space=pl.ANY)],
        out_shape=[jax.ShapeDtypeStruct(shape, bf16) for shape in shapes],
        scratch_shapes=[
            pltpu.VMEM((3, 8 * rows, k), f32),
            pltpu.VMEM(mix_own.shape, bf16),
            pltpu.SemaphoreType.DMA,
        ],
        compiler_params=pltpu.CompilerParams(vmem_limit_bytes=8 << 20),
        name="unpack",
    )(returned, mix_own, *in_hbm(mix_other))


def piece(at, size, turned, weights, xs, cs, mix):
    both = turned.shape[1]
    k = cs.shape[1] // 2
    total = both // 2
    parts = 2
    chunk = size // parts

    def kernel(at_ref, t_ref, w_ref, xs_ref, cs_ref, mix_ref, major, minor, t_buf, w_buf, sems):
        copies = []
        for i in range(parts):
            rows = pl.ds(pl.multiple_of(at_ref[0] + i * chunk, 16), chunk)
            copies.append(
                [
                    pltpu.make_async_copy(t_ref.at[rows, :], t_buf.at[i], sems.at[i, 0]),
                    pltpu.make_async_copy(w_ref.at[rows, :], w_buf.at[i], sems.at[i, 1]),
                ]
            )
        for copy in copies[0] + copies[1]:
            copy.start()
        for i in range(parts):
            rows = slice(i * chunk, (i + 1) * chunk)
            for copy in copies[i]:
                copy.wait()
            if i + 2 < parts:
                for copy in copies[i + 2]:
                    copy.start()
            value = dot(t_buf[i, :, :total], xs_ref[...]) + dot(w_buf[i], mix_ref[...])
            last = dot(t_buf[i, :, total:], cs_ref[...])
            major[rows, : 2 * k] = value[:, : 2 * k].astype(bf16)
            major[rows, 2 * k :] = (value[:, 2 * k : 3 * k] + last[:, :k]).astype(bf16)
            minor[rows, :] = (value[:, 3 * k :] + last[:, k:]).astype(bf16)

    local_ref = pl.BlockSpec(memory_space=pltpu.VMEM)
    far_ref = pl.BlockSpec(memory_space=pl.ANY)
    return pl.pallas_call(
        kernel,
        in_specs=[pl.BlockSpec(memory_space=pltpu.SMEM)] + [far_ref] * 2 + [local_ref] * 3,
        out_specs=[local_ref] * 2,
        out_shape=[
            jax.ShapeDtypeStruct((size, 3 * k), bf16),
            jax.ShapeDtypeStruct((size, k), bf16),
        ],
        scratch_shapes=[
            pltpu.VMEM((parts, chunk, both), bf16),
            pltpu.VMEM((parts, chunk, 6 * k), bf16),
            pltpu.SemaphoreType.DMA((parts, 2)),
        ],
        compiler_params=pltpu.CompilerParams(vmem_limit_bytes=16 << 20),
        name="piece",
    )(at[None], *in_hbm(turned, weights), xs, cs, mix)


def squares(block):
    rows, width = block.shape

    def kernel(ref, out):
        v = ref[...].astype(f32)
        out[...] = jnp.sum((v * v).reshape(4, rows // 32, 8, width), axis=1)

    return pl.pallas_call(
        kernel,
        out_shape=jax.ShapeDtypeStruct((4, 8, width), f32),
        compiler_params=pltpu.CompilerParams(vmem_limit_bytes=8 << 20),
        name="squares",
    )(block)


def finish(starts, major, minor, features, k):
    quarter = features // 4
    part = quarter // 4
    late = 2
    early = [i for i in range(4) if i != late]
    blocks = [*major, *minor]
    known = [squares(major[i]) for i in early] + [squares(minor[i]) for i in early]

    def kernel(at, *refs):
        ins, known, (down, up, out, sems) = refs[:8], refs[8:14], refs[14:]

        def run(which, group, columns):
            sums = [None] * 4
            for i in range(4):
                if i == late:
                    v = ins[which * 4 + i][:, columns].astype(f32)
                    v = jnp.sum((v * v).reshape(4, part // 8, 8, k), axis=1)
                else:
                    v = known[which * 3 + early.index(i)][:, :, columns]
                sums[i] = ring_sum(v[0], v[2], v[1], v[3])
            total = ring_sum(sums[0], sums[2], sums[1], sums[3])
            mean = jnp.sum(total) * (1.0 / (features * k))
            scale = lax.rsqrt(jnp.full((1, k), mean, f32) + step_eps)
            for i in range(4):
                for j in range(4):
                    row = pl.multiple_of(at[which, i, j], 16)
                    v = ins[which * 4 + i][j * part : (j + 1) * part, columns].astype(f32)
                    out[group, pl.ds(row, part), :] = (v * scale).astype(bf16)

        copies = []
        for group in range(4):
            which = group // 3
            run(which, group, slice(0, k) if which else slice(group * k, (group + 1) * k))
            target = (down, up)[group // 2].at[group % 2]
            copies.append(pltpu.make_async_copy(out.at[group], target, sems.at[group]))
            copies[-1].start()
        for copy in copies:
            copy.wait()

    local_ref = pl.BlockSpec(memory_space=pltpu.VMEM)
    far_ref = pl.BlockSpec(memory_space=pl.ANY)
    return pl.pallas_call(
        kernel,
        in_specs=[pl.BlockSpec(memory_space=pltpu.SMEM)] + [local_ref] * 14,
        out_specs=[far_ref] * 2,
        out_shape=[jax.ShapeDtypeStruct((2, features, k), bf16)] * 2,
        scratch_shapes=[
            pltpu.VMEM((4, features, k), bf16),
            pltpu.SemaphoreType.DMA((4,)),
        ],
        compiler_params=pltpu.CompilerParams(vmem_limit_bytes=16 << 20),
        name="finish",
    )(starts, *blocks, *known)


def coords(peer):
    return peer // 16, (peer // 4) % 4, peer % 4


MAJOR = ((0, 1, 2), (1, 2, 0))
MINOR = ((2, 1, 0), (2, 0, 1))


def hop(values, order, stage, by):
    pairs = []
    for s in range(2):
        axis = order[s][stage]
        for p in range(64):
            c = list(coords(p))
            c[axis] = (c[axis] + by) % 4
            pairs.append((s * 64 + p, s * 64 + c[0] * 16 + c[1] * 4 + c[2]))
    return lax.ppermute(values, ("section", "peer"), pairs)


def ring_sum(own, two, one, three):
    return (own + two) + (one + three)


def summed(parts, order, at, gains=None):
    step = parts[0].shape[0] // 4

    def cut(by):
        start = ((at[1] + by) % 4) * step
        return sum(lax.dynamic_slice_in_dim(p, start, step, axis=0).astype(f32) for p in parts)

    arrived = [hop(cut(by).astype(bf16), order, 1, by) for by in (2, 1, 3)]
    own = cut(0) + sum(part.astype(f32) for part in arrived)
    own = lax.optimization_barrier(own.astype(bf16))
    two, one, three = [hop(own, order, 2, by).astype(f32) for by in (2, 1, 3)]
    total = ring_sum(own.astype(f32), two, one, three)
    return (total if gains is None else total * gains).astype(bf16)


def gathered(block, order):
    wide = jnp.concatenate([block] + [hop(block, order, 1, by) for by in (1, 2, 3)], axis=0)
    return [wide] + [hop(wide, order, 0, by) for by in (1, 2, 3)]


def local(inputs, cotangent, down_proj, up_proj, norm_gain, wiring, live_mask):
    section = lax.axis_index("section")
    peer = lax.axis_index("peer")
    _, lanes, rows, features = inputs.shape
    k = down_proj.shape[3]
    x, c = inputs[0], cotangent[0]
    gain, up = norm_gain[0], up_proj[0]
    is_first = section == 0
    swap = [(0, 1), (1, 0)]
    down = down_proj[0]
    down_other = lax.ppermute(down, "section", swap)
    up_other = lax.ppermute(up, "section", swap)
    gain_other = lax.ppermute(gain, "section", swap)
    sent = front(x, c, down, up, gain)
    received = lax.all_to_all(
        sent.reshape(rows, 8, 3 * k), ("section", "peer"), 0, 0, tiled=True
    ).reshape(2, -1, 3 * k)
    weights, gram_low, gram_high = prepare(
        section, down, up, gain, down_other, up_other, gain_other
    )
    holders = peer_table(wiring, live_mask)
    total = holders.shape[1]
    lane_of = jnp.arange(total, dtype=jnp.int32) // (total // lanes)
    base = holders * 8 + 2 * lane_of
    out, mix_own, mix_leaving = meet(
        section, received, base[0], base[1], gram_low, gram_high, lanes, features
    )
    mix_other = lax.ppermute(mix_leaving, "section", swap)
    returned = lax.all_to_all(
        out.reshape(rows, 8, 3 * k), ("section", "peer"), 0, 0, tiled=True
    ).reshape(8 * rows, 3 * k)
    turned = turn(*lax.optimization_barrier((x, c, mix_own))[:2])
    xs, cs, mix = unpack(returned, mix_own, mix_other, lanes)

    where = jnp.stack(coords(peer))
    at_major, at_minor = (
        [jnp.where(is_first, where[order[0][i]], where[order[1][i]]) for i in range(3)]
        for order in (MAJOR, MINOR)
    )
    quarter = features // 4
    major, minor = [], []
    for by in (2, 1, 3, 0):
        index = ((at_major[0] + by) % 4) * quarter
        part, rest = piece(index.astype(jnp.int32), quarter, turned, weights, xs, cs, mix)
        major.append(hop(part, MAJOR, 0, by) if by else part)
        minor.append(rest)

    def pick_minor(by):
        ahead = (at_minor[0] + by - at_major[0]) % 4
        return lax.select_n(
            jnp.broadcast_to(ahead, minor[0].shape), minor[3], minor[1], minor[0], minor[2]
        )

    step = features // 16
    row = at_major[0] * quarter + at_major[1] * step
    gains = lax.dynamic_slice_in_dim(gain, row, step, axis=1).T
    gains = joined([jnp.broadcast_to(gains[:, l : l + 1], (step, k)) for l in range(2)])
    gains = joined([gains, jnp.ones((step, k), f32)])
    minor = [hop(pick_minor(by), MINOR, 0, by) for by in (2, 1, 3)] + [pick_minor(0)]
    minor = gathered(summed(minor, MINOR, at_minor), MINOR)
    major = gathered(summed(major, MAJOR, at_major, gains), MAJOR)

    back = jnp.arange(4, dtype=jnp.int32)
    starts = jnp.stack(
        [
            ((at[0] - back) % 4)[:, None] * quarter + ((at[1] - back) % 4)[None, :] * step
            for at in (at_major, at_minor)
        ]
    ).astype(jnp.int32)
    down_step, up_step = finish(starts, major, minor, features, k)
    return down_step[None], up_step[None]


def solution(mesh):
    placed = (
        P("peer", None, None, None),
        P("peer", None, None, None),
        P("section", None, None, None),
        P("section", None, None, None),
        P("section", None, None),
        P(),
        P(),
    )
    return jax.shard_map(
        local,
        mesh=mesh,
        in_specs=placed,
        out_specs=(P("section", None, None, None), P("section", None, None, None)),
        check_vma=False,
    )
```

```python
import jax
import jax.numpy as jnp
from jax import lax
from jax.experimental import pallas as pl
from jax.experimental.pallas import tpu as pltpu
from jax.sharding import PartitionSpec as P

norm_eps = 1e-05
step_eps = 1e-06
bf16 = jnp.bfloat16
f32 = jnp.float32


def dot(a, b):
    return jnp.dot(a.astype(bf16), b.astype(bf16), preferred_element_type=f32)


def dot_nt(a, b):
    return lax.dot_general(
        a.astype(bf16), b.astype(bf16), (((1,), (1,)), ((), ())), preferred_element_type=f32
    )


def dot_tn(a, b):
    return lax.dot_general(
        a.astype(bf16), b.astype(bf16), (((0,), (0,)), ((), ())), preferred_element_type=f32
    )


def peer_table(wiring, live_mask):
    live_rank = jnp.cumsum(live_mask, axis=1) - 1
    matches = (live_mask[:, None, :] == 1) & (live_rank[:, None, :] == wiring[:, :, None])
    peer_ids = jnp.arange(live_mask.shape[1], dtype=jnp.int32)
    return jnp.sum(jnp.where(matches, peer_ids, 0), axis=2)


def row_sum(values):
    return jnp.sum(values, axis=1, keepdims=True)


def row_stage(proj, cot, square_sum, grams, feature_count):
    k = cot[0].shape[1]

    def activated(pre):
        r = lax.rsqrt(square_sum * (1.0 / feature_count) + norm_eps)
        h = r * pre
        return r, h, (h * jax.nn.sigmoid(h)).astype(bf16)

    first_layer = activated(proj[0][0])
    gram_low, gram_high = grams()

    def cut(g, i, j):
        return g[i * k : (i + 1) * k, j * k : (j + 1) * k].astype(bf16)

    ugd = {(0, 1): cut(gram_low, 0, 0), (2, 3): cut(gram_high, 0, 0)}
    uu = {
        (0, 0): cut(gram_low, 0, 1),
        (0, 1): cut(gram_low, 0, 2),
        (1, 1): cut(gram_low, 1, 2),
        (2, 2): cut(gram_high, 0, 1),
    }
    for i in (0, 1):
        ugd[(i, 2)] = cut(gram_low, i, 3)
        ugd[(i, 3)] = cut(gram_low, i, 4)
        uu[(i, 2)] = cut(gram_low, i, 5)

    hidden, active, inverse, full = [], [], [], []
    for l in range(4):
        pre = proj[l][0]
        for i in range(l):
            pre = pre + dot(active[i], ugd[(i, l)])
        r, h, a = activated(pre) if l else first_layer
        hidden.append(h)
        active.append(a)
        inverse.append(r)
        if l < 3:
            along = proj[l][1]
            for i in range(l):
                along = along + dot(active[i], uu[(i, l)])
            own = dot(a, uu[(l, l)])
            square_sum = square_sum + row_sum((2.0 * along + own) * a.astype(f32))
            full.append(along + own)

    back = [None] * 4
    weight = [None] * 4
    weight[3] = jnp.zeros_like(square_sum)
    for l in (3, 2, 1, 0):
        grad = cot[l]
        for j in range(l + 1, 4):
            grad = grad + dot_nt(back[j], ugd[(l, j)])
        if l < 3:
            grad = grad - weight[l] * full[l]
        for i in range(l + 1, 3):
            grad = grad - weight[i] * dot_nt(active[i], uu[(l, i)])
        sig = jax.nn.sigmoid(hidden[l])
        hid_grad = (grad * sig * (1.0 + hidden[l] * (1.0 - sig))).astype(bf16).astype(f32)
        back[l] = (inverse[l] * hid_grad).astype(bf16)
        if l > 0:
            centred = row_sum(hidden[l] * hid_grad) * (1.0 / feature_count)
            weight[l - 1] = weight[l] + inverse[l] * inverse[l] * centred
    less = [(-weight[l] * active[l].astype(f32)).astype(bf16) for l in range(4)]

    def scaled(w, l):
        return (-w * active[l].astype(f32)).astype(bf16)

    def against(left, parts):
        turned = left.astype(f32).T.astype(bf16)
        product = dot(turned, jnp.concatenate(parts, axis=1))
        return [product[:, i * k : (i + 1) * k] for i in range(len(parts))]

    a, b, w = active, back, weight
    a0 = against(a[0], [b[1], less[0], less[1], b[2], b[3], less[2]])
    a1 = against(a[1], [scaled(w[1], 0), less[1], b[2], b[3], less[2]])
    a2 = against(a[2], [scaled(w[2], 0), scaled(w[2], 1), b[3], less[2]])
    b1 = against(b[1], [a[0]])
    b2 = against(b[2], [a[0], a[1]])
    b3 = against(b[3], [a[0], a[1], a[2]])
    none = jnp.zeros((k, k), f32)
    mix_first = [
        [none, none, b1[0], none],
        [none, a0[0], a0[1], a0[2]],
        [none, none, a1[0], a1[1]],
        [none, none, b2[0], b2[1]],
        [none, none, b3[0], b3[1]],
        [none, none, a2[0], a2[1]],
    ]
    mix_second = [
        [none, none, none, none],
        [a0[3], a0[4], a0[5], none],
        [a1[2], a1[3], a1[4], none],
        [none, none, none, none],
        [none, none, b3[2], none],
        [none, a2[2], a2[3], none],
    ]
    return active, back, less, mix_first, mix_second


def in_hbm(*arrays):
    return [pltpu.with_memory_space_constraint(array, pltpu.HBM) for array in arrays]


def joined(parts):
    return jnp.concatenate(list(parts), axis=1)


def front(x, c, down, up, gain):
    lanes, rows, features = x.shape
    k = down.shape[2]
    block = 1280
    steps = features // block
    total = lanes * rows

    def kernel(x_ref, c_ref, d_ref, u_ref, g_ref, sent_ref, acc, squares, packed):
        step = pl.program_id(0)
        columns = jnp.concatenate([g_ref[...]] * 4, axis=0).T
        gained = [
            (d_ref[l].astype(f32) * columns[:, l : l + 1]).astype(bf16) for l in range(2)
        ]
        ups = [u_ref[0], u_ref[1]]
        flat = x_ref[...].reshape(total, block)
        of_x = dot(flat, joined(gained + ups))
        of_c = dot(c_ref[...].reshape(total, block), joined(ups))
        part = jnp.zeros((total, k), f32)
        for j in range(block // k):
            wide = flat[:, j * k : (j + 1) * k].astype(f32)
            part = part + wide * wide

        @pl.when(step == 0)
        def _():
            acc[:, : 4 * k] = of_x
            acc[:, 4 * k :] = of_c
            squares[...] = part

        @pl.when(step > 0)
        def _():
            acc[:, : 4 * k] += of_x
            acc[:, 4 * k :] += of_c
            squares[...] += part

        @pl.when(step == steps - 1)
        def _():
            for j in range(lanes):
                at = slice(j * rows, (j + 1) * rows)
                for half in range(2):
                    for t in range(3):
                        packed[t, pl.ds(2 * j + half, rows, stride=8), :] = acc[
                            at, (half * 3 + t) * k : (half * 3 + t + 1) * k
                        ]
                square = jnp.broadcast_to(row_sum(squares[at, :]), (rows, k))
                coarse = square.astype(bf16).astype(f32)
                packed[j, pl.ds(6, rows, stride=8), :] = coarse
                packed[j, pl.ds(7, rows, stride=8), :] = square - coarse
            for t in range(3):
                sent_ref[:, t * k : (t + 1) * k] = packed[t].astype(bf16)

    return pl.pallas_call(
        kernel,
        grid=(steps,),
        in_specs=[
            pl.BlockSpec((lanes, rows, block), lambda i: (0, 0, i)),
            pl.BlockSpec((lanes, rows, block), lambda i: (0, 0, i)),
            pl.BlockSpec((2, block, k), lambda i: (0, i, 0)),
            pl.BlockSpec((2, block, k), lambda i: (0, i, 0)),
            pl.BlockSpec((2, block), lambda i: (0, i)),
        ],
        out_specs=pl.BlockSpec((8 * rows, 3 * k), lambda i: (0, 0)),
        out_shape=jax.ShapeDtypeStruct((8 * rows, 3 * k), bf16),
        scratch_shapes=[
            pltpu.VMEM((total, 6 * k), f32),
            pltpu.VMEM((total, k), f32),
            pltpu.VMEM((3, 8 * rows, k), f32),
        ],
        compiler_params=pltpu.CompilerParams(vmem_limit_bytes=20 << 20),
        name="front",
    )(*in_hbm(x, c, down, up, gain))


def prepare(section, down, up, gain, down_other, up_other, gain_other):
    _, features, k = down.shape
    block = 1024
    steps = features // block

    def kernel(s_ref, d, u, g, d2, u2, g2, w_ref, low_out, high_out, low_ref, high_ref):
        step = pl.program_id(0)
        gains = jnp.concatenate([g[...], g2[...]] * 2, axis=0).T
        first = s_ref[0] == 0

        def choose(one, two):
            return jnp.where(first, one.astype(f32), two.astype(f32))

        gain_one = choose(gains[:, :2], gains[:, 2:4])
        gain_two = choose(gains[:, 2:4], gains[:, :2])
        parts = [
            choose(d[1], d2[1]) * gain_one[:, 1:2],
            choose(u[0], u2[0]),
            choose(u[1], u2[1]),
            choose(d2[0], d[0]) * gain_two[:, :1],
            choose(d2[1], d[1]) * gain_two[:, 1:2],
            choose(u2[0], u[0]),
        ]
        parts = [part.astype(bf16) for part in parts]
        weights = joined(parts)
        w_ref[...] = weights
        low = dot_tn(joined(parts[1:3]), weights)
        high = dot_tn(parts[5], joined(parts[4:]))

        @pl.when(step == 0)
        def _():
            low_ref[...] = low
            high_ref[...] = high

        @pl.when(step > 0)
        def _():
            low_ref[...] += low
            high_ref[...] += high

        @pl.when(step == steps - 1)
        def _():
            low_out[...] = low_ref[...].astype(bf16)
            high_out[...] = high_ref[...].astype(bf16)

    two = pl.BlockSpec((2, block, k), lambda i, s: (0, i, 0))
    row = pl.BlockSpec((2, block), lambda i, s: (0, i))
    return pl.pallas_call(
        kernel,
        grid_spec=pltpu.PrefetchScalarGridSpec(
            num_scalar_prefetch=1,
            grid=(steps,),
            in_specs=[two, two, row, two, two, row],
            out_specs=[
                pl.BlockSpec((block, 6 * k), lambda i, s: (i, 0)),
                pl.BlockSpec((2 * k, 6 * k), lambda i, s: (0, 0)),
                pl.BlockSpec((k, 2 * k), lambda i, s: (0, 0)),
            ],
            scratch_shapes=[pltpu.VMEM((2 * k, 6 * k), f32), pltpu.VMEM((k, 2 * k), f32)],
        ),
        out_shape=[
            pltpu.HBM((features, 6 * k), bf16),
            pltpu.HBM((2 * k, 6 * k), bf16),
            pltpu.HBM((k, 2 * k), bf16),
        ],
        compiler_params=pltpu.CompilerParams(vmem_limit_bytes=24 << 20),
        name="prepare",
    )(section[None], *in_hbm(down, up, gain), down_other, up_other, gain_other)


def turn(x, c):
    lanes, rows, features = x.shape
    block = 1024

    def kernel(x_ref, c_ref, out):
        for j in range(lanes):
            out[:, j * rows : (j + 1) * rows] = x_ref[j].T
            out[:, (lanes + j) * rows : (lanes + j + 1) * rows] = c_ref[j].T

    spec = pl.BlockSpec((lanes, rows, block), lambda i: (0, 0, i))
    return pl.pallas_call(
        kernel,
        grid=(features // block,),
        in_specs=[spec, spec],
        out_specs=pl.BlockSpec((block, 2 * lanes * rows), lambda i: (i, 0)),
        out_shape=pltpu.HBM((features, 2 * lanes * rows), bf16),
        compiler_params=pltpu.CompilerParams(vmem_limit_bytes=12 << 20),
        name="turn",
    )(*in_hbm(x, c))


def meet(section, received, first, second, gram_low, gram_high, lanes, features):
    total = first.shape[0]
    group = total // lanes
    slots = received.shape[1]
    k = received.shape[2] // 3

    def kernel(mine, rec, columns, rows, far_low, far_high, out, own, oth, low, high, sems):
        copies = [
            pltpu.make_async_copy(far_low, low, sems.at[0]),
            pltpu.make_async_copy(far_high, high, sems.at[1]),
        ]
        for copy in copies:
            copy.start()
        i0, i1 = columns[:, :1], columns[:, 1:]
        t0, t1 = rows[:1, :], rows[1:, :]
        grid = lax.broadcasted_iota(jnp.int32, (total, slots), 1)
        turned = lax.broadcasted_iota(jnp.int32, (slots, total), 0)

        def pick(base):
            return (grid == base).astype(f32).astype(bf16)

        def place(base):
            return (turned == base).astype(f32).astype(bf16)

        at_start = pick(i0)
        at_start_next = pick(i0 + 1)
        at_end = pick(i1 + 1)
        lane = lax.broadcasted_iota(jnp.int32, (total, 1), 0) // group
        norm_row = i0 - 2 * lane + 6
        sums = dot(pick(norm_row), rec[0]) + dot(pick(norm_row + 1), rec[0])
        square_sum = jnp.concatenate(
            [sums[j * group : (j + 1) * group, j * k : (j + 1) * k] for j in range(lanes)], axis=0
        )[:, :1]
        proj, cot = [], []
        for s in range(2):
            near = dot(at_start, rec[s])
            next_up = dot(at_start_next, rec[s, :, :k])
            tail = dot(at_end, rec[s, :, k:])
            proj += [(near[:, :k], near[:, 2 * k :]), (near[:, k : 2 * k], next_up)]
            cot += [tail[:, :k], tail[:, k:]]
        to_start = place(t0)
        to_start_next = place(t0 + 1)
        to_end = place(t1 + 1)

        def grams():
            for copy in copies:
                copy.wait()
            return low[...], high[...]

        active, back, less, mix_first, mix_second = row_stage(
            proj, cot, square_sum, grams, features
        )
        for s in range(2):
            l0, l1 = 2 * s, 2 * s + 1
            out[s] = dot(to_start, joined([back[l0], back[l1], less[l0]])).astype(bf16)
            weighted = dot(to_start_next, less[l1])
            tail = dot(to_end, joined([active[l0], active[l1]]))
            out[s] += joined([weighted, tail]).astype(bf16)
        first_section = mine[0] == 0
        for i, (one, two) in enumerate(zip(mix_first, mix_second)):
            at = slice(i * k, (i + 1) * k)
            one, two = joined(one), joined(two)
            own[at, :] = jnp.where(first_section, one, two).astype(bf16)
            oth[at, :] = jnp.where(first_section, two, one).astype(bf16)

    columns = jnp.stack([first, second], axis=1)
    rows = jnp.stack([first, second])
    local_ref = pl.BlockSpec(memory_space=pltpu.VMEM)
    far_ref = pl.BlockSpec(memory_space=pl.ANY)
    mix = jax.ShapeDtypeStruct((6 * k, 4 * k), bf16)
    return pl.pallas_call(
        kernel,
        in_specs=[pl.BlockSpec(memory_space=pltpu.SMEM)] + [local_ref] * 3 + [far_ref] * 2,
        out_shape=[jax.ShapeDtypeStruct(received.shape, bf16), mix, mix],
        scratch_shapes=[
            pltpu.VMEM(gram_low.shape, bf16),
            pltpu.VMEM(gram_high.shape, bf16),
            pltpu.SemaphoreType.DMA((2,)),
        ],
        compiler_params=pltpu.CompilerParams(vmem_limit_bytes=16 << 20),
        name="meet",
    )(section[None], received, columns, rows, *in_hbm(gram_low, gram_high))


def unpack(returned, mix_own, mix_other, lanes):
    rows, k = returned.shape[0] // 8, returned.shape[1] // 3

    def kernel(ret, own, far, xs, cs, mix, wide, oth, sem):
        copy = pltpu.make_async_copy(far, oth, sem)
        copy.start()
        for t in range(3):
            wide[t] = ret[:, t * k : (t + 1) * k].astype(f32)
        for j in range(lanes):
            at = slice(j * rows, (j + 1) * rows)
            low = [wide[t, pl.ds(2 * j, rows, stride=8), :].astype(bf16) for t in range(3)]
            high = [wide[t, pl.ds(2 * j + 1, rows, stride=8), :].astype(bf16) for t in range(3)]
            xs[at, :] = joined(low + high[:1])
            cs[at, :] = joined(high[1:])
        copy.wait()
        mix[...] = (own[...].astype(f32) + oth[...].astype(f32)).astype(bf16)

    local_ref = pl.BlockSpec(memory_space=pltpu.VMEM)
    shapes = [(lanes * rows, 4 * k), (lanes * rows, 2 * k), mix_own.shape]
    return pl.pallas_call(
        kernel,
        in_specs=[local_ref, local_ref, pl.BlockSpec(memory_space=pl.ANY)],
        out_shape=[jax.ShapeDtypeStruct(shape, bf16) for shape in shapes],
        scratch_shapes=[
            pltpu.VMEM((3, 8 * rows, k), f32),
            pltpu.VMEM(mix_own.shape, bf16),
            pltpu.SemaphoreType.DMA,
        ],
        compiler_params=pltpu.CompilerParams(vmem_limit_bytes=8 << 20),
        name="unpack",
    )(returned, mix_own, *in_hbm(mix_other))


def piece(at, size, turned, weights, xs, cs, mix):
    both = turned.shape[1]
    k = cs.shape[1] // 2
    total = both // 2
    parts = 2
    chunk = size // parts

    def kernel(at_ref, t_ref, w_ref, xs_ref, cs_ref, mix_ref, major, minor, t_buf, w_buf, sems):
        copies = []
        for i in range(parts):
            rows = pl.ds(pl.multiple_of(at_ref[0] + i * chunk, 16), chunk)
            copies.append(
                [
                    pltpu.make_async_copy(t_ref.at[rows, :], t_buf.at[i], sems.at[i, 0]),
                    pltpu.make_async_copy(w_ref.at[rows, :], w_buf.at[i], sems.at[i, 1]),
                ]
            )
        for copy in copies[0] + copies[1]:
            copy.start()
        for i in range(parts):
            rows = slice(i * chunk, (i + 1) * chunk)
            for copy in copies[i]:
                copy.wait()
            if i + 2 < parts:
                for copy in copies[i + 2]:
                    copy.start()
            value = dot(t_buf[i, :, :total], xs_ref[...]) + dot(w_buf[i], mix_ref[...])
            last = dot(t_buf[i, :, total:], cs_ref[...])
            major[rows, : 2 * k] = value[:, : 2 * k].astype(bf16)
            major[rows, 2 * k :] = (value[:, 2 * k : 3 * k] + last[:, :k]).astype(bf16)
            minor[rows, :] = (value[:, 3 * k :] + last[:, k:]).astype(bf16)

    local_ref = pl.BlockSpec(memory_space=pltpu.VMEM)
    far_ref = pl.BlockSpec(memory_space=pl.ANY)
    return pl.pallas_call(
        kernel,
        in_specs=[pl.BlockSpec(memory_space=pltpu.SMEM)] + [far_ref] * 2 + [local_ref] * 3,
        out_specs=[local_ref] * 2,
        out_shape=[
            jax.ShapeDtypeStruct((size, 3 * k), bf16),
            jax.ShapeDtypeStruct((size, k), bf16),
        ],
        scratch_shapes=[
            pltpu.VMEM((parts, chunk, both), bf16),
            pltpu.VMEM((parts, chunk, 6 * k), bf16),
            pltpu.SemaphoreType.DMA((parts, 2)),
        ],
        compiler_params=pltpu.CompilerParams(vmem_limit_bytes=16 << 20),
        name="piece",
    )(at[None], *in_hbm(turned, weights), xs, cs, mix)


def squares(block):
    rows, width = block.shape

    def kernel(ref, out):
        v = ref[...].astype(f32)
        out[...] = jnp.sum((v * v).reshape(4, rows // 32, 8, width), axis=1)

    return pl.pallas_call(
        kernel,
        out_shape=jax.ShapeDtypeStruct((4, 8, width), f32),
        compiler_params=pltpu.CompilerParams(vmem_limit_bytes=8 << 20),
        name="squares",
    )(block)


def finish(starts, major, minor, features, k):
    quarter = features // 4
    part = quarter // 4
    late = 2
    early = [i for i in range(4) if i != late]
    blocks = [*major, *minor]
    known = [squares(major[i]) for i in early] + [squares(minor[i]) for i in early]

    def kernel(at, *refs):
        ins, known, (down, up, out, sems) = refs[:8], refs[8:14], refs[14:]

        def run(which, group, columns):
            sums = [None] * 4
            for i in range(4):
                if i == late:
                    v = ins[which * 4 + i][:, columns].astype(f32)
                    v = jnp.sum((v * v).reshape(4, part // 8, 8, k), axis=1)
                else:
                    v = known[which * 3 + early.index(i)][:, :, columns]
                sums[i] = ring_sum(v[0], v[2], v[1], v[3])
            total = ring_sum(sums[0], sums[2], sums[1], sums[3])
            mean = jnp.sum(total) * (1.0 / (features * k))
            scale = lax.rsqrt(jnp.full((1, k), mean, f32) + step_eps)
            for i in range(4):
                for j in range(4):
                    row = pl.multiple_of(at[which, i, j], 16)
                    v = ins[which * 4 + i][j * part : (j + 1) * part, columns].astype(f32)
                    out[group, pl.ds(row, part), :] = (v * scale).astype(bf16)

        copies = []
        for group in range(4):
            which = group // 3
            run(which, group, slice(0, k) if which else slice(group * k, (group + 1) * k))
            target = (down, up)[group // 2].at[group % 2]
            copies.append(pltpu.make_async_copy(out.at[group], target, sems.at[group]))
            copies[-1].start()
        for copy in copies:
            copy.wait()

    local_ref = pl.BlockSpec(memory_space=pltpu.VMEM)
    far_ref = pl.BlockSpec(memory_space=pl.ANY)
    return pl.pallas_call(
        kernel,
        in_specs=[pl.BlockSpec(memory_space=pltpu.SMEM)] + [local_ref] * 14,
        out_specs=[far_ref] * 2,
        out_shape=[jax.ShapeDtypeStruct((2, features, k), bf16)] * 2,
        scratch_shapes=[
            pltpu.VMEM((4, features, k), bf16),
            pltpu.SemaphoreType.DMA((4,)),
        ],
        compiler_params=pltpu.CompilerParams(vmem_limit_bytes=16 << 20),
        name="finish",
    )(starts, *blocks, *known)


def coords(peer):
    return peer // 16, (peer // 4) % 4, peer % 4


MAJOR = ((0, 1, 2), (1, 2, 0))
MINOR = ((2, 0, 1), (2, 0, 1))


def hop(values, order, stage, by):
    pairs = []
    for s in range(2):
        axis = order[s][stage]
        for p in range(64):
            c = list(coords(p))
            c[axis] = (c[axis] + by) % 4
            pairs.append((s * 64 + p, s * 64 + c[0] * 16 + c[1] * 4 + c[2]))
    return lax.ppermute(values, ("section", "peer"), pairs)


def ring_sum(own, two, one, three):
    return (own + two) + (one + three)


def summed(parts, order, at, gains=None):
    step = parts[0].shape[0] // 4

    def cut(by):
        start = ((at[1] + by) % 4) * step
        return sum(lax.dynamic_slice_in_dim(p, start, step, axis=0).astype(f32) for p in parts)

    arrived = [hop(cut(by).astype(bf16), order, 1, by) for by in (2, 1, 3)]
    own = cut(0) + sum(part.astype(f32) for part in arrived)
    own = lax.optimization_barrier(own.astype(bf16))
    two, one, three = [hop(own, order, 2, by).astype(f32) for by in (2, 1, 3)]
    total = ring_sum(own.astype(f32), two, one, three)
    return (total if gains is None else total * gains).astype(bf16)


def gathered(block, order):
    wide = jnp.concatenate([block] + [hop(block, order, 1, by) for by in (1, 2, 3)], axis=0)
    return [wide] + [hop(wide, order, 0, by) for by in (1, 2, 3)]


def local(inputs, cotangent, down_proj, up_proj, norm_gain, wiring, live_mask):
    section = lax.axis_index("section")
    peer = lax.axis_index("peer")
    _, lanes, rows, features = inputs.shape
    k = down_proj.shape[3]
    x, c = inputs[0], cotangent[0]
    gain, up = norm_gain[0], up_proj[0]
    is_first = section == 0
    swap = [(0, 1), (1, 0)]
    down = down_proj[0]
    down_other = lax.ppermute(down, "section", swap)
    up_other = lax.ppermute(up, "section", swap)
    gain_other = lax.ppermute(gain, "section", swap)
    sent = front(x, c, down, up, gain)
    received = lax.all_to_all(
        sent.reshape(rows, 8, 3 * k), ("section", "peer"), 0, 0, tiled=True
    ).reshape(2, -1, 3 * k)
    weights, gram_low, gram_high = prepare(
        section, down, up, gain, down_other, up_other, gain_other
    )
    holders = peer_table(wiring, live_mask)
    total = holders.shape[1]
    lane_of = jnp.arange(total, dtype=jnp.int32) // (total // lanes)
    base = holders * 8 + 2 * lane_of
    out, mix_own, mix_leaving = meet(
        section, received, base[0], base[1], gram_low, gram_high, lanes, features
    )
    mix_other = lax.ppermute(mix_leaving, "section", swap)
    returned = lax.all_to_all(
        out.reshape(rows, 8, 3 * k), ("section", "peer"), 0, 0, tiled=True
    ).reshape(8 * rows, 3 * k)
    turned = turn(*lax.optimization_barrier((x, c, mix_own))[:2])
    xs, cs, mix = unpack(returned, mix_own, mix_other, lanes)

    where = jnp.stack(coords(peer))
    at_major, at_minor = (
        [jnp.where(is_first, where[order[0][i]], where[order[1][i]]) for i in range(3)]
        for order in (MAJOR, MINOR)
    )
    quarter = features // 4
    major, minor = [], []
    for by in (2, 1, 3, 0):
        index = ((at_major[0] + by) % 4) * quarter
        part, rest = piece(index.astype(jnp.int32), quarter, turned, weights, xs, cs, mix)
        major.append(hop(part, MAJOR, 0, by) if by else part)
        minor.append(rest)

    def pick_minor(by):
        ahead = (at_minor[0] + by - at_major[0]) % 4
        return lax.select_n(
            jnp.broadcast_to(ahead, minor[0].shape), minor[3], minor[1], minor[0], minor[2]
        )

    step = features // 16
    row = at_major[0] * quarter + at_major[1] * step
    gains = lax.dynamic_slice_in_dim(gain, row, step, axis=1).T
    gains = joined([jnp.broadcast_to(gains[:, l : l + 1], (step, k)) for l in range(2)])
    gains = joined([gains, jnp.ones((step, k), f32)])
    minor = [hop(pick_minor(by), MINOR, 0, by) for by in (2, 1, 3)] + [pick_minor(0)]
    minor = gathered(summed(minor, MINOR, at_minor), MINOR)
    major = gathered(summed(major, MAJOR, at_major, gains), MAJOR)

    back = jnp.arange(4, dtype=jnp.int32)
    starts = jnp.stack(
        [
            ((at[0] - back) % 4)[:, None] * quarter + ((at[1] - back) % 4)[None, :] * step
            for at in (at_major, at_minor)
        ]
    ).astype(jnp.int32)
    down_step, up_step = finish(starts, major, minor, features, k)
    return down_step[None], up_step[None]


def solution(mesh):
    placed = (
        P("peer", None, None, None),
        P("peer", None, None, None),
        P("section", None, None, None),
        P("section", None, None, None),
        P("section", None, None),
        P(),
        P(),
    )
    return jax.shard_map(
        local,
        mesh=mesh,
        in_specs=placed,
        out_specs=(P("section", None, None, None), P("section", None, None, None)),
        check_vma=False,
    )
```

```python
import jax
import jax.numpy as jnp
from jax import lax
from jax.experimental import pallas as pl
from jax.experimental.pallas import tpu as pltpu
from jax.sharding import PartitionSpec as P

norm_eps = 1e-05
step_eps = 1e-06
bf16 = jnp.bfloat16
f32 = jnp.float32


def dot(a, b):
    return jnp.dot(a.astype(bf16), b.astype(bf16), preferred_element_type=f32)


def dot_nt(a, b):
    return lax.dot_general(
        a.astype(bf16), b.astype(bf16), (((1,), (1,)), ((), ())), preferred_element_type=f32
    )


def dot_tn(a, b):
    return lax.dot_general(
        a.astype(bf16), b.astype(bf16), (((0,), (0,)), ((), ())), preferred_element_type=f32
    )


def peer_table(wiring, live_mask):
    live_rank = jnp.cumsum(live_mask, axis=1) - 1
    matches = (live_mask[:, None, :] == 1) & (live_rank[:, None, :] == wiring[:, :, None])
    peer_ids = jnp.arange(live_mask.shape[1], dtype=jnp.int32)
    return jnp.sum(jnp.where(matches, peer_ids, 0), axis=2)


def row_sum(values):
    return jnp.sum(values, axis=1, keepdims=True)


def row_stage(proj, cot, square_sum, grams, feature_count):
    k = cot[0].shape[1]

    def activated(pre):
        r = lax.rsqrt(jnp.maximum(square_sum, 0.0) * (1.0 / feature_count) + norm_eps)
        h = r * pre
        return r, h, (h * jax.nn.sigmoid(h)).astype(bf16)

    first_layer = activated(proj[0][0])
    gram_low, gram_high = grams()

    def cut(g, i, j):
        return g[i * k : (i + 1) * k, j * k : (j + 1) * k].astype(bf16)

    ugd = {(0, 1): cut(gram_low, 0, 0), (2, 3): cut(gram_high, 0, 0)}
    uu = {
        (0, 0): cut(gram_low, 0, 1),
        (0, 1): cut(gram_low, 0, 2),
        (1, 1): cut(gram_low, 1, 2),
        (2, 2): cut(gram_high, 0, 1),
    }
    for i in (0, 1):
        ugd[(i, 2)] = cut(gram_low, i, 3)
        ugd[(i, 3)] = cut(gram_low, i, 4)
        uu[(i, 2)] = cut(gram_low, i, 5)

    hidden, active, inverse, full = [], [], [], []
    for l in range(4):
        pre = proj[l][0]
        for i in range(l):
            pre = pre + dot(active[i], ugd[(i, l)])
        r, h, a = activated(pre) if l else first_layer
        hidden.append(h)
        active.append(a)
        inverse.append(r)
        if l < 3:
            along = proj[l][1]
            for i in range(l):
                along = along + dot(active[i], uu[(i, l)])
            own = dot(a, uu[(l, l)])
            square_sum = square_sum + row_sum((2.0 * along + own) * a.astype(f32))
            full.append(along + own)

    back = [None] * 4
    weight = [None] * 4
    weight[3] = jnp.zeros_like(square_sum)
    for l in (3, 2, 1, 0):
        grad = cot[l]
        for j in range(l + 1, 4):
            grad = grad + dot_nt(back[j], ugd[(l, j)])
        if l < 3:
            grad = grad - weight[l] * full[l]
        for i in range(l + 1, 3):
            grad = grad - weight[i] * dot_nt(active[i], uu[(l, i)])
        sig = jax.nn.sigmoid(hidden[l])
        hid_grad = (grad * sig * (1.0 + hidden[l] * (1.0 - sig))).astype(bf16).astype(f32)
        back[l] = (inverse[l] * hid_grad).astype(bf16)
        if l > 0:
            centred = row_sum(hidden[l] * hid_grad) * (1.0 / feature_count)
            weight[l - 1] = weight[l] + inverse[l] * inverse[l] * centred
    less = [(-weight[l] * active[l].astype(f32)).astype(bf16) for l in range(4)]

    def scaled(w, l):
        return (-w * active[l].astype(f32)).astype(bf16)

    def against(left, parts):
        turned = left.astype(f32).T.astype(bf16)
        product = dot(turned, jnp.concatenate(parts, axis=1))
        return [product[:, i * k : (i + 1) * k] for i in range(len(parts))]

    a, b, w = active, back, weight
    a0 = against(a[0], [b[1], less[0], less[1], b[2], b[3], less[2]])
    a1 = against(a[1], [scaled(w[1], 0), less[1], b[2], b[3], less[2]])
    a2 = against(a[2], [scaled(w[2], 0), scaled(w[2], 1), b[3], less[2]])
    b1 = against(b[1], [a[0]])
    b2 = against(b[2], [a[0], a[1]])
    b3 = against(b[3], [a[0], a[1], a[2]])
    none = jnp.zeros((k, k), f32)
    mix_first = [
        [none, none, b1[0], none],
        [none, a0[0], a0[1], a0[2]],
        [none, none, a1[0], a1[1]],
        [none, none, b2[0], b2[1]],
        [none, none, b3[0], b3[1]],
        [none, none, a2[0], a2[1]],
    ]
    mix_second = [
        [none, none, none, none],
        [a0[3], a0[4], a0[5], none],
        [a1[2], a1[3], a1[4], none],
        [none, none, none, none],
        [none, none, b3[2], none],
        [none, a2[2], a2[3], none],
    ]
    return active, back, less, mix_first, mix_second


def in_hbm(*arrays):
    return [pltpu.with_memory_space_constraint(array, pltpu.HBM) for array in arrays]


def joined(parts):
    return jnp.concatenate(list(parts), axis=1)


def front(x, c, down, up, gain):
    lanes, rows, features = x.shape
    k = down.shape[2]
    block = 1280
    steps = features // block
    total = lanes * rows

    def kernel(x_ref, c_ref, d_ref, u_ref, g_ref, sent_ref, acc, squares, packed):
        step = pl.program_id(0)
        columns = jnp.concatenate([g_ref[...]] * 4, axis=0).T
        gained = [
            (d_ref[l].astype(f32) * columns[:, l : l + 1]).astype(bf16) for l in range(2)
        ]
        ups = [u_ref[0], u_ref[1]]
        flat = x_ref[...].reshape(total, block)
        of_x = dot(flat, joined(gained + ups))
        of_c = dot(c_ref[...].reshape(total, block), joined(ups))
        part = jnp.zeros((total, k), f32)
        for j in range(block // k):
            wide = flat[:, j * k : (j + 1) * k].astype(f32)
            part = part + wide * wide

        @pl.when(step == 0)
        def _():
            acc[:, : 4 * k] = of_x
            acc[:, 4 * k :] = of_c
            squares[...] = part

        @pl.when(step > 0)
        def _():
            acc[:, : 4 * k] += of_x
            acc[:, 4 * k :] += of_c
            squares[...] += part

        @pl.when(step == steps - 1)
        def _():
            for j in range(lanes):
                at = slice(j * rows, (j + 1) * rows)
                for half in range(2):
                    for t in range(3):
                        packed[t, pl.ds(2 * j + half, rows, stride=8), :] = acc[
                            at, (half * 3 + t) * k : (half * 3 + t + 1) * k
                        ]
                square = jnp.broadcast_to(row_sum(squares[at, :]), (rows, k))
                coarse = square.astype(bf16).astype(f32)
                packed[j, pl.ds(6, rows, stride=8), :] = coarse
                packed[j, pl.ds(7, rows, stride=8), :] = square - coarse
            for t in range(3):
                sent_ref[:, t * k : (t + 1) * k] = packed[t].astype(bf16)

    return pl.pallas_call(
        kernel,
        grid=(steps,),
        in_specs=[
            pl.BlockSpec((lanes, rows, block), lambda i: (0, 0, i)),
            pl.BlockSpec((lanes, rows, block), lambda i: (0, 0, i)),
            pl.BlockSpec((2, block, k), lambda i: (0, i, 0)),
            pl.BlockSpec((2, block, k), lambda i: (0, i, 0)),
            pl.BlockSpec((2, block), lambda i: (0, i)),
        ],
        out_specs=pl.BlockSpec((8 * rows, 3 * k), lambda i: (0, 0)),
        out_shape=jax.ShapeDtypeStruct((8 * rows, 3 * k), bf16),
        scratch_shapes=[
            pltpu.VMEM((total, 6 * k), f32),
            pltpu.VMEM((total, k), f32),
            pltpu.VMEM((3, 8 * rows, k), f32),
        ],
        compiler_params=pltpu.CompilerParams(vmem_limit_bytes=20 << 20),
        name="front",
    )(*in_hbm(x, c, down, up, gain))


def prepare(section, down, up, gain, down_other, up_other, gain_other):
    _, features, k = down.shape
    block = 1024
    steps = features // block

    def kernel(s_ref, d, u, g, d2, u2, g2, w_ref, low_out, high_out, low_ref, high_ref):
        step = pl.program_id(0)
        gains = jnp.concatenate([g[...], g2[...]] * 2, axis=0).T
        first = s_ref[0] == 0

        def choose(one, two):
            return jnp.where(first, one.astype(f32), two.astype(f32))

        gain_one = choose(gains[:, :2], gains[:, 2:4])
        gain_two = choose(gains[:, 2:4], gains[:, :2])
        parts = [
            choose(d[1], d2[1]) * gain_one[:, 1:2],
            choose(u[0], u2[0]),
            choose(u[1], u2[1]),
            choose(d2[0], d[0]) * gain_two[:, :1],
            choose(d2[1], d[1]) * gain_two[:, 1:2],
            choose(u2[0], u[0]),
        ]
        parts = [part.astype(bf16) for part in parts]
        weights = joined(parts)
        w_ref[...] = weights
        low = dot_tn(joined(parts[1:3]), weights)
        high = dot_tn(parts[5], joined(parts[4:]))

        @pl.when(step == 0)
        def _():
            low_ref[...] = low
            high_ref[...] = high

        @pl.when(step > 0)
        def _():
            low_ref[...] += low
            high_ref[...] += high

        @pl.when(step == steps - 1)
        def _():
            low_out[...] = low_ref[...].astype(bf16)
            high_out[...] = high_ref[...].astype(bf16)

    two = pl.BlockSpec((2, block, k), lambda i, s: (0, i, 0))
    row = pl.BlockSpec((2, block), lambda i, s: (0, i))
    return pl.pallas_call(
        kernel,
        grid_spec=pltpu.PrefetchScalarGridSpec(
            num_scalar_prefetch=1,
            grid=(steps,),
            in_specs=[two, two, row, two, two, row],
            out_specs=[
                pl.BlockSpec((block, 6 * k), lambda i, s: (i, 0)),
                pl.BlockSpec((2 * k, 6 * k), lambda i, s: (0, 0)),
                pl.BlockSpec((k, 2 * k), lambda i, s: (0, 0)),
            ],
            scratch_shapes=[pltpu.VMEM((2 * k, 6 * k), f32), pltpu.VMEM((k, 2 * k), f32)],
        ),
        out_shape=[
            pltpu.HBM((features, 6 * k), bf16),
            pltpu.HBM((2 * k, 6 * k), bf16),
            pltpu.HBM((k, 2 * k), bf16),
        ],
        compiler_params=pltpu.CompilerParams(vmem_limit_bytes=24 << 20),
        name="prepare",
    )(section[None], *in_hbm(down, up, gain), down_other, up_other, gain_other)


def turn(x, c):
    lanes, rows, features = x.shape
    block = 1024

    def kernel(x_ref, c_ref, out):
        for j in range(lanes):
            out[:, j * rows : (j + 1) * rows] = x_ref[j].T
            out[:, (lanes + j) * rows : (lanes + j + 1) * rows] = c_ref[j].T

    spec = pl.BlockSpec((lanes, rows, block), lambda i: (0, 0, i))
    return pl.pallas_call(
        kernel,
        grid=(features // block,),
        in_specs=[spec, spec],
        out_specs=pl.BlockSpec((block, 2 * lanes * rows), lambda i: (i, 0)),
        out_shape=pltpu.HBM((features, 2 * lanes * rows), bf16),
        compiler_params=pltpu.CompilerParams(vmem_limit_bytes=12 << 20),
        name="turn",
    )(*in_hbm(x, c))


def meet(section, received, first, second, gram_low, gram_high, lanes, features):
    total = first.shape[0]
    group = total // lanes
    slots = received.shape[1]
    k = received.shape[2] // 3

    def kernel(mine, rec, columns, rows, far_low, far_high, out, own, oth, low, high, sems):
        copies = [
            pltpu.make_async_copy(far_low, low, sems.at[0]),
            pltpu.make_async_copy(far_high, high, sems.at[1]),
        ]
        for copy in copies:
            copy.start()
        i0, i1 = columns[:, :1], columns[:, 1:]
        t0, t1 = rows[:1, :], rows[1:, :]
        grid = lax.broadcasted_iota(jnp.int32, (total, slots), 1)
        turned = lax.broadcasted_iota(jnp.int32, (slots, total), 0)

        def pick(base):
            return (grid == base).astype(f32).astype(bf16)

        def place(base):
            return (turned == base).astype(f32).astype(bf16)

        at_start = pick(i0)
        at_start_next = pick(i0 + 1)
        at_end = pick(i1 + 1)
        lane = lax.broadcasted_iota(jnp.int32, (total, 1), 0) // group
        norm_row = i0 - 2 * lane + 6
        sums = dot(pick(norm_row), rec[0]) + dot(pick(norm_row + 1), rec[0])
        square_sum = jnp.concatenate(
            [sums[j * group : (j + 1) * group, j * k : (j + 1) * k] for j in range(lanes)], axis=0
        )[:, :1]
        proj, cot = [], []
        for s in range(2):
            near = dot(at_start, rec[s])
            next_up = dot(at_start_next, rec[s, :, :k])
            tail = dot(at_end, rec[s, :, k:])
            proj += [(near[:, :k], near[:, 2 * k :]), (near[:, k : 2 * k], next_up)]
            cot += [tail[:, :k], tail[:, k:]]
        to_start = place(t0)
        to_start_next = place(t0 + 1)
        to_end = place(t1 + 1)

        def grams():
            for copy in copies:
                copy.wait()
            return low[...], high[...]

        active, back, less, mix_first, mix_second = row_stage(
            proj, cot, square_sum, grams, features
        )
        for s in range(2):
            l0, l1 = 2 * s, 2 * s + 1
            out[s] = dot(to_start, joined([back[l0], back[l1], less[l0]])).astype(bf16)
            weighted = dot(to_start_next, less[l1])
            tail = dot(to_end, joined([active[l0], active[l1]]))
            out[s] += joined([weighted, tail]).astype(bf16)
        first_section = mine[0] == 0
        for i, (one, two) in enumerate(zip(mix_first, mix_second)):
            at = slice(i * k, (i + 1) * k)
            one, two = joined(one), joined(two)
            own[at, :] = jnp.where(first_section, one, two).astype(bf16)
            oth[at, :] = jnp.where(first_section, two, one).astype(bf16)

    columns = jnp.stack([first, second], axis=1)
    rows = jnp.stack([first, second])
    local_ref = pl.BlockSpec(memory_space=pltpu.VMEM)
    far_ref = pl.BlockSpec(memory_space=pl.ANY)
    mix = jax.ShapeDtypeStruct((6 * k, 4 * k), bf16)
    return pl.pallas_call(
        kernel,
        in_specs=[pl.BlockSpec(memory_space=pltpu.SMEM)] + [local_ref] * 3 + [far_ref] * 2,
        out_shape=[jax.ShapeDtypeStruct(received.shape, bf16), mix, mix],
        scratch_shapes=[
            pltpu.VMEM(gram_low.shape, bf16),
            pltpu.VMEM(gram_high.shape, bf16),
            pltpu.SemaphoreType.DMA((2,)),
        ],
        compiler_params=pltpu.CompilerParams(vmem_limit_bytes=16 << 20),
        name="meet",
    )(section[None], received, columns, rows, *in_hbm(gram_low, gram_high))


def unpack(returned, mix_own, mix_other, lanes):
    rows, k = returned.shape[0] // 8, returned.shape[1] // 3

    def kernel(ret, own, far, xs, cs, mix, wide, oth, sem):
        copy = pltpu.make_async_copy(far, oth, sem)
        copy.start()
        for t in range(3):
            wide[t] = ret[:, t * k : (t + 1) * k].astype(f32)
        for j in range(lanes):
            at = slice(j * rows, (j + 1) * rows)
            low = [wide[t, pl.ds(2 * j, rows, stride=8), :].astype(bf16) for t in range(3)]
            high = [wide[t, pl.ds(2 * j + 1, rows, stride=8), :].astype(bf16) for t in range(3)]
            xs[at, :] = joined(low + high[:1])
            cs[at, :] = joined(high[1:])
        copy.wait()
        mix[...] = (own[...].astype(f32) + oth[...].astype(f32)).astype(bf16)

    local_ref = pl.BlockSpec(memory_space=pltpu.VMEM)
    shapes = [(lanes * rows, 4 * k), (lanes * rows, 2 * k), mix_own.shape]
    return pl.pallas_call(
        kernel,
        in_specs=[local_ref, local_ref, pl.BlockSpec(memory_space=pl.ANY)],
        out_shape=[jax.ShapeDtypeStruct(shape, bf16) for shape in shapes],
        scratch_shapes=[
            pltpu.VMEM((3, 8 * rows, k), f32),
            pltpu.VMEM(mix_own.shape, bf16),
            pltpu.SemaphoreType.DMA,
        ],
        compiler_params=pltpu.CompilerParams(vmem_limit_bytes=8 << 20),
        name="unpack",
    )(returned, mix_own, *in_hbm(mix_other))


def piece(at, size, turned, weights, xs, cs, mix):
    both = turned.shape[1]
    k = cs.shape[1] // 2
    total = both // 2
    parts = 2
    chunk = size // parts

    def kernel(at_ref, t_ref, w_ref, xs_ref, cs_ref, mix_ref, major, minor, t_buf, w_buf, sems):
        copies = []
        for i in range(parts):
            rows = pl.ds(pl.multiple_of(at_ref[0] + i * chunk, 16), chunk)
            copies.append(
                [
                    pltpu.make_async_copy(t_ref.at[rows, :], t_buf.at[i], sems.at[i, 0]),
                    pltpu.make_async_copy(w_ref.at[rows, :], w_buf.at[i], sems.at[i, 1]),
                ]
            )
        for copy in copies[0] + copies[1]:
            copy.start()
        for i in range(parts):
            rows = slice(i * chunk, (i + 1) * chunk)
            for copy in copies[i]:
                copy.wait()
            if i + 2 < parts:
                for copy in copies[i + 2]:
                    copy.start()
            value = dot(t_buf[i, :, :total], xs_ref[...]) + dot(w_buf[i], mix_ref[...])
            last = dot(t_buf[i, :, total:], cs_ref[...])
            major[rows, : 2 * k] = value[:, : 2 * k].astype(bf16)
            major[rows, 2 * k :] = (value[:, 2 * k : 3 * k] + last[:, :k]).astype(bf16)
            minor[rows, :] = (value[:, 3 * k :] + last[:, k:]).astype(bf16)

    local_ref = pl.BlockSpec(memory_space=pltpu.VMEM)
    far_ref = pl.BlockSpec(memory_space=pl.ANY)
    return pl.pallas_call(
        kernel,
        in_specs=[pl.BlockSpec(memory_space=pltpu.SMEM)] + [far_ref] * 2 + [local_ref] * 3,
        out_specs=[local_ref] * 2,
        out_shape=[
            jax.ShapeDtypeStruct((size, 3 * k), bf16),
            jax.ShapeDtypeStruct((size, k), bf16),
        ],
        scratch_shapes=[
            pltpu.VMEM((parts, chunk, both), bf16),
            pltpu.VMEM((parts, chunk, 6 * k), bf16),
            pltpu.SemaphoreType.DMA((parts, 2)),
        ],
        compiler_params=pltpu.CompilerParams(vmem_limit_bytes=16 << 20),
        name="piece",
    )(at[None], *in_hbm(turned, weights), xs, cs, mix)


def squares(block):
    rows, width = block.shape

    def kernel(ref, out):
        v = ref[...].astype(f32)
        out[...] = jnp.sum((v * v).reshape(4, rows // 32, 8, width), axis=1)

    return pl.pallas_call(
        kernel,
        out_shape=jax.ShapeDtypeStruct((4, 8, width), f32),
        compiler_params=pltpu.CompilerParams(vmem_limit_bytes=8 << 20),
        name="squares",
    )(block)


def finish(starts, major, minor, features, k):
    quarter = features // 4
    part = quarter // 4
    late = 2
    early = [i for i in range(4) if i != late]
    blocks = [*major, *minor]
    known = [squares(major[i]) for i in early] + [squares(minor[i]) for i in early]

    def kernel(at, *refs):
        ins, known, (down, up, out, sems) = refs[:8], refs[8:14], refs[14:]

        def run(which, group, columns):
            sums = [None] * 4
            for i in range(4):
                if i == late:
                    v = ins[which * 4 + i][:, columns].astype(f32)
                    v = jnp.sum((v * v).reshape(4, part // 8, 8, k), axis=1)
                else:
                    v = known[which * 3 + early.index(i)][:, :, columns]
                sums[i] = ring_sum(v[0], v[2], v[1], v[3])
            total = ring_sum(sums[0], sums[2], sums[1], sums[3])
            mean = jnp.sum(total) * (1.0 / (features * k))
            scale = lax.rsqrt(jnp.full((1, k), mean, f32) + step_eps)
            for i in range(4):
                for j in range(4):
                    row = pl.multiple_of(at[which, i, j], 16)
                    v = ins[which * 4 + i][j * part : (j + 1) * part, columns].astype(f32)
                    out[group, pl.ds(row, part), :] = (v * scale).astype(bf16)

        copies = []
        for group in range(4):
            which = group // 3
            run(which, group, slice(0, k) if which else slice(group * k, (group + 1) * k))
            target = (down, up)[group // 2].at[group % 2]
            copies.append(pltpu.make_async_copy(out.at[group], target, sems.at[group]))
            copies[-1].start()
        for copy in copies:
            copy.wait()

    local_ref = pl.BlockSpec(memory_space=pltpu.VMEM)
    far_ref = pl.BlockSpec(memory_space=pl.ANY)
    return pl.pallas_call(
        kernel,
        in_specs=[pl.BlockSpec(memory_space=pltpu.SMEM)] + [local_ref] * 14,
        out_specs=[far_ref] * 2,
        out_shape=[jax.ShapeDtypeStruct((2, features, k), bf16)] * 2,
        scratch_shapes=[
            pltpu.VMEM((4, features, k), bf16),
            pltpu.SemaphoreType.DMA((4,)),
        ],
        compiler_params=pltpu.CompilerParams(vmem_limit_bytes=16 << 20),
        name="finish",
    )(starts, *blocks, *known)


def coords(peer):
    return peer // 16, (peer // 4) % 4, peer % 4


MAJOR = ((0, 1, 2), (1, 2, 0))
MINOR = ((2, 0, 1), (2, 0, 1))


def hop(values, order, stage, by):
    pairs = []
    for s in range(2):
        axis = order[s][stage]
        for p in range(64):
            c = list(coords(p))
            c[axis] = (c[axis] + by) % 4
            pairs.append((s * 64 + p, s * 64 + c[0] * 16 + c[1] * 4 + c[2]))
    return lax.ppermute(values, ("section", "peer"), pairs)


def ring_sum(own, two, one, three):
    return (own + two) + (one + three)


def summed(parts, order, at, gains=None):
    step = parts[0].shape[0] // 4

    def cut(by):
        start = ((at[1] + by) % 4) * step
        return sum(lax.dynamic_slice_in_dim(p, start, step, axis=0).astype(f32) for p in parts)

    arrived = [hop(cut(by).astype(bf16), order, 1, by) for by in (2, 1, 3)]
    own = cut(0) + sum(part.astype(f32) for part in arrived)
    own = lax.optimization_barrier(own.astype(bf16))
    two, one, three = [hop(own, order, 2, by).astype(f32) for by in (2, 1, 3)]
    total = ring_sum(own.astype(f32), two, one, three)
    return (total if gains is None else total * gains).astype(bf16)


def gathered(block, order):
    wide = jnp.concatenate([block] + [hop(block, order, 1, by) for by in (1, 2, 3)], axis=0)
    return [wide] + [hop(wide, order, 0, by) for by in (1, 2, 3)]


def local(inputs, cotangent, down_proj, up_proj, norm_gain, wiring, live_mask):
    section = lax.axis_index("section")
    peer = lax.axis_index("peer")
    _, lanes, rows, features = inputs.shape
    k = down_proj.shape[3]
    x, c = inputs[0], cotangent[0]
    gain, up = norm_gain[0], up_proj[0]
    is_first = section == 0
    swap = [(0, 1), (1, 0)]
    down = down_proj[0]
    down_other = lax.ppermute(down, "section", swap)
    up_other = lax.ppermute(up, "section", swap)
    gain_other = lax.ppermute(gain, "section", swap)
    sent = front(x, c, down, up, gain)
    received = lax.all_to_all(
        sent.reshape(rows, 8, 3 * k), ("section", "peer"), 0, 0, tiled=True
    ).reshape(2, -1, 3 * k)
    weights, gram_low, gram_high = prepare(
        section, down, up, gain, down_other, up_other, gain_other
    )
    holders = peer_table(wiring, live_mask)
    total = holders.shape[1]
    lane_of = jnp.arange(total, dtype=jnp.int32) // (total // lanes)
    base = holders * 8 + 2 * lane_of
    out, mix_own, mix_leaving = meet(
        section, received, base[0], base[1], gram_low, gram_high, lanes, features
    )
    mix_other = lax.ppermute(mix_leaving, "section", swap)
    returned = lax.all_to_all(
        out.reshape(rows, 8, 3 * k), ("section", "peer"), 0, 0, tiled=True
    ).reshape(8 * rows, 3 * k)
    turned = turn(*lax.optimization_barrier((x, c, mix_own))[:2])
    xs, cs, mix = unpack(returned, mix_own, mix_other, lanes)

    where = jnp.stack(coords(peer))
    at_major, at_minor = (
        [jnp.where(is_first, where[order[0][i]], where[order[1][i]]) for i in range(3)]
        for order in (MAJOR, MINOR)
    )
    quarter = features // 4
    major, minor = [], []
    for by in (2, 1, 3, 0):
        index = ((at_major[0] + by) % 4) * quarter
        part, rest = piece(index.astype(jnp.int32), quarter, turned, weights, xs, cs, mix)
        major.append(hop(part, MAJOR, 0, by) if by else part)
        minor.append(rest)

    def pick_minor(by):
        ahead = (at_minor[0] + by - at_major[0]) % 4
        return lax.select_n(
            jnp.broadcast_to(ahead, minor[0].shape), minor[3], minor[1], minor[0], minor[2]
        )

    step = features // 16
    row = at_major[0] * quarter + at_major[1] * step
    gains = lax.dynamic_slice_in_dim(gain, row, step, axis=1).T
    gains = joined([jnp.broadcast_to(gains[:, l : l + 1], (step, k)) for l in range(2)])
    gains = joined([gains, jnp.ones((step, k), f32)])
    minor = [hop(pick_minor(by), MINOR, 0, by) for by in (2, 1, 3)] + [pick_minor(0)]
    minor = gathered(summed(minor, MINOR, at_minor), MINOR)
    major = gathered(summed(major, MAJOR, at_major, gains), MAJOR)

    back = jnp.arange(4, dtype=jnp.int32)
    starts = jnp.stack(
        [
            ((at[0] - back) % 4)[:, None] * quarter + ((at[1] - back) % 4)[None, :] * step
            for at in (at_major, at_minor)
        ]
    ).astype(jnp.int32)
    down_step, up_step = finish(starts, major, minor, features, k)
    return down_step[None], up_step[None]


def solution(mesh):
    placed = (
        P("peer", None, None, None),
        P("peer", None, None, None),
        P("section", None, None, None),
        P("section", None, None, None),
        P("section", None, None),
        P(),
        P(),
    )
    return jax.shard_map(
        local,
        mesh=mesh,
        in_specs=placed,
        out_specs=(P("section", None, None, None), P("section", None, None, None)),
        check_vma=False,
    )
```

```python
import jax
import jax.numpy as jnp
from jax import lax
from jax.experimental import pallas as pl
from jax.experimental.pallas import tpu as pltpu
from jax.sharding import PartitionSpec as P

norm_eps = 1e-05
step_eps = 1e-06
bf16 = jnp.bfloat16
f32 = jnp.float32


def dot(a, b):
    return jnp.dot(a.astype(bf16), b.astype(bf16), preferred_element_type=f32)


def dot_nt(a, b):
    return lax.dot_general(
        a.astype(bf16), b.astype(bf16), (((1,), (1,)), ((), ())), preferred_element_type=f32
    )


def dot_tn(a, b):
    return lax.dot_general(
        a.astype(bf16), b.astype(bf16), (((0,), (0,)), ((), ())), preferred_element_type=f32
    )


def peer_table(wiring, live_mask):
    live_rank = jnp.cumsum(live_mask, axis=1) - 1
    matches = (live_mask[:, None, :] == 1) & (live_rank[:, None, :] == wiring[:, :, None])
    peer_ids = jnp.arange(live_mask.shape[1], dtype=jnp.int32)
    return jnp.sum(jnp.where(matches, peer_ids, 0), axis=2)


def row_sum(values):
    return jnp.sum(values, axis=1, keepdims=True)


def row_stage(proj, cot, square_sum, grams, feature_count):
    k = cot[0].shape[1]

    def activated(pre):
        r = lax.rsqrt(jnp.maximum(square_sum, 0.0) * (1.0 / feature_count) + norm_eps)
        h = r * pre
        return r, h, (h * jax.nn.sigmoid(h)).astype(bf16)

    first_layer = activated(proj[0][0])
    gram_low, gram_high = grams()

    def cut(g, i, j):
        return g[i * k : (i + 1) * k, j * k : (j + 1) * k].astype(bf16)

    ugd = {(0, 1): cut(gram_low, 0, 0), (2, 3): cut(gram_high, 0, 0)}
    uu = {
        (0, 0): cut(gram_low, 0, 1),
        (0, 1): cut(gram_low, 0, 2),
        (1, 1): cut(gram_low, 1, 2),
        (2, 2): cut(gram_high, 0, 1),
    }
    for i in (0, 1):
        ugd[(i, 2)] = cut(gram_low, i, 3)
        ugd[(i, 3)] = cut(gram_low, i, 4)
        uu[(i, 2)] = cut(gram_low, i, 5)

    hidden, active, inverse, full = [], [], [], []
    for l in range(4):
        pre = proj[l][0]
        for i in range(l):
            pre = pre + dot(active[i], ugd[(i, l)])
        r, h, a = activated(pre) if l else first_layer
        hidden.append(h)
        active.append(a)
        inverse.append(r)
        if l < 3:
            along = proj[l][1]
            for i in range(l):
                along = along + dot(active[i], uu[(i, l)])
            own = dot(a, uu[(l, l)])
            square_sum = square_sum + row_sum((2.0 * along + own) * a.astype(f32))
            full.append(along + own)

    back = [None] * 4
    weight = [None] * 4
    weight[3] = jnp.zeros_like(square_sum)
    for l in (3, 2, 1, 0):
        grad = cot[l]
        for j in range(l + 1, 4):
            grad = grad + dot_nt(back[j], ugd[(l, j)])
        if l < 3:
            grad = grad - weight[l] * full[l]
        for i in range(l + 1, 3):
            grad = grad - weight[i] * dot_nt(active[i], uu[(l, i)])
        sig = jax.nn.sigmoid(hidden[l])
        hid_grad = (grad * sig * (1.0 + hidden[l] * (1.0 - sig))).astype(bf16).astype(f32)
        back[l] = (inverse[l] * hid_grad).astype(bf16)
        if l > 0:
            centred = row_sum(hidden[l] * hid_grad) * (1.0 / feature_count)
            weight[l - 1] = weight[l] + inverse[l] * inverse[l] * centred
    less = [(-weight[l] * active[l].astype(f32)).astype(bf16) for l in range(4)]

    def scaled(w, l):
        return (-w * active[l].astype(f32)).astype(bf16)

    def against(left, parts):
        turned = left.astype(f32).T.astype(bf16)
        product = dot(turned, jnp.concatenate(parts, axis=1))
        return [product[:, i * k : (i + 1) * k] for i in range(len(parts))]

    a, b, w = active, back, weight
    a0 = against(a[0], [b[1], less[0], less[1], b[2], b[3], less[2]])
    a1 = against(a[1], [scaled(w[1], 0), less[1], b[2], b[3], less[2]])
    a2 = against(a[2], [scaled(w[2], 0), scaled(w[2], 1), b[3], less[2]])
    b1 = against(b[1], [a[0]])
    b2 = against(b[2], [a[0], a[1]])
    b3 = against(b[3], [a[0], a[1], a[2]])
    none = jnp.zeros((k, k), f32)
    mix_first = [
        [none, none, b1[0], none],
        [none, a0[0], a0[1], a0[2]],
        [none, none, a1[0], a1[1]],
        [none, none, b2[0], b2[1]],
        [none, none, b3[0], b3[1]],
        [none, none, a2[0], a2[1]],
    ]
    mix_second = [
        [none, none, none, none],
        [a0[3], a0[4], a0[5], none],
        [a1[2], a1[3], a1[4], none],
        [none, none, none, none],
        [none, none, b3[2], none],
        [none, a2[2], a2[3], none],
    ]
    return active, back, less, mix_first, mix_second


def in_hbm(*arrays):
    return [pltpu.with_memory_space_constraint(array, pltpu.HBM) for array in arrays]


def joined(parts):
    return jnp.concatenate(list(parts), axis=1)


def front(x, c, down, up, gain):
    lanes, rows, features = x.shape
    k = down.shape[2]
    block = 1280
    steps = features // block
    total = lanes * rows

    def kernel(x_ref, c_ref, d_ref, u_ref, g_ref, sent_ref, acc, squares, packed):
        step = pl.program_id(0)
        columns = jnp.concatenate([g_ref[...]] * 4, axis=0).T
        gained = [
            (d_ref[l].astype(f32) * columns[:, l : l + 1]).astype(bf16) for l in range(2)
        ]
        ups = [u_ref[0], u_ref[1]]
        flat = x_ref[...].reshape(total, block)
        of_x = dot(flat, joined(gained + ups))
        of_c = dot(c_ref[...].reshape(total, block), joined(ups))
        part = jnp.zeros((total, k), f32)
        for j in range(block // k):
            wide = flat[:, j * k : (j + 1) * k].astype(f32)
            part = part + wide * wide

        @pl.when(step == 0)
        def _():
            acc[:, : 4 * k] = of_x
            acc[:, 4 * k :] = of_c
            squares[...] = part

        @pl.when(step > 0)
        def _():
            acc[:, : 4 * k] += of_x
            acc[:, 4 * k :] += of_c
            squares[...] += part

        @pl.when(step == steps - 1)
        def _():
            for j in range(lanes):
                at = slice(j * rows, (j + 1) * rows)
                for half in range(2):
                    for t in range(3):
                        packed[t, pl.ds(2 * j + half, rows, stride=8), :] = acc[
                            at, (half * 3 + t) * k : (half * 3 + t + 1) * k
                        ]
                square = jnp.broadcast_to(row_sum(squares[at, :]), (rows, k))
                coarse = square.astype(bf16).astype(f32)
                packed[j, pl.ds(6, rows, stride=8), :] = coarse
                packed[j, pl.ds(7, rows, stride=8), :] = square - coarse
            for t in range(3):
                sent_ref[:, t * k : (t + 1) * k] = packed[t].astype(bf16)

    return pl.pallas_call(
        kernel,
        grid=(steps,),
        in_specs=[
            pl.BlockSpec((lanes, rows, block), lambda i: (0, 0, i)),
            pl.BlockSpec((lanes, rows, block), lambda i: (0, 0, i)),
            pl.BlockSpec((2, block, k), lambda i: (0, i, 0)),
            pl.BlockSpec((2, block, k), lambda i: (0, i, 0)),
            pl.BlockSpec((2, block), lambda i: (0, i)),
        ],
        out_specs=pl.BlockSpec((8 * rows, 3 * k), lambda i: (0, 0)),
        out_shape=jax.ShapeDtypeStruct((8 * rows, 3 * k), bf16),
        scratch_shapes=[
            pltpu.VMEM((total, 6 * k), f32),
            pltpu.VMEM((total, k), f32),
            pltpu.VMEM((3, 8 * rows, k), f32),
        ],
        compiler_params=pltpu.CompilerParams(vmem_limit_bytes=20 << 20),
        name="front",
    )(*in_hbm(x, c, down, up, gain))


def prepare(section, down, up, gain, down_other, up_other, gain_other):
    _, features, k = down.shape
    block = 1024
    steps = features // block

    def kernel(s_ref, d, u, g, d2, u2, g2, w_ref, low_out, high_out, low_ref, high_ref):
        step = pl.program_id(0)
        gains = jnp.concatenate([g[...], g2[...]] * 2, axis=0).T
        first = s_ref[0] == 0

        def choose(one, two):
            return jnp.where(first, one.astype(f32), two.astype(f32))

        gain_one = choose(gains[:, :2], gains[:, 2:4])
        gain_two = choose(gains[:, 2:4], gains[:, :2])
        parts = [
            choose(d[1], d2[1]) * gain_one[:, 1:2],
            choose(u[0], u2[0]),
            choose(u[1], u2[1]),
            choose(d2[0], d[0]) * gain_two[:, :1],
            choose(d2[1], d[1]) * gain_two[:, 1:2],
            choose(u2[0], u[0]),
        ]
        parts = [part.astype(bf16) for part in parts]
        weights = joined(parts)
        w_ref[...] = weights
        low = dot_tn(joined(parts[1:3]), weights)
        high = dot_tn(parts[5], joined(parts[4:]))

        @pl.when(step == 0)
        def _():
            low_ref[...] = low
            high_ref[...] = high

        @pl.when(step > 0)
        def _():
            low_ref[...] += low
            high_ref[...] += high

        @pl.when(step == steps - 1)
        def _():
            low_out[...] = low_ref[...].astype(bf16)
            high_out[...] = high_ref[...].astype(bf16)

    two = pl.BlockSpec((2, block, k), lambda i, s: (0, i, 0))
    row = pl.BlockSpec((2, block), lambda i, s: (0, i))
    return pl.pallas_call(
        kernel,
        grid_spec=pltpu.PrefetchScalarGridSpec(
            num_scalar_prefetch=1,
            grid=(steps,),
            in_specs=[two, two, row, two, two, row],
            out_specs=[
                pl.BlockSpec((block, 6 * k), lambda i, s: (i, 0)),
                pl.BlockSpec((2 * k, 6 * k), lambda i, s: (0, 0)),
                pl.BlockSpec((k, 2 * k), lambda i, s: (0, 0)),
            ],
            scratch_shapes=[pltpu.VMEM((2 * k, 6 * k), f32), pltpu.VMEM((k, 2 * k), f32)],
        ),
        out_shape=[
            pltpu.HBM((features, 6 * k), bf16),
            pltpu.HBM((2 * k, 6 * k), bf16),
            pltpu.HBM((k, 2 * k), bf16),
        ],
        compiler_params=pltpu.CompilerParams(vmem_limit_bytes=24 << 20),
        name="prepare",
    )(section[None], *in_hbm(down, up, gain), down_other, up_other, gain_other)


def turn(x, c):
    lanes, rows, features = x.shape
    block = 1024

    def kernel(x_ref, c_ref, out):
        for j in range(lanes):
            out[:, j * rows : (j + 1) * rows] = x_ref[j].T
            out[:, (lanes + j) * rows : (lanes + j + 1) * rows] = c_ref[j].T

    spec = pl.BlockSpec((lanes, rows, block), lambda i: (0, 0, i))
    return pl.pallas_call(
        kernel,
        grid=(features // block,),
        in_specs=[spec, spec],
        out_specs=pl.BlockSpec((block, 2 * lanes * rows), lambda i: (i, 0)),
        out_shape=pltpu.HBM((features, 2 * lanes * rows), bf16),
        compiler_params=pltpu.CompilerParams(vmem_limit_bytes=12 << 20),
        name="turn",
    )(*in_hbm(x, c))


def meet(section, received, first, second, gram_low, gram_high, lanes, features):
    total = first.shape[0]
    group = total // lanes
    slots = received.shape[1]
    k = received.shape[2] // 3

    def kernel(mine, rec, columns, rows, far_low, far_high, out, own, oth, low, high, sems):
        copies = [
            pltpu.make_async_copy(far_low, low, sems.at[0]),
            pltpu.make_async_copy(far_high, high, sems.at[1]),
        ]
        for copy in copies:
            copy.start()
        i0, i1 = columns[:, :1], columns[:, 1:]
        t0, t1 = rows[:1, :], rows[1:, :]
        grid = lax.broadcasted_iota(jnp.int32, (total, slots), 1)
        turned = lax.broadcasted_iota(jnp.int32, (slots, total), 0)

        def pick(base):
            return (grid == base).astype(f32).astype(bf16)

        def place(base):
            return (turned == base).astype(f32).astype(bf16)

        at_start = pick(i0)
        at_start_next = pick(i0 + 1)
        at_end = pick(i1 + 1)
        lane = lax.broadcasted_iota(jnp.int32, (total, 1), 0) // group
        norm_row = i0 - 2 * lane + 6
        both = (grid == norm_row) | (grid == norm_row + 1)
        sums = dot(both.astype(f32), rec[0])
        square_sum = jnp.concatenate(
            [sums[j * group : (j + 1) * group, j * k : (j + 1) * k] for j in range(lanes)], axis=0
        )[:, :1]
        proj, cot = [], []
        for s in range(2):
            near = dot(at_start, rec[s])
            next_up = dot(at_start_next, rec[s, :, :k])
            tail = dot(at_end, rec[s, :, k:])
            proj += [(near[:, :k], near[:, 2 * k :]), (near[:, k : 2 * k], next_up)]
            cot += [tail[:, :k], tail[:, k:]]
        to_start = place(t0)
        to_start_next = place(t0 + 1)
        to_end = place(t1 + 1)

        def grams():
            for copy in copies:
                copy.wait()
            return low[...], high[...]

        active, back, less, mix_first, mix_second = row_stage(
            proj, cot, square_sum, grams, features
        )
        for s in range(2):
            l0, l1 = 2 * s, 2 * s + 1
            near = dot(to_start, joined([back[l0], back[l1], less[l0]]))
            weighted = dot(to_start_next, less[l1])
            tail = dot(to_end, joined([active[l0], active[l1]]))
            out[s] = (near + joined([weighted, tail])).astype(bf16)
        first_section = mine[0] == 0
        for i, (one, two) in enumerate(zip(mix_first, mix_second)):
            at = slice(i * k, (i + 1) * k)
            one, two = joined(one), joined(two)
            own[at, :] = jnp.where(first_section, one, two).astype(bf16)
            oth[at, :] = jnp.where(first_section, two, one).astype(bf16)

    columns = jnp.stack([first, second], axis=1)
    rows = jnp.stack([first, second])
    local_ref = pl.BlockSpec(memory_space=pltpu.VMEM)
    far_ref = pl.BlockSpec(memory_space=pl.ANY)
    mix = jax.ShapeDtypeStruct((6 * k, 4 * k), bf16)
    return pl.pallas_call(
        kernel,
        in_specs=[pl.BlockSpec(memory_space=pltpu.SMEM)] + [local_ref] * 3 + [far_ref] * 2,
        out_shape=[jax.ShapeDtypeStruct(received.shape, bf16), mix, mix],
        scratch_shapes=[
            pltpu.VMEM(gram_low.shape, bf16),
            pltpu.VMEM(gram_high.shape, bf16),
            pltpu.SemaphoreType.DMA((2,)),
        ],
        compiler_params=pltpu.CompilerParams(vmem_limit_bytes=16 << 20),
        name="meet",
    )(section[None], received, columns, rows, *in_hbm(gram_low, gram_high))


def unpack(returned, mix_own, mix_other, lanes):
    rows, k = returned.shape[0] // 8, returned.shape[1] // 3

    def kernel(ret, own, far, xs, cs, mix, wide, oth, sem):
        copy = pltpu.make_async_copy(far, oth, sem)
        copy.start()
        for t in range(3):
            wide[t] = ret[:, t * k : (t + 1) * k].astype(f32)
        for j in range(lanes):
            at = slice(j * rows, (j + 1) * rows)
            low = [wide[t, pl.ds(2 * j, rows, stride=8), :].astype(bf16) for t in range(3)]
            high = [wide[t, pl.ds(2 * j + 1, rows, stride=8), :].astype(bf16) for t in range(3)]
            xs[at, :] = joined(low + high[:1])
            cs[at, :] = joined(high[1:])
        copy.wait()
        mix[...] = (own[...].astype(f32) + oth[...].astype(f32)).astype(bf16)

    local_ref = pl.BlockSpec(memory_space=pltpu.VMEM)
    shapes = [(lanes * rows, 4 * k), (lanes * rows, 2 * k), mix_own.shape]
    return pl.pallas_call(
        kernel,
        in_specs=[local_ref, local_ref, pl.BlockSpec(memory_space=pl.ANY)],
        out_shape=[jax.ShapeDtypeStruct(shape, bf16) for shape in shapes],
        scratch_shapes=[
            pltpu.VMEM((3, 8 * rows, k), f32),
            pltpu.VMEM(mix_own.shape, bf16),
            pltpu.SemaphoreType.DMA,
        ],
        compiler_params=pltpu.CompilerParams(vmem_limit_bytes=8 << 20),
        name="unpack",
    )(returned, mix_own, *in_hbm(mix_other))


def piece(at, size, turned, weights, xs, cs, mix):
    both = turned.shape[1]
    k = cs.shape[1] // 2
    total = both // 2
    parts = 2
    chunk = size // parts

    def kernel(at_ref, t_ref, w_ref, xs_ref, cs_ref, mix_ref, major, minor, t_buf, w_buf, sems):
        copies = []
        for i in range(parts):
            rows = pl.ds(pl.multiple_of(at_ref[0] + i * chunk, 16), chunk)
            copies.append(
                [
                    pltpu.make_async_copy(t_ref.at[rows, :], t_buf.at[i], sems.at[i, 0]),
                    pltpu.make_async_copy(w_ref.at[rows, :], w_buf.at[i], sems.at[i, 1]),
                ]
            )
        for copy in copies[0] + copies[1]:
            copy.start()
        for i in range(parts):
            rows = slice(i * chunk, (i + 1) * chunk)
            for copy in copies[i]:
                copy.wait()
            if i + 2 < parts:
                for copy in copies[i + 2]:
                    copy.start()
            value = dot(t_buf[i, :, :total], xs_ref[...]) + dot(w_buf[i], mix_ref[...])
            last = dot(t_buf[i, :, total:], cs_ref[...])
            major[rows, : 2 * k] = value[:, : 2 * k].astype(bf16)
            major[rows, 2 * k :] = (value[:, 2 * k : 3 * k] + last[:, :k]).astype(bf16)
            minor[rows, :] = (value[:, 3 * k :] + last[:, k:]).astype(bf16)

    local_ref = pl.BlockSpec(memory_space=pltpu.VMEM)
    far_ref = pl.BlockSpec(memory_space=pl.ANY)
    return pl.pallas_call(
        kernel,
        in_specs=[pl.BlockSpec(memory_space=pltpu.SMEM)] + [far_ref] * 2 + [local_ref] * 3,
        out_specs=[local_ref] * 2,
        out_shape=[
            jax.ShapeDtypeStruct((size, 3 * k), bf16),
            jax.ShapeDtypeStruct((size, k), bf16),
        ],
        scratch_shapes=[
            pltpu.VMEM((parts, chunk, both), bf16),
            pltpu.VMEM((parts, chunk, 6 * k), bf16),
            pltpu.SemaphoreType.DMA((parts, 2)),
        ],
        compiler_params=pltpu.CompilerParams(vmem_limit_bytes=16 << 20),
        name="piece",
    )(at[None], *in_hbm(turned, weights), xs, cs, mix)


def squares(block):
    rows, width = block.shape

    def kernel(ref, out):
        v = ref[...].astype(f32)
        out[...] = jnp.sum((v * v).reshape(4, rows // 32, 8, width), axis=1)

    return pl.pallas_call(
        kernel,
        out_shape=jax.ShapeDtypeStruct((4, 8, width), f32),
        compiler_params=pltpu.CompilerParams(vmem_limit_bytes=8 << 20),
        name="squares",
    )(block)


def finish(starts, major, minor, features, k):
    quarter = features // 4
    part = quarter // 4
    late = 2
    early = [i for i in range(4) if i != late]
    blocks = [*major, *minor]
    known = [squares(major[i]) for i in early] + [squares(minor[i]) for i in early]

    def kernel(at, *refs):
        ins, known, (down, up, out, sems) = refs[:8], refs[8:14], refs[14:]

        def run(which, group, columns):
            sums = [None] * 4
            for i in range(4):
                if i == late:
                    v = ins[which * 4 + i][:, columns].astype(f32)
                    v = jnp.sum((v * v).reshape(4, part // 8, 8, k), axis=1)
                else:
                    v = known[which * 3 + early.index(i)][:, :, columns]
                sums[i] = ring_sum(v[0], v[2], v[1], v[3])
            total = ring_sum(sums[0], sums[2], sums[1], sums[3])
            mean = jnp.sum(total) * (1.0 / (features * k))
            scale = lax.rsqrt(jnp.full((1, k), mean, f32) + step_eps)
            for i in range(4):
                for j in range(4):
                    row = pl.multiple_of(at[which, i, j], 16)
                    v = ins[which * 4 + i][j * part : (j + 1) * part, columns].astype(f32)
                    out[group, pl.ds(row, part), :] = (v * scale).astype(bf16)

        copies = []
        for group in range(4):
            which = group // 3
            run(which, group, slice(0, k) if which else slice(group * k, (group + 1) * k))
            target = (down, up)[group // 2].at[group % 2]
            copies.append(pltpu.make_async_copy(out.at[group], target, sems.at[group]))
            copies[-1].start()
        for copy in copies:
            copy.wait()

    local_ref = pl.BlockSpec(memory_space=pltpu.VMEM)
    far_ref = pl.BlockSpec(memory_space=pl.ANY)
    return pl.pallas_call(
        kernel,
        in_specs=[pl.BlockSpec(memory_space=pltpu.SMEM)] + [local_ref] * 14,
        out_specs=[far_ref] * 2,
        out_shape=[jax.ShapeDtypeStruct((2, features, k), bf16)] * 2,
        scratch_shapes=[
            pltpu.VMEM((4, features, k), bf16),
            pltpu.SemaphoreType.DMA((4,)),
        ],
        compiler_params=pltpu.CompilerParams(vmem_limit_bytes=16 << 20),
        name="finish",
    )(starts, *blocks, *known)


def coords(peer):
    return peer // 16, (peer // 4) % 4, peer % 4


MAJOR = ((0, 1, 2), (1, 2, 0))
MINOR = ((2, 0, 1), (2, 0, 1))


def hop(values, order, stage, by):
    pairs = []
    for s in range(2):
        axis = order[s][stage]
        for p in range(64):
            c = list(coords(p))
            c[axis] = (c[axis] + by) % 4
            pairs.append((s * 64 + p, s * 64 + c[0] * 16 + c[1] * 4 + c[2]))
    return lax.ppermute(values, ("section", "peer"), pairs)


def ring_sum(own, two, one, three):
    return (own + two) + (one + three)


def summed(parts, order, at, gains=None):
    step = parts[0].shape[0] // 4

    def cut(by):
        start = ((at[1] + by) % 4) * step
        return sum(lax.dynamic_slice_in_dim(p, start, step, axis=0).astype(f32) for p in parts)

    arrived = [hop(cut(by).astype(bf16), order, 1, by) for by in (2, 1, 3)]
    own = cut(0) + sum(part.astype(f32) for part in arrived)
    own = lax.optimization_barrier(own.astype(bf16))
    two, one, three = [hop(own, order, 2, by).astype(f32) for by in (2, 1, 3)]
    total = ring_sum(own.astype(f32), two, one, three)
    return (total if gains is None else total * gains).astype(bf16)


def gathered(block, order):
    wide = jnp.concatenate([block] + [hop(block, order, 1, by) for by in (1, 2, 3)], axis=0)
    return [wide] + [hop(wide, order, 0, by) for by in (1, 2, 3)]


def local(inputs, cotangent, down_proj, up_proj, norm_gain, wiring, live_mask):
    section = lax.axis_index("section")
    peer = lax.axis_index("peer")
    _, lanes, rows, features = inputs.shape
    k = down_proj.shape[3]
    x, c = inputs[0], cotangent[0]
    gain, up = norm_gain[0], up_proj[0]
    is_first = section == 0
    swap = [(0, 1), (1, 0)]
    down = down_proj[0]
    down_other = lax.ppermute(down, "section", swap)
    up_other = lax.ppermute(up, "section", swap)
    gain_other = lax.ppermute(gain, "section", swap)
    sent = front(x, c, down, up, gain)
    received = lax.all_to_all(
        sent.reshape(rows, 8, 3 * k), ("section", "peer"), 0, 0, tiled=True
    ).reshape(2, -1, 3 * k)
    weights, gram_low, gram_high = prepare(
        section, down, up, gain, down_other, up_other, gain_other
    )
    holders = peer_table(wiring, live_mask)
    total = holders.shape[1]
    lane_of = jnp.arange(total, dtype=jnp.int32) // (total // lanes)
    base = holders * 8 + 2 * lane_of
    out, mix_own, mix_leaving = meet(
        section, received, base[0], base[1], gram_low, gram_high, lanes, features
    )
    mix_other = lax.ppermute(mix_leaving, "section", swap)
    returned = lax.all_to_all(
        out.reshape(rows, 8, 3 * k), ("section", "peer"), 0, 0, tiled=True
    ).reshape(8 * rows, 3 * k)
    turned = turn(*lax.optimization_barrier((x, c, mix_own))[:2])
    xs, cs, mix = unpack(returned, mix_own, mix_other, lanes)

    where = jnp.stack(coords(peer))
    at_major, at_minor = (
        [jnp.where(is_first, where[order[0][i]], where[order[1][i]]) for i in range(3)]
        for order in (MAJOR, MINOR)
    )
    quarter = features // 4
    major, minor = [], []
    for by in (2, 1, 3, 0):
        index = ((at_major[0] + by) % 4) * quarter
        part, rest = piece(index.astype(jnp.int32), quarter, turned, weights, xs, cs, mix)
        major.append(hop(part, MAJOR, 0, by) if by else part)
        minor.append(rest)

    def pick_minor(by):
        ahead = (at_minor[0] + by - at_major[0]) % 4
        return lax.select_n(
            jnp.broadcast_to(ahead, minor[0].shape), minor[3], minor[1], minor[0], minor[2]
        )

    step = features // 16
    row = at_major[0] * quarter + at_major[1] * step
    gains = lax.dynamic_slice_in_dim(gain, row, step, axis=1).T
    gains = joined([jnp.broadcast_to(gains[:, l : l + 1], (step, k)) for l in range(2)])
    gains = joined([gains, jnp.ones((step, k), f32)])
    minor = [hop(pick_minor(by), MINOR, 0, by) for by in (2, 1, 3)] + [pick_minor(0)]
    minor = gathered(summed(minor, MINOR, at_minor), MINOR)
    major = gathered(summed(major, MAJOR, at_major, gains), MAJOR)

    back = jnp.arange(4, dtype=jnp.int32)
    starts = jnp.stack(
        [
            ((at[0] - back) % 4)[:, None] * quarter + ((at[1] - back) % 4)[None, :] * step
            for at in (at_major, at_minor)
        ]
    ).astype(jnp.int32)
    down_step, up_step = finish(starts, major, minor, features, k)
    return down_step[None], up_step[None]


def solution(mesh):
    placed = (
        P("peer", None, None, None),
        P("peer", None, None, None),
        P("section", None, None, None),
        P("section", None, None, None),
        P("section", None, None),
        P(),
        P(),
    )
    return jax.shard_map(
        local,
        mesh=mesh,
        in_specs=placed,
        out_specs=(P("section", None, None, None), P("section", None, None, None)),
        check_vma=False,
    )
```
